32 devices in a mesh: section: 2 (over core), dp: 16 (over z, y, x).
Axes of the slice: x: 2, y: 2, z: 4, core: 2. Of those that a mesh axis runs over, the one named last changes fastest.
Arguments:
- input_rows: bfloat16 [49152, 512], P('dp'), may hold values from -6 to 6
- conditioning: bfloat16 [49152, 512], P('dp'), may hold values from -6 to 6
- prompt: bfloat16 [48, 4, 32, 512], P('dp'), may hold values from -6 to 6
- buckets: int32 [48], P('dp'), may hold values from 0 to 2, as said below
- item_len: int32 [48, 4], P('dp'), may hold values from 0 to 1024, as said below
- step_index: int32 [48, 4], P('dp'), may hold values from 0 to 999
- output_gradient: bfloat16 [49152, 512], P('dp'), may hold values from -6 to 6
- grad_skip: bfloat16 [49152, 512], P('dp'), may hold values from -6 to 6
- step_w: bfloat16 [512, 512], replicated, may hold values from -0.25 to 0.25
- conv_w: bfloat16 [3, 512, 1024], replicated, may hold values from -0.15625 to 0.15625
- cond_w: bfloat16 [512, 1024], replicated, may hold values from -0.25 to 0.25
- conv_b: float32 [1024], replicated, may hold values from -2 to 2
- res_w: bfloat16 [512, 1024], replicated, may hold values from -0.25 to 0.25
- res_b: float32 [1024], replicated, may hold values from -2 to 2
- query_w: bfloat16 [512, 512], replicated, may hold values from -0.25 to 0.25
- key_w: bfloat16 [512, 512], replicated, may hold values from -0.25 to 0.25
- value_w: bfloat16 [512, 512], replicated, may hold values from -0.25 to 0.25
- out_w: bfloat16 [512, 1024], replicated, may hold values from -0.75 to 0.75
- out_b: float32 [1024], replicated, may hold values from -2 to 2
Outputs:
- block_out: bfloat16 [49152, 512], P('dp', 'section')
- skip_out: bfloat16 [49152, 512], P('dp', 'section')
- in_grad: bfloat16 [49152, 512], P('dp', 'section')
- step_w_grad: float32 [512, 512], replicated
- conv_w_grad: float32 [3, 512, 1024], replicated
- cond_w_grad: float32 [512, 1024], replicated
- conv_b_grad: float32 [1024], replicated
- res_w_grad: float32 [512, 1024], replicated
- res_b_grad: float32 [1024], replicated
- query_w_grad: float32 [512, 512], replicated
- key_w_grad: float32 [512, 512], replicated
- value_w_grad: float32 [512, 512], replicated
- out_w_grad: float32 [512, 1024], replicated
- out_b_grad: float32 [1024], replicated
- norm_levels: float32 [3], replicated
The draws below stay inside these ranges and needn't reach their ends.
Inputs may be any that keep to these rules, and one draw needn't show every extreme that they name: micro-batch j holds 2**buckets[j] item slots of 1024 / 2**buckets[j] frames each; micro-batch 0 has bucket 0. `item_len`: slot s of micro-batch j is used for s < 2**buckets[j], with between half of the slot's frames and all of them valid; unused slots hold 0; slot 0 of micro-batch 0 has 1024 valid frames.
All inputs are finite; a program needn't handle non-finite values.
Results may differ from the reference program's by a relative error of at most 0.014.
Values may be sent and summed in bfloat16 or wider, within the bound.
No kernel may reach another device: no remote copies, remote signals or barrier semaphores. Data moves between devices by JAX's collectives and lax.ppermute only.
A program may use at most 192 MiB of HBM per device.

```python
import math
import jax
import jax.numpy as jnp
from jax import lax

D = 512
HEADS = 8
NQ = 32
KS = 3
DILATION_SIZE = 2
SLOTS = 4
MB_LEN = 1024
BATCHES = 48
TOKENS = 49152


def draw_plan(key):
    bucket_key, length_key = jax.random.split(key)
    buckets = jax.random.randint(bucket_key, (BATCHES,), 0, 3, dtype=jnp.int32)
    buckets = buckets.at[0].set(0)
    count = jnp.left_shift(jnp.int32(1), buckets)
    span = jnp.int32(MB_LEN) // count
    lower = span // 2
    spread = jax.random.randint(length_key, (BATCHES, SLOTS), 0, 1 << 20, dtype=jnp.int32)
    lengths = lower[:, None] + spread % (span[:, None] - lower[:, None] + 1)
    used = jnp.arange(SLOTS, dtype=jnp.int32)[None, :] < count[:, None]
    lengths = jnp.where(used, lengths, 0)
    lengths = lengths.at[0, 0].set(MB_LEN)
    return (buckets, lengths.astype(jnp.int32))


def draw_buckets(key, part):
    return draw_plan(key)[0]


def draw_item_len(key, part):
    return draw_plan(key)[1]


def set_ends(result, rng, low, top_value):
    extent = result.shape
    index_at = [jax.random.randint(jax.random.fold_in(rng, axis), (), 0, extent[axis]) for axis in range(len(extent))]
    result = result.at[tuple(index_at)].set(low)
    longest = extent.index(max(extent))
    index_at[longest] = (index_at[longest] + 1) % extent[longest]
    return result.at[tuple(index_at)].set(top_value)


def block_levels(key, extent, cuts, low, high):
    def one(position, parts):
        draws = jax.random.uniform(jax.random.fold_in(jax.random.fold_in(key, 6), position), (parts,), jnp.float32, low / len(cuts), high / len(cuts))
        return jnp.repeat(jnp.exp(draws), extent[position] // parts).reshape((-1,) + (1,) * (len(extent) - position - 1))

    loudness = one(*cuts[0])
    for cut in cuts[1:]:
        loudness = loudness * one(*cut)
    return loudness


def normal_values(key, shape, scale, most, cuts=(), kind=jnp.bfloat16):
    values = scale * jax.random.normal(key, shape, jnp.float32)
    if cuts:
        values = values * block_levels(key, shape, cuts, -0.22, 0.18)
    return jnp.clip(values, -most, most).astype(kind)


def setup_inputs(seed: int = 0) -> dict:
    seeds = jax.random.split(jax.random.key(seed), 20)
    return {
        "input_rows": normal_values(seeds[0], (TOKENS, D), 1.0, 6.0, ((0, 16),)),
        "conditioning": normal_values(seeds[1], (TOKENS, D), 1.0, 6.0, ((0, 16),)),
        "prompt": normal_values(seeds[2], (BATCHES, SLOTS, NQ, D), 1.0, 6.0, ((0, 16),)),
        "buckets": draw_buckets(jax.random.fold_in(seeds[19], 71), 0),
        "item_len": draw_item_len(jax.random.fold_in(seeds[19], 71), 0),
        "step_index": set_ends(jax.random.randint(seeds[5], (BATCHES, SLOTS), 0, 1000), jax.random.fold_in(seeds[5], 1), 0, 999).astype(jnp.int32),
        "output_gradient": normal_values(seeds[6], (TOKENS, D), 1.0, 6.0, ((0, 16),)),
        "grad_skip": normal_values(seeds[7], (TOKENS, D), 1.0, 6.0, ((0, 16),)),
        "step_w": normal_values(seeds[8], (D, D), D ** -0.5, 0.25),
        "conv_w": normal_values(seeds[9], (KS, D, 2 * D), (KS * D) ** -0.5, 0.15625),
        "cond_w": normal_values(seeds[10], (D, 2 * D), D ** -0.5, 0.25),
        "conv_b": normal_values(seeds[11], (2 * D,), 0.3, 2.0, (), jnp.float32),
        "res_w": normal_values(seeds[12], (D, 2 * D), D ** -0.5, 0.25),
        "res_b": normal_values(seeds[13], (2 * D,), 0.3, 2.0, (), jnp.float32),
        "query_w": normal_values(seeds[14], (D, D), D ** -0.5, 0.25),
        "key_w": normal_values(seeds[15], (D, D), D ** -0.5, 0.25),
        "value_w": normal_values(seeds[16], (D, D), D ** -0.5, 0.25),
        "out_w": normal_values(seeds[17], (D, 2 * D), (D // 8) ** -0.5, 0.75),
        "out_b": normal_values(seeds[18], (2 * D,), 0.3, 2.0, (), jnp.float32),
    }


ISQ2 = 0.7071067811865476
HIGH = lax.Precision.HIGHEST

@jax.custom_vjp
def low(v):
    return lax.optimization_barrier(v.astype(jnp.bfloat16)).astype(jnp.float32)

@jax.custom_vjp
def low_back(v):
    return v

def low_keep(v):
    return (low(v), None)

def low_pass(kept, grad):
    return (grad,)

def back_keep(v):
    return (v, None)

def back_low(kept, grad):
    return (low(grad),)
low.defvjp(low_keep, low_pass)
low_back.defvjp(back_keep, back_low)

def matmul_hi(left, right):
    return jnp.dot(left, right, precision=HIGH)

def layout(bucket, lengths, frames):
    slots = lengths.shape[0]
    place = jnp.arange(frames, dtype=jnp.int32)
    span = jnp.int32(frames) // jnp.left_shift(jnp.int32(1), bucket.astype(jnp.int32))
    segment = (place // span).astype(jnp.int32)
    inside = place - segment * span
    onehot = (segment[:, None] == jnp.arange(slots, dtype=jnp.int32)[None, :]).astype(jnp.float32)
    limit = lax.optimization_barrier(jnp.sum(onehot * lengths.astype(jnp.float32)[None, :], axis=1))
    valid = (inside.astype(jnp.float32) < limit).astype(jnp.float32)
    return (segment, onehot, valid)

def embed(steps, width):
    half = width // 2
    freqs = jnp.exp(-math.log(10000.0) * jnp.arange(half, dtype=jnp.float32) / half)
    angles = steps.astype(jnp.float32)[:, None] * freqs[None, :]
    return jnp.concatenate([jnp.sin(angles), jnp.cos(angles)], axis=1)

def neighbour_ok(segment, start_offset):
    frames = segment.shape[0]
    place = jnp.arange(frames, dtype=jnp.int32)
    moved = jnp.roll(segment, -start_offset)
    return (moved == segment) & (place + start_offset >= 0) & (place + start_offset < frames)

def tap_stack(field, segment):
    pieces = []
    for start_offset in (-DILATION_SIZE, 0, DILATION_SIZE):
        inside = neighbour_ok(segment, start_offset)
        pieces.append(jnp.where(inside[:, None], jnp.roll(field, -start_offset, axis=0), jnp.zeros_like(field)))
    return jnp.concatenate(pieces, axis=1)

def forward(params, rows, cond_rows, prompt_rows, segment, onehot, valid, embedding):
    step_w, conv_w, cond_w, conv_b, res_w, res_b, query_w, key_w, value_w, out_w, out_b = params
    width = rows.shape[1]
    head_size = width // HEADS
    step_proj = matmul_hi(low(embedding), step_w)
    mixed = (rows + matmul_hi(onehot, step_proj)) * valid[:, None]
    stacked = tap_stack(low(mixed), segment)
    pre_gate = low_back(matmul_hi(stacked, conv_w.reshape(-1, 2 * width)) + matmul_hi(cond_rows, cond_w) + conv_b)
    gate = low(jnp.tanh(pre_gate[:, :width]) * jax.nn.sigmoid(pre_gate[:, width:]))
    branch = low_back(matmul_hi(gate, res_w) + res_b)
    hidden = (mixed + branch[:, :width]) * valid[:, None] * ISQ2
    sent = low_back(low(hidden))
    keys_in = prompt_rows.reshape(-1, width)
    keys = low(low_back(matmul_hi(keys_in, key_w)))
    values = low(low_back(matmul_hi(keys_in, value_w)))
    queries = low(low_back(matmul_hi(sent, query_w)))
    owner = jnp.arange(keys.shape[0], dtype=jnp.int32) // prompt_rows.shape[1]
    allowed = segment[:, None] == owner[None, :]
    scores = jnp.einsum('fhc,khc->fhk', queries.reshape(-1, HEADS, head_size), keys.reshape(-1, HEADS, head_size), precision=HIGH) * head_size ** (-0.5)
    scores = low_back(jnp.where(allowed[:, None, :], scores, -1e+30))
    peak = lax.optimization_barrier(jnp.max(scores, axis=-1, keepdims=True))
    expo = jnp.exp(scores - peak)
    probs = low(expo / lax.optimization_barrier(jnp.sum(expo, axis=-1, keepdims=True)))
    attended = jnp.einsum('fhk,khc->fhc', probs, values.reshape(-1, HEADS, head_size), precision=HIGH).reshape(-1, width)
    attended = low(low_back(attended))
    film = low_back(matmul_hi(attended, out_w) + out_b)
    scale = film[:, :width]
    shift = film[:, width:]
    output = (sent * (1.0 + scale) + shift) * valid[:, None]
    skip = branch[:, width:] * valid[:, None]
    change = sent * scale + shift
    res_part = branch[:, :width]
    stats = jnp.stack([jnp.sum(valid[:, None] * hidden * hidden), jnp.sum(valid[:, None] * res_part * res_part), jnp.sum(valid), jnp.sum(valid[:, None] * change * change)])
    return ((output, skip), stats)

def reference(input_rows, conditioning, prompt, buckets, item_len, step_index, output_gradient, grad_skip, step_w, conv_w, cond_w, conv_b, res_w, res_b, query_w, key_w, value_w, out_w, out_b):
    params = tuple((p.astype(jnp.float32) for p in (step_w, conv_w, cond_w, conv_b, res_w, res_b, query_w, key_w, value_w, out_w, out_b)))
    rows_all = input_rows.astype(jnp.float32).reshape(BATCHES, MB_LEN, D)
    cond_all = conditioning.astype(jnp.float32).reshape(BATCHES, MB_LEN, D)
    prompt_all = prompt.astype(jnp.float32)
    gout_all = output_gradient.astype(jnp.float32).reshape(BATCHES, MB_LEN, D)
    gskip_all = grad_skip.astype(jnp.float32).reshape(BATCHES, MB_LEN, D)

    def one(carry, inputs):
        grads, stats = carry
        rows, cond_rows, prompt_rows, bucket, lengths, steps, gout, gskip = inputs
        segment, onehot, valid = layout(bucket, lengths, MB_LEN)
        embedding = embed(steps, D)

        def apply(prm, incoming_rows):
            return forward(prm, incoming_rows, cond_rows, prompt_rows, segment, onehot, valid, embedding)
        (output, skip), pull, part = jax.vjp(apply, params, rows, has_aux=True)
        d_params, d_rows = pull((gout, gskip))
        grads = jax.tree.map(jnp.add, grads, d_params)
        return ((grads, stats + part), (output, skip, d_rows))
    start = (tuple((jnp.zeros_like(p) for p in params)), jnp.zeros((4,), jnp.float32))
    (grads, stats), (outputs, skips, d_rows) = lax.scan(one, start, (rows_all, cond_all, prompt_all, buckets, item_len, step_index, gout_all, gskip_all))
    levels = jnp.sqrt(jnp.stack([stats[0], stats[1], stats[3]]) / (stats[2] * D))
    return (outputs.reshape(TOKENS, D).astype(jnp.bfloat16), skips.reshape(TOKENS, D).astype(jnp.bfloat16), d_rows.reshape(TOKENS, D).astype(jnp.bfloat16), grads[0], grads[1], grads[2], grads[3], grads[4], grads[5], grads[6], grads[7], grads[8], grads[9], grads[10], levels)
```

```python
import functools
import math

import jax
import jax.numpy as jnp
from jax import lax
from jax.experimental import pallas as pl
from jax.experimental.pallas import tpu as pltpu
from jax.sharding import PartitionSpec as P

HEADS = 8
SHIFT = 2
EDGE = 16
ISQ2 = 0.7071067811865476
F32 = jnp.float32
BF16 = jnp.bfloat16
VMEM = 56 * 1024 * 1024
KB_VMEM = 48 * 1024 * 1024
KC_VMEM = 48 * 1024 * 1024


def nn(a, b):
    return lax.dot_general(a, b, (((1,), (0,)), ((), ())), preferred_element_type=F32)


def nt(a, b):
    return lax.dot_general(a, b, (((1,), (1,)), ((), ())), preferred_element_type=F32)


def tn(a, b):
    return lax.dot_general(a, b, (((0,), (0,)), ((), ())), preferred_element_type=F32)


def rows_iota(rows, cols):
    return lax.broadcasted_iota(jnp.int32, (rows, cols), 0)


def col_sums(x):
    rows, cols = x.shape
    return jnp.sum(x.reshape(rows // 8, 8, cols), axis=0)


def plan(g, tile, slots, buckets, item_len):
    mb = g // slots
    q = g - mb * slots
    span = slots >> buckets[mb]
    slot = q // span
    off = q - slot * span
    lim = item_len[mb, slot] - off * tile
    return mb, slot, lim, off > 0, off < span - 1


def forward_kernel(
    cfg,
    sec_ref,
    buckets,
    item_len,
    steps,
    prev_ref,
    rows_ref,
    next_ref,
    cond_ref,
    gout_ref,
    gskip_ref,
    prompt_ref,
    mask_ref,
    step_w,
    conv_w,
    cond_w,
    conv_b,
    res_w,
    res_b,
    query_w,
    key_w,
    value_w,
    out_w,
    out_b,
    o_stack,
    o_dpre,
    o_dsent,
    o_block_keep,
    o_block_give,
    o_skip_keep,
    o_skip_give,
    o_keep,
    o_give,
    o_vec,
    o_emb,
    proj,
    keys,
    values,
    d_keys,
    d_values,
    g_out,
    g_res,
    g_query,
    sums,
    stats,
    count,
):
    tile, slots, nq, subs, tiles, mb_own, micro = cfg
    t = pl.program_id(0)
    section = sec_ref[0]
    size = subs * tile
    width = rows_ref.shape[1]
    half = width // 2
    head = width // HEADS
    mb0 = section * (micro - mb_own)
    items = mb_own * slots
    keep_left = section == 0

    @pl.when(t == 0)
    def _():
        row = rows_iota(items, half)
        when = jnp.zeros((items, half), F32)
        for i in range(items):
            s = steps[mb0 + i // slots, i % slots].astype(F32)
            when = jnp.where(row == i, s, when)
        lane = lax.broadcasted_iota(jnp.int32, (items, half), 1).astype(F32)
        angle = when * jnp.exp(lane * F32(-math.log(10000.0) / half))
        emb = jnp.concatenate([jnp.sin(angle), jnp.cos(angle)], axis=1)
        o_emb[...] = emb
        proj[...] = nn(emb.astype(BF16), step_w[...])
        here = prompt_ref[pl.ds(pl.multiple_of(mb0 * slots * nq, 16), items * nq), :]
        factor = head ** (-0.5)
        keys[...] = (nn(here, key_w[...]).astype(BF16) * BF16(factor)).astype(BF16)
        values[...] = nn(here, value_w[...]).astype(BF16)
        d_keys[...] = jnp.zeros_like(d_keys)
        d_values[...] = jnp.zeros_like(d_values)
        g_out[...] = jnp.zeros_like(g_out)
        g_res[...] = jnp.zeros_like(g_res)
        g_query[...] = jnp.zeros_like(g_query)
        sums[...] = jnp.zeros_like(sums)
        stats[...] = jnp.zeros_like(stats)
        count[0] = 0

    ext = jnp.concatenate([prev_ref[...], rows_ref[...], next_ref[...]], axis=0)
    place = rows_iota(tile + 2 * EDGE, width)
    spread = tile + 2 * EDGE
    mixed, behind, ahead, at = [], [], [], []
    limit = jnp.zeros((size, width), jnp.int32)
    row = rows_iota(size, width)
    for k in range(subs):
        mb, slot, lim, prev_in, next_in = plan(
            section * tiles + t * subs + k, tile, slots, buckets, item_len
        )
        item = (mb - mb0) * slots + slot
        at.append(pl.multiple_of(item * nq, nq))
        lo = jnp.where(prev_in, 0, EDGE)
        hi = jnp.where(next_in, tile + 2 * EDGE, tile + EDGE)
        hi = jnp.minimum(hi, lim + EDGE)
        part = ext[k * tile : k * tile + spread].astype(F32) + proj[pl.ds(item, 1), :]
        part = jnp.where((place >= lo) & (place < hi), part, 0.0)
        mixed.append(part[EDGE : EDGE + tile])
        behind.append(pltpu.roll(part, SHIFT, 0)[EDGE : EDGE + tile].astype(BF16))
        ahead.append(pltpu.roll(part, spread - SHIFT, 0)[EDGE : EDGE + tile].astype(BF16))
        limit = jnp.where(row >= k * tile, lim + k * tile, limit)
        count[0] += jnp.clip(lim, 0, tile)
    mixed = jnp.concatenate(mixed, axis=0)
    valid = row < limit
    stacked = jnp.concatenate(
        [jnp.concatenate(behind, axis=0), mixed.astype(BF16), jnp.concatenate(ahead, axis=0)],
        axis=1,
    )
    o_stack[...] = stacked
    pre = nn(stacked, conv_w[...]) + nn(cond_ref[...], cond_w[...]) + conv_b[...]
    a = jnp.tanh(pre[:, :width])
    s = 0.5 * jnp.tanh(0.5 * pre[:, width:]) + 0.5
    both = a * s
    gate = both.astype(BF16)
    slope_a = s - both * a
    slope_s = both - both * s
    branch = nn(gate, res_w[...]) + res_b[...]
    res_part = jnp.where(valid, branch[:, :width], 0.0)
    skip = jnp.where(valid, branch[:, width:], 0.0).astype(BF16)
    o_skip_keep[...] = jnp.where(keep_left, skip[:, :half], skip[:, half:])
    o_skip_give[...] = jnp.where(keep_left, skip[:, half:], skip[:, :half])
    hidden = (mixed + res_part) * ISQ2
    sent = hidden.astype(BF16)
    sent_f = sent.astype(F32)
    stats[0] += col_sums(hidden * hidden)
    stats[1] += col_sums(res_part * res_part)

    query = nn(sent, query_w[...]).astype(BF16)
    mask = mask_ref[...]
    probs, probs_low, key_bd, value_bd, attended = [], [], [], [], []
    for k in range(subs):
        key_bd.append(jnp.concatenate([keys[pl.ds(at[k], nq), :]] * HEADS, axis=0) * mask)
        value_bd.append(jnp.concatenate([values[pl.ds(at[k], nq), :]] * HEADS, axis=0) * mask)
        scores = nt(key_bd[k], query[k * tile : (k + 1) * tile]).reshape(HEADS, nq, tile)
        expo = jnp.exp(scores - jnp.max(scores, axis=1, keepdims=True))
        probs.append(expo * (1.0 / jnp.sum(expo, axis=1, keepdims=True)))
        probs_low.append(probs[k].astype(BF16).reshape(HEADS * nq, tile))
        attended.append(tn(probs_low[k], value_bd[k]).astype(BF16))
    attended = jnp.concatenate(attended, axis=0)
    film = nn(attended, out_w[...]) + out_b[...]
    scale = film[:, :width]
    change = jnp.where(valid, sent_f * scale + film[:, width:], 0.0)
    block = (sent_f + change).astype(BF16)
    o_block_keep[...] = jnp.where(keep_left, block[:, :half], block[:, half:])
    o_block_give[...] = jnp.where(keep_left, block[:, half:], block[:, :half])
    stats[2] += col_sums(change * change)

    gy = jnp.where(valid, gout_ref[...].astype(F32), 0.0)
    d_film = jnp.concatenate([(gy * sent_f).astype(BF16), gy.astype(BF16)], axis=1)
    sums[2] += col_sums(d_film.astype(F32))
    g_out[...] += tn(attended, d_film)
    d_att = nt(d_film, out_w[...]).astype(BF16)
    low_lane = lax.broadcasted_iota(jnp.int32, (nq, 2 * head), 1) < head

    def own_heads(x):
        pieces = []
        for p in range(HEADS // 2):
            at_row, at_lane = 2 * p * nq, 2 * p * head
            first = x[at_row : at_row + nq, at_lane : at_lane + 2 * head]
            second = x[at_row + nq : at_row + 2 * nq, at_lane : at_lane + 2 * head]
            pieces.append(jnp.where(low_lane, first, second))
        return jnp.concatenate(pieces, axis=1)

    d_query = []
    for k in range(subs):
        here = slice(k * tile, (k + 1) * tile)
        d_probs = nt(value_bd[k], d_att[here]).reshape(HEADS, nq, tile)
        weighted = probs[k] * d_probs
        inner = jnp.sum(weighted, axis=1, keepdims=True)
        d_scores = (weighted - probs[k] * inner).astype(BF16).reshape(HEADS * nq, tile)
        d_values[pl.ds(at[k], nq), :] += own_heads(nn(probs_low[k], d_att[here]))
        d_keys[pl.ds(at[k], nq), :] += own_heads(nn(d_scores, query[here]))
        d_query.append(tn(d_scores, key_bd[k]).astype(BF16))
    d_query = jnp.concatenate(d_query, axis=0)
    g_query[...] += tn(sent, d_query)
    d_sent = (gy * (1.0 + scale) + nt(d_query, query_w[...])).astype(BF16)
    o_dsent[...] = d_sent

    d_res = jnp.where(valid, d_sent.astype(F32) * ISQ2, 0.0).astype(BF16)
    gs = jnp.where(valid, gskip_ref[...].astype(F32), 0.0).astype(BF16)
    d_branch = jnp.concatenate([d_res, gs], axis=1)
    sums[1] += col_sums(d_branch.astype(F32))
    g_res[...] += tn(gate, d_branch)
    d_gate = nt(d_branch, res_w[...])
    d_pre = jnp.concatenate(
        [(d_gate * slope_a).astype(BF16), (d_gate * slope_s).astype(BF16)], axis=1
    )
    sums[0] += col_sums(d_pre.astype(F32))
    o_dpre[...] = d_pre

    @pl.when(t == tiles // subs - 1)
    def _():
        here = prompt_ref[pl.ds(pl.multiple_of(mb0 * slots * nq, 16), items * nq), :]
        factor = head ** (-0.5)
        mine = pl.multiple_of(section * half, half)
        theirs = pl.multiple_of(half - section * half, half)

        def put(i, ref, left):
            o_keep[i] = ref[pl.ds(mine, half), pl.ds(left, width)].astype(BF16)
            o_give[i] = ref[pl.ds(theirs, half), pl.ds(left, width)].astype(BF16)

        put(0, g_out, 0)
        put(1, g_out, width)
        put(2, g_res, 0)
        put(3, g_res, width)
        put(4, g_query, 0)
        g_query[...] = tn(here, (d_keys[...] * factor).astype(BF16))
        put(5, g_query, 0)
        g_query[...] = tn(here, d_values[...].astype(BF16))
        put(6, g_query, 0)
        for i in range(3):
            line = jnp.sum(sums[i], axis=0, keepdims=True)
            o_vec[2 * i : 2 * i + 1, :] = line[:, :width]
            o_vec[2 * i + 1 : 2 * i + 2, :] = line[:, width:]
        for i in range(3):
            o_vec[6 + i : 7 + i, :] = jnp.sum(stats[i], axis=0, keepdims=True)
        lane = lax.broadcasted_iota(jnp.int32, (16 - 9, width), 1)
        digits = (count[0] >> (3 * jnp.minimum(lane, 8))) & 7
        o_vec[9:16, :] = jnp.where(lane < 8, digits, 0).astype(F32)


def weight_kernel(cfg, sec_ref, stack_ref, cond_ref, dpre_ref, o_keep, o_give, acc):
    taps = cfg
    i = pl.program_id(0)
    section = sec_ref[0]
    width = acc.shape[0]
    half = width // 2

    @pl.when(i < taps)
    def _():
        acc[...] = tn(stack_ref[...], dpre_ref[...])

    @pl.when(i == taps)
    def _():
        acc[...] = tn(cond_ref[...], dpre_ref[...])

    mine = pl.multiple_of(section * half, half)
    theirs = pl.multiple_of(half - section * half, half)
    for side in range(2):
        o_keep[side] = acc[pl.ds(mine, half), pl.ds(side * width, width)].astype(BF16)
        o_give[side] = acc[pl.ds(theirs, half), pl.ds(side * width, width)].astype(BF16)


def back_kernel(
    cfg,
    sec_ref,
    buckets,
    item_len,
    prev_ref,
    dpre_ref,
    next_ref,
    other_ref,
    dsent_ref,
    conv_w,
    emb_ref,
    vec_ref,
    after_ref,
    o_keep,
    o_give,
    o_rows,
    d_step,
):
    tile, slots, subs, tiles, mb_own, micro = cfg
    t = pl.program_id(0)
    section = sec_ref[0]
    size = subs * tile
    width = dsent_ref.shape[1]
    half = width // 2
    mb0 = section * (micro - mb_own)

    @pl.when(t == 0)
    def _():
        d_step[...] = jnp.zeros_like(d_step)

    steps = tiles // subs
    before = jnp.where(t == 0, other_ref[EDGE:, :], prev_ref[...])
    after = jnp.where(t == steps - 1, other_ref[:EDGE, :], next_ref[...])
    ext = jnp.concatenate([before, dpre_ref[...], after], axis=0)
    spread = tile + 2 * EDGE
    place = rows_iota(spread, 2 * width)
    ahead, behind, item = [], [], []
    limit = jnp.zeros((size, width), jnp.int32)
    row = rows_iota(size, width)
    for k in range(subs):
        mb, slot, lim, prev_in, next_in = plan(
            section * tiles + t * subs + k, tile, slots, buckets, item_len
        )
        item.append((mb - mb0) * slots + slot)
        lo = jnp.where(prev_in, 0, EDGE)
        hi = jnp.where(next_in, spread, tile + EDGE)
        part = ext[k * tile : k * tile + spread].astype(F32)
        part = jnp.where((place >= lo) & (place < hi), part, 0.0)
        ahead.append(pltpu.roll(part, spread - SHIFT, 0)[EDGE : EDGE + tile].astype(BF16))
        behind.append(pltpu.roll(part, SHIFT, 0)[EDGE : EDGE + tile].astype(BF16))
        limit = jnp.where(row >= k * tile, lim + k * tile, limit)
    d_in = nt(jnp.concatenate(ahead, axis=0), conv_w[:width, :])
    d_in += nt(dpre_ref[...], conv_w[width : 2 * width, :])
    d_in += nt(jnp.concatenate(behind, axis=0), conv_w[2 * width :, :])
    d_mixed = jnp.where(row < limit, dsent_ref[...].astype(F32) * ISQ2 + d_in, 0.0)
    for k in range(subs):
        line = jnp.sum(col_sums(d_mixed[k * tile : (k + 1) * tile]), axis=0, keepdims=True)
        d_step[pl.ds(item[k], 1), :] += line
    low = d_mixed.astype(BF16)
    o_keep[...] = jnp.where(section == 0, low[:, :half], low[:, half:])
    o_give[...] = jnp.where(section == 0, low[:, half:], low[:, :half])

    @pl.when(t == steps - 1)
    def _():
        both = jnp.concatenate([emb_ref[...], d_step[...], vec_ref[...]], axis=0)
        o_rows[...] = both.astype(BF16)


SMALL = pl.CostEstimate(flops=1024, bytes_accessed=1024, transcendentals=0)
LARGE = pl.CostEstimate(flops=1 << 36, bytes_accessed=1024, transcendentals=0)
ANYWHERE = pl.BlockSpec(memory_space=pl.ANY)
PARAMS = pltpu.CompilerParams(vmem_limit_bytes=VMEM)


IN_VMEM = pl.BlockSpec(memory_space=pltpu.VMEM)
IN_SMEM = pl.BlockSpec(memory_space=pltpu.SMEM)
IN_HBM = pl.BlockSpec(memory_space=pltpu.HBM)


def struct(rows, width, dtype=BF16):
    return jax.ShapeDtypeStruct((rows, width), dtype)


def total(a, b):
    return (a.astype(F32) + b.astype(F32)).astype(BF16)


def at_bit(bit, rows):
    return pl.ds(pl.multiple_of(bit * rows, 16), rows)


def split_body(bit, held, got, keep, give):
    rows = keep.shape[0]
    keep[...] = total(held[at_bit(bit, rows), :], got[at_bit(bit, rows), :])
    give[...] = total(held[at_bit(1 - bit, rows), :], got[at_bit(1 - bit, rows), :])


def add_body(bit, held, got, out):
    out[...] = total(held[...], got[...])


def merge_body(bit, cur, got, out):
    rows = cur.shape[0]
    out[at_bit(bit, rows), :] = cur[...]
    out[at_bit(1 - bit, rows), :] = got[...]


def gather_body(bit, cur, got, out):
    rows = cur.shape[0] - EDGE
    out[at_bit(bit, rows), :] = cur[:rows, :]
    out[at_bit(1 - bit, rows), :] = got[:rows, :]
    out[2 * rows :, :] = total(cur[rows:, :], got[rows:, :])


def pair_kernel(bodies, outs, *refs):
    n = len(bodies)
    bits, arrays, results = refs[:n], refs[n : 3 * n], refs[3 * n + 1 :]
    for i, body in enumerate(bodies):
        count = outs[i]
        body(bits[i][0], arrays[2 * i], arrays[2 * i + 1], *results[:count])
        results = results[count:]


def pair_call(works, after, cost):
    outs = [len(w[4]) for w in works]
    shapes = [x for w in works for x in w[4]]
    return pl.pallas_call(
        functools.partial(pair_kernel, [w[0] for w in works], outs),
        in_specs=[IN_SMEM] * len(works) + [IN_VMEM] * (2 * len(works)) + [ANYWHERE],
        out_specs=[IN_VMEM] * len(shapes),
        out_shape=shapes,
        compiler_params=pltpu.CompilerParams(vmem_limit_bytes=24 * 1024 * 1024),
        cost_estimate=cost,
        name=works[0][0].__name__,
    )(*[w[1] for w in works], *[x for w in works for x in w[2:4]], after)


def then_kernel(x_ref, after_ref, out_ref):
    pass


def then(x, after):
    return pl.pallas_call(
        then_kernel,
        in_specs=[ANYWHERE, ANYWHERE],
        out_specs=ANYWHERE,
        out_shape=jax.ShapeDtypeStruct(x.shape, x.dtype),
        input_output_aliases={0: 0},
        cost_estimate=SMALL,
        name="then",
    )(x, after)


def join_kernel(count, sec_ref, *refs):
    section = sec_ref[0]
    arrays, outs = refs[: 2 * count], refs[2 * count + 1 : 3 * count + 1]
    mark, sems = refs[-2:]
    mark[...] = jnp.zeros_like(mark)
    copies = []
    for i in range(count):
        rows = arrays[2 * i].shape[0]
        for j, place in enumerate((section, 1 - section)):
            copies.append(
                pltpu.make_async_copy(
                    arrays[2 * i + j], outs[i].at[at_bit(place, rows), :], sems.at[2 * i + j]
                )
            )
    for copy in copies:
        copy.start()
    for copy in copies:
        copy.wait()


def join(sec, after, *pairs):
    rows, width = pairs[0][0].shape
    count = len(pairs)
    return pl.pallas_call(
        functools.partial(join_kernel, count),
        in_specs=[IN_SMEM] + [IN_VMEM] * (2 * count) + [ANYWHERE],
        out_specs=[IN_HBM] * count + [IN_VMEM],
        out_shape=[struct(2 * rows, width)] * count + [struct(8, 128, F32)],
        scratch_shapes=[pltpu.SemaphoreType.DMA((2 * count,))],
        compiler_params=pltpu.CompilerParams(vmem_limit_bytes=16 * 1024 * 1024),
        cost_estimate=SMALL,
        name="join",
    )(sec, *[x for pair in pairs for x in pair], after)


def swap(x):
    return lax.ppermute(x, "section", [(0, 1), (1, 0)])


class Sum:
    def __init__(self, orders):
        self.chips = lax.axis_size("dp")
        self.section = lax.axis_index("section")
        self.chip = lax.axis_index("dp")
        self.orders = orders
        self.levels = len(orders[0])

    def bit_of(self, step, section):
        where = jnp.where(section == 0, self.orders[0][step], self.orders[1][step])
        return ((self.chip >> where) & 1).astype(jnp.int32)

    def bit(self, step):
        return self.bit_of(step, self.section).reshape(1)

    def send(self, x, step):
        chips = self.chips
        route = [
            (s * chips + d, s * chips + (d ^ (1 << self.orders[s][step])))
            for s in range(2)
            for d in range(chips)
        ]
        return lax.ppermute(x, ("section", "dp"), route)

    def runs(self):
        mine, theirs = self.section, 1 - self.section
        own, other = self.bit_of(0, mine), self.bit_of(0, theirs)
        return jnp.stack(
            [2 * mine + own, 2 * mine + 1 - own, 2 * theirs + other, 2 * theirs + 1 - other]
        ).astype(jnp.int32)


class Batch:
    def __init__(self, sums, keep, give):
        self.sums = sums
        self.held = keep
        self.got = swap(give)
        self.step = 0

    def turn(self, after, more=(), cost=LARGE):
        sums, last = self.sums, self.sums.levels - 1
        at = self.step
        self.step += 1
        rows, width = self.held.shape
        if at < last:
            work = (split_body, sums.bit(at), self.held, self.got, [struct(rows // 2, width)] * 2)
            self.held, give, *rest = pair_call([work, *more], after, cost)
            self.got = sums.send(give, at)
        elif at <= last + 1:
            work = (add_body, sums.bit(0), self.held, self.got, [struct(rows, width)])
            self.held, *rest = pair_call([work, *more], after, cost)
            self.got = sums.send(self.held, at if at == last else last - 1)
        else:
            back = 2 * last + 1 - at
            work = (merge_body, sums.bit(back), self.held, self.got, [struct(2 * rows, width)])
            self.held, *rest = pair_call([work, *more], after, cost)
            self.got = sums.send(self.held, back - 1)
        return (self.held, *rest)

    @property
    def turns(self):
        return 2 * self.sums.levels - 1

    def spread(self, kinds, first):
        runs = self.sums.runs()
        *outs, done = place(runs, (0, 2), (self.held, swap(self.held)), kinds, first)
        self.got = then(self.got, done)
        return place(runs, (1, 3), (self.got, swap(self.got)), kinds, done, outs)


def place_kernel(which, spots, runs, p0, p1, after_ref, *refs):
    count = len(set(spot[0] for spot in spots if spot is not None))
    outs, (mark, buf, sems) = refs[-3 - count : -3], refs[-3:]
    mark[...] = jnp.zeros_like(mark)
    rows = buf.shape[1]
    per_run = p0.shape[0] // rows
    for wait in (False, True):
        for run in range(4):
            mine, theirs = runs[which[0]] == run, runs[which[1]] == run
            base = run * per_run

            @pl.when(mine | theirs)
            def _(run=run, mine=mine):
                slot = jnp.where(mine, 0, 1)
                for w in range(run * per_run, (run + 1) * per_run):
                    spot = spots[w]
                    if spot is None:
                        continue
                    j = w - base
                    k, row, col = spot
                    copy = pltpu.make_async_copy(
                        buf.at[slot * per_run + j],
                        outs[k].at[pl.ds(row, rows), pl.ds(col, buf.shape[2])],
                        sems.at[slot * per_run + j],
                    )
                    if wait:
                        copy.wait()
                    else:
                        part = slice(j * rows, (j + 1) * rows)
                        value = jnp.where(mine, p0[part, :], p1[part, :])
                        buf[slot * per_run + j] = value.astype(F32)
                        copy.start()


def place(runs, which, pieces, kinds, after, outs=()):
    length, width = pieces[0].shape
    quarter = width // 4
    per_run = length // quarter
    spots, shapes = [None] * (4 * per_run), []
    first = 0
    for k, count in enumerate(kinds):
        across = min(count, 2)
        for i in range(count):
            for section in range(2):
                for u in range(2):
                    w = section * 2 * per_run + 2 * (first + i) + u
                    row = (i // across) * width + (2 * section + u) * quarter
                    spots[w] = (k, row, (i % across) * width)
        shapes.append(struct(width * max(count // 2, 1), across * width, F32))
        first += count
    return pl.pallas_call(
        functools.partial(place_kernel, which, spots),
        in_specs=[IN_SMEM] + [IN_VMEM] * 2 + [ANYWHERE] + [IN_HBM] * len(outs),
        out_specs=[IN_HBM] * len(kinds) + [IN_VMEM],
        out_shape=shapes + [struct(8, 128, F32)],
        input_output_aliases={4 + k: k for k in range(len(outs))},
        scratch_shapes=[
            pltpu.VMEM((2 * per_run, quarter, width), F32),
            pltpu.SemaphoreType.DMA((2 * per_run,)),
        ],
        compiler_params=pltpu.CompilerParams(vmem_limit_bytes=24 * 1024 * 1024),
        cost_estimate=SMALL,
        name="place",
    )(runs, *pieces, after, *outs)


def step_kernel(group, rows_ref, after_ref, out_ref, mark):
    mark[...] = jnp.zeros_like(mark)
    width = rows_ref.shape[1]
    rows = rows_ref[: rows_ref.shape[0] - EDGE, :].astype(F32).reshape(-1, 2 * group, width)
    emb = rows[:, :group].reshape(-1, width).astype(BF16)
    out_ref[...] = tn(emb, rows[:, group:].reshape(-1, width).astype(BF16))


def padded(x, rows):
    return x if x.shape[0] == rows else jnp.pad(x, ((0, rows - x.shape[0]), (0, 0)))


def on_device(
    input_rows,
    conditioning,
    prompt,
    buckets,
    item_len,
    step_index,
    output_gradient,
    grad_skip,
    step_w,
    conv_w,
    cond_w,
    conv_b,
    res_w,
    res_b,
    query_w,
    key_w,
    value_w,
    out_w,
    out_b,
):
    section = lax.axis_index("section")
    sec = section.astype(jnp.int32).reshape(1)
    total, width = input_rows.shape
    micro, slots = item_len.shape
    nq = prompt.shape[2]
    frames = total // micro
    tile = frames // slots
    own = total // 2
    tiles = own // tile
    subs = 2
    size = subs * tile
    grid = tiles // subs
    mb_own = -(-own // frames)
    items = mb_own * slots
    half = width // 2
    taps = conv_w.shape[0]
    per = size // EDGE
    last = total // EDGE - 1
    wide = 2 * width
    conv_flat = conv_w.reshape(taps * width, wide)
    flat_prompt = prompt.reshape(-1, width)
    head = width // HEADS
    mask = (
        jnp.arange(HEADS * nq)[:, None] // nq == jnp.arange(width)[None, :] // head
    ).astype(BF16)

    def whole(x):
        n = x.ndim
        return pl.BlockSpec(x.shape, lambda t, *_: (0,) * n, pipeline_mode=pl.Buffered(1))

    smem = pl.BlockSpec(memory_space=pltpu.SMEM)

    def chip_tile(cols):
        return pl.BlockSpec((size, cols), lambda t, s, *_: (s[0] * grid + t, 0))

    def own_tile(cols):
        return pl.BlockSpec((size, cols), lambda t, *_: (t, 0))

    def const(shape):
        return pl.BlockSpec(shape, lambda t, *_: (0,) * len(shape))

    prev_chip = pl.BlockSpec(
        (EDGE, width), lambda t, s, *_: (jnp.maximum((s[0] * grid + t) * per - 1, 0), 0)
    )
    next_chip = pl.BlockSpec(
        (EDGE, width), lambda t, s, *_: (jnp.minimum((s[0] * grid + t + 1) * per, last), 0)
    )
    vectors = [x.reshape(1, -1) for x in (conv_b, res_b, out_b)]
    weights = [
        step_w,
        conv_flat,
        cond_w,
        vectors[0],
        res_w,
        vectors[1],
        query_w,
        key_w,
        value_w,
        out_w,
        vectors[2],
    ]

    def shape(*dims, dtype=BF16):
        return jax.ShapeDtypeStruct(dims, dtype)

    macs = own * width * width * 25
    (
        stack,
        d_pre,
        d_sent,
        block_keep,
        block_give,
        skip_keep,
        skip_give,
        keep_a,
        give_a,
        vec,
        emb,
    ) = pl.pallas_call(
        functools.partial(forward_kernel, (tile, slots, nq, subs, tiles, mb_own, micro)),
        grid_spec=pltpu.PrefetchScalarGridSpec(
            num_scalar_prefetch=1,
            grid=(grid,),
            in_specs=[smem, smem, smem, prev_chip, chip_tile(width), next_chip]
            + [chip_tile(width)] * 3
            + [whole(flat_prompt), whole(mask)]
            + [whole(w) for w in weights],
            out_specs=[own_tile(taps * width), own_tile(wide), own_tile(width)]
            + [own_tile(half)] * 4
            + [const((7, half, width)), const((7, half, width)), const((16, width))]
            + [const((items, width))],
            scratch_shapes=[
                pltpu.VMEM((items, width), F32),
                pltpu.VMEM((items * nq, width), BF16),
                pltpu.VMEM((items * nq, width), BF16),
                pltpu.VMEM((items * nq, width), F32),
                pltpu.VMEM((items * nq, width), F32),
                pltpu.VMEM((width, wide), F32),
                pltpu.VMEM((width, wide), F32),
                pltpu.VMEM((width, width), F32),
                pltpu.VMEM((3, 8, wide), F32),
                pltpu.VMEM((3, 8, width), F32),
                pltpu.SMEM((1,), jnp.int32),
            ],
        ),
        out_shape=[
            shape(own, taps * width),
            shape(own, wide),
            shape(own, width),
            shape(own, half),
            shape(own, half),
            shape(own, half),
            shape(own, half),
            shape(7, half, width),
            shape(7, half, width),
            shape(16, width, dtype=F32),
            shape(items, width, dtype=F32),
        ],
        compiler_params=pltpu.CompilerParams(vmem_limit_bytes=VMEM),
        cost_estimate=LARGE,
        name="forward",
    )(
        sec,
        buckets,
        item_len,
        step_index,
        input_rows,
        input_rows,
        input_rows,
        conditioning,
        output_gradient,
        grad_skip,
        flat_prompt,
        mask,
        *weights,
    )

    edge = swap(jnp.concatenate([d_pre[:EDGE], d_pre[own - EDGE :]], axis=0))

    bits = list(range(lax.axis_size("dp").bit_length() - 1))
    other = [bits[1], bits[0]] + bits[2:]
    if len(other) > 3:
        other[-2], other[-1] = other[-1], other[-2]
    sums = Sum((bits, other))
    unit = 16 * lax.axis_size("dp") // 2

    film_blocks = 7
    rows_a = -(-film_blocks * half // unit) * unit
    batch_a = Batch(
        sums,
        padded(keep_a.reshape(-1, width), rows_a),
        padded(give_a.reshape(-1, width), rows_a),
    )
    conv_blocks = 2 * (taps + 1)
    pair = pl.BlockSpec((2, half, width), lambda i, *_: (i, 0, 0))
    keep_b, give_b = pl.pallas_call(
        functools.partial(weight_kernel, taps),
        grid_spec=pltpu.PrefetchScalarGridSpec(
            num_scalar_prefetch=1,
            grid=(taps + 1,),
            in_specs=[
                pl.BlockSpec((own, width), lambda i, s: (0, jnp.minimum(i, taps - 1))),
                pl.BlockSpec(
                    (own, width), lambda i, s: (s[0], 0), pipeline_mode=pl.Buffered(1)
                ),
                whole(d_pre),
            ],
            out_specs=[pair, pair],
            scratch_shapes=[pltpu.VMEM((width, wide), F32)],
        ),
        out_shape=[shape(conv_blocks, half, width)] * 2,
        compiler_params=pltpu.CompilerParams(vmem_limit_bytes=KB_VMEM),
        cost_estimate=LARGE,
        name="weights",
    )(sec, stack, conditioning, d_pre)

    rows_b = -(-conv_blocks * half // unit) * unit
    batch_b = Batch(
        sums,
        padded(keep_b.reshape(-1, width), rows_b),
        padded(give_b.reshape(-1, width), rows_b),
    )
    (after,) = batch_a.turn(keep_b)
    (after,) = batch_b.turn(after)

    rows_last = own // EDGE - 1
    in_keep, in_give, rows_now = pl.pallas_call(
        functools.partial(back_kernel, (tile, slots, subs, tiles, mb_own, micro)),
        grid_spec=pltpu.PrefetchScalarGridSpec(
            num_scalar_prefetch=1,
            grid=(grid,),
            in_specs=[
                smem,
                smem,
                pl.BlockSpec((EDGE, wide), lambda t, *_: (jnp.maximum(t * per - 1, 0), 0)),
                own_tile(wide),
                pl.BlockSpec(
                    (EDGE, wide), lambda t, *_: (jnp.minimum((t + 1) * per, rows_last), 0)
                ),
                whole(edge),
                own_tile(width),
                whole(conv_flat),
                whole(emb),
                whole(vec),
                ANYWHERE,
            ],
            out_specs=[own_tile(half), own_tile(half), const((2 * items + EDGE, width))],
            scratch_shapes=[pltpu.VMEM((items, width), F32)],
        ),
        out_shape=[shape(own, half), shape(own, half), shape(2 * items + EDGE, width)],
        compiler_params=pltpu.CompilerParams(vmem_limit_bytes=KC_VMEM),
        cost_estimate=LARGE,
        name="back",
    )(
        sec,
        buckets,
        item_len,
        d_pre,
        d_pre,
        d_pre,
        edge,
        d_sent,
        conv_flat,
        emb,
        vec,
        after,
    )

    block_got, skip_got, in_got = swap(block_give), swap(skip_give), swap(in_give)
    gathers = sums.levels + 1
    rows_got, rows_bit = swap(rows_now), sec

    block_out, skip_out, after = join(
        sec, rows_now, (block_keep, block_got), (skip_keep, skip_got)
    )
    done = 0
    for name in "ab" * (batch_a.turns - 1):
        if name == "b" and done < gathers:
            n = 2 * rows_now.shape[0] - EDGE
            work = (gather_body, rows_bit, rows_now, rows_got, [struct(n, width)])
            after, rows_now = batch_b.turn(after, [work])
            if done < sums.levels:
                route = [(d, d ^ (1 << done)) for d in range(sums.chips)]
                rows_got = lax.ppermute(rows_now, "dp", route)
                rows_bit = ((sums.chip >> done) & 1).astype(jnp.int32).reshape(1)
            done += 1
        else:
            cost = LARGE if done else SMALL
            (after,) = (batch_a if name == "a" else batch_b).turn(after, cost=cost)

    in_grad, mark = join(sec, after, (in_keep, in_got))
    g_step, mark = pl.pallas_call(
        functools.partial(step_kernel, items),
        in_specs=[IN_VMEM, ANYWHERE],
        out_specs=[IN_VMEM, IN_VMEM],
        out_shape=[struct(width, width, F32), struct(8, 128, F32)],
        compiler_params=pltpu.CompilerParams(vmem_limit_bytes=24 * 1024 * 1024),
        cost_estimate=SMALL,
        name="step_grad",
    )(rows_now, mark)
    g_out, g_res, g_query, g_key, g_value, mark = batch_a.spread((2, 2, 1, 1, 1), mark)
    g_conv, g_cond, mark = batch_b.spread((2 * taps, 2), mark)
    vec = rows_now[rows_now.shape[0] - EDGE :].astype(F32)
    g_conv = g_conv.reshape(conv_w.shape)
    g_convb, g_resb, g_outb = (vec[2 * i : 2 * i + 2].reshape(wide) for i in range(3))
    sizes = jnp.sum(vec[6:9], axis=1)
    frames_valid = sum(vec[9, i] * (1 << 3 * i) for i in range(8))
    levels = jnp.sqrt(sizes / (frames_valid * width))
    return (
        block_out,
        skip_out,
        in_grad,
        g_step,
        g_conv,
        g_cond,
        g_convb,
        g_res,
        g_resb,
        g_query,
        g_key,
        g_value,
        g_out,
        g_outb,
        levels,
    )


def solution(mesh):
    rows = P("dp", None)
    split = P("dp", "section")
    return jax.shard_map(
        on_device,
        mesh=mesh,
        in_specs=(rows, rows, P("dp", None, None, None), P("dp"), rows, rows, rows, rows)
        + (P(),) * 11,
        out_specs=(split,) * 3 + (P(),) * 12,
        check_vma=False,
    )
```

```python
import functools
import math

import jax
import jax.numpy as jnp
from jax import lax
from jax.experimental import pallas as pl
from jax.experimental.pallas import tpu as pltpu
from jax.sharding import PartitionSpec as P

HEADS = 8
SHIFT = 2
EDGE = 16
ISQ2 = 0.7071067811865476
F32 = jnp.float32
BF16 = jnp.bfloat16
VMEM = 56 * 1024 * 1024
KB_VMEM = 48 * 1024 * 1024
KC_VMEM = 48 * 1024 * 1024


def nn(a, b):
    return lax.dot_general(a, b, (((1,), (0,)), ((), ())), preferred_element_type=F32)


def nt(a, b):
    return lax.dot_general(a, b, (((1,), (1,)), ((), ())), preferred_element_type=F32)


def tn(a, b):
    return lax.dot_general(a, b, (((0,), (0,)), ((), ())), preferred_element_type=F32)


def rows_iota(rows, cols):
    return lax.broadcasted_iota(jnp.int32, (rows, cols), 0)


def col_sums(x):
    rows, cols = x.shape
    return jnp.sum(x.reshape(rows // 8, 8, cols), axis=0)


def plan(g, tile, slots, buckets, item_len):
    mb = g // slots
    q = g - mb * slots
    span = slots >> buckets[mb]
    slot = q // span
    off = q - slot * span
    lim = item_len[mb, slot] - off * tile
    return mb, slot, lim, off > 0, off < span - 1


def forward_kernel(
    cfg,
    sec_ref,
    buckets,
    item_len,
    steps,
    prev_ref,
    rows_ref,
    next_ref,
    cond_ref,
    gout_ref,
    prompt_ref,
    mask_ref,
    step_w,
    conv_w,
    cond_w,
    conv_b,
    res_w,
    res_b,
    query_w,
    key_w,
    value_w,
    out_w,
    out_b,
    o_stack,
    o_slope,
    o_gate,
    o_dsent,
    o_block_keep,
    o_block_give,
    o_skip_keep,
    o_skip_give,
    o_keep,
    o_give,
    o_vec,
    o_emb,
    proj,
    keys,
    values,
    d_keys,
    d_values,
    g_out,
    g_query,
    sums,
    stats,
    count,
    out_t,
    query_t,
):
    tile, slots, nq, subs, tiles, mb_own, micro = cfg
    t = pl.program_id(0)
    section = sec_ref[0]
    size = subs * tile
    width = rows_ref.shape[1]
    half = width // 2
    head = width // HEADS
    mb0 = section * (micro - mb_own)
    items = mb_own * slots
    keep_left = section == 0

    @pl.when(t == 0)
    def _():
        row = rows_iota(items, half)
        when = jnp.zeros((items, half), F32)
        for i in range(items):
            s = steps[mb0 + i // slots, i % slots].astype(F32)
            when = jnp.where(row == i, s, when)
        lane = lax.broadcasted_iota(jnp.int32, (items, half), 1).astype(F32)
        angle = when * jnp.exp(lane * F32(-math.log(10000.0) / half))
        emb = jnp.concatenate([jnp.sin(angle), jnp.cos(angle)], axis=1)
        o_emb[...] = emb
        proj[...] = nn(emb.astype(BF16), step_w[...])
        here = prompt_ref[pl.ds(pl.multiple_of(mb0 * slots * nq, 16), items * nq), :]
        factor = head ** (-0.5)
        keys[...] = (nn(here, key_w[...]).astype(BF16) * BF16(factor)).astype(BF16)
        values[...] = nn(here, value_w[...]).astype(BF16)
        d_keys[...] = jnp.zeros_like(d_keys)
        d_values[...] = jnp.zeros_like(d_values)
        g_out[...] = jnp.zeros_like(g_out)
        out_t[...] = out_w[...].T
        query_t[...] = query_w[...].T
        g_query[...] = jnp.zeros_like(g_query)
        sums[...] = jnp.zeros_like(sums)
        stats[...] = jnp.zeros_like(stats)
        count[0] = 0

    ext = jnp.concatenate([prev_ref[...], rows_ref[...], next_ref[...]], axis=0)
    place = rows_iota(tile + 2 * EDGE, width)
    spread = tile + 2 * EDGE
    mixed, behind, ahead, at = [], [], [], []
    limit = jnp.zeros((size, width), jnp.int32)
    row = rows_iota(size, width)
    for k in range(subs):
        mb, slot, lim, prev_in, next_in = plan(
            section * tiles + t * subs + k, tile, slots, buckets, item_len
        )
        item = (mb - mb0) * slots + slot
        at.append(pl.multiple_of(item * nq, nq))
        lo = jnp.where(prev_in, 0, EDGE)
        hi = jnp.where(next_in, tile + 2 * EDGE, tile + EDGE)
        hi = jnp.minimum(hi, lim + EDGE)
        part = ext[k * tile : k * tile + spread].astype(F32) + proj[pl.ds(item, 1), :]
        part = jnp.where((place >= lo) & (place < hi), part, 0.0)
        mixed.append(part[EDGE : EDGE + tile])
        behind.append(pltpu.roll(part, SHIFT, 0)[EDGE : EDGE + tile].astype(BF16))
        ahead.append(pltpu.roll(part, spread - SHIFT, 0)[EDGE : EDGE + tile].astype(BF16))
        limit = jnp.where(row >= k * tile, lim + k * tile, limit)
        count[0] += jnp.clip(lim, 0, tile)
    mixed = jnp.concatenate(mixed, axis=0)
    valid = row < limit
    stacked = jnp.concatenate(
        [jnp.concatenate(behind, axis=0), mixed.astype(BF16), jnp.concatenate(ahead, axis=0)],
        axis=1,
    )
    o_stack[...] = stacked
    pre = nn(stacked, conv_w[...]) + nn(cond_ref[...], cond_w[...]) + conv_b[...]
    a = jnp.tanh(pre[:, :width])
    s = 0.5 * jnp.tanh(0.5 * pre[:, width:]) + 0.5
    both = a * s
    gate = both.astype(BF16)
    o_gate[...] = gate
    o_slope[...] = jnp.concatenate(
        [(s - both * a).astype(BF16), (both - both * s).astype(BF16)], axis=1
    )
    branch = nn(gate, res_w[...]) + res_b[...]
    res_part = jnp.where(valid, branch[:, :width], 0.0)
    skip = jnp.where(valid, branch[:, width:], 0.0).astype(BF16)
    o_skip_keep[...] = jnp.where(keep_left, skip[:, :half], skip[:, half:])
    o_skip_give[...] = jnp.where(keep_left, skip[:, half:], skip[:, :half])
    hidden = (mixed + res_part) * ISQ2
    sent = hidden.astype(BF16)
    sent_f = sent.astype(F32)
    stats[0] += col_sums(hidden * hidden)
    stats[1] += col_sums(res_part * res_part)

    query = nn(sent, query_w[...]).astype(BF16)
    mask = mask_ref[...]
    probs, probs_low, key_bd, value_bd, attended = [], [], [], [], []
    for k in range(subs):
        key_bd.append(jnp.concatenate([keys[pl.ds(at[k], nq), :]] * HEADS, axis=0) * mask)
        value_bd.append(jnp.concatenate([values[pl.ds(at[k], nq), :]] * HEADS, axis=0) * mask)
        scores = nt(key_bd[k], query[k * tile : (k + 1) * tile]).reshape(HEADS, nq, tile)
        expo = jnp.exp(scores - jnp.max(scores, axis=1, keepdims=True))
        probs.append(expo * (1.0 / jnp.sum(expo, axis=1, keepdims=True)))
        probs_low.append(probs[k].astype(BF16).reshape(HEADS * nq, tile))
        attended.append(tn(probs_low[k], value_bd[k]).astype(BF16))
    attended = jnp.concatenate(attended, axis=0)
    film = nn(attended, out_w[...]) + out_b[...]
    scale = film[:, :width]
    change = jnp.where(valid, sent_f * scale + film[:, width:], 0.0)
    block = (sent_f + change).astype(BF16)
    o_block_keep[...] = jnp.where(keep_left, block[:, :half], block[:, half:])
    o_block_give[...] = jnp.where(keep_left, block[:, half:], block[:, :half])
    stats[2] += col_sums(change * change)

    gy = jnp.where(valid, gout_ref[...].astype(F32), 0.0)
    d_film = jnp.concatenate([(gy * sent_f).astype(BF16), gy.astype(BF16)], axis=1)
    sums[...] += col_sums(d_film.astype(F32))
    g_out[...] += tn(attended, d_film)
    d_att = nn(d_film, out_t[...]).astype(BF16)
    low_lane = lax.broadcasted_iota(jnp.int32, (nq, 2 * head), 1) < head

    def own_heads(x):
        pieces = []
        for p in range(HEADS // 2):
            at_row, at_lane = 2 * p * nq, 2 * p * head
            first = x[at_row : at_row + nq, at_lane : at_lane + 2 * head]
            second = x[at_row + nq : at_row + 2 * nq, at_lane : at_lane + 2 * head]
            pieces.append(jnp.where(low_lane, first, second))
        return jnp.concatenate(pieces, axis=1)

    d_query = []
    for k in range(subs):
        here = slice(k * tile, (k + 1) * tile)
        d_probs = nt(value_bd[k], d_att[here]).reshape(HEADS, nq, tile)
        weighted = probs[k] * d_probs
        inner = jnp.sum(weighted, axis=1, keepdims=True)
        d_scores = (weighted - probs[k] * inner).astype(BF16).reshape(HEADS * nq, tile)
        d_values[pl.ds(at[k], nq), :] += own_heads(nn(probs_low[k], d_att[here]))
        d_keys[pl.ds(at[k], nq), :] += own_heads(nn(d_scores, query[here]))
        d_query.append(tn(d_scores, key_bd[k]).astype(BF16))
    d_query = jnp.concatenate(d_query, axis=0)
    g_query[...] += tn(sent, d_query)
    d_sent = (gy * (1.0 + scale) + nn(d_query, query_t[...])).astype(BF16)
    o_dsent[...] = d_sent

    @pl.when(t == tiles // subs - 1)
    def _():
        here = prompt_ref[pl.ds(pl.multiple_of(mb0 * slots * nq, 16), items * nq), :]
        factor = head ** (-0.5)
        mine = pl.multiple_of(section * half, half)
        theirs = pl.multiple_of(half - section * half, half)

        def put(i, ref, left):
            o_keep[i] = ref[pl.ds(mine, half), pl.ds(left, width)].astype(BF16)
            o_give[i] = ref[pl.ds(theirs, half), pl.ds(left, width)].astype(BF16)

        put(0, g_out, 0)
        put(1, g_out, width)
        put(2, g_query, 0)
        g_query[...] = tn(here, (d_keys[...] * factor).astype(BF16))
        put(3, g_query, 0)
        g_query[...] = tn(here, d_values[...].astype(BF16))
        put(4, g_query, 0)
        o_vec[0:4, :] = jnp.zeros((4, width), F32)
        line = jnp.sum(sums[...], axis=0, keepdims=True)
        o_vec[4:5, :] = line[:, :width]
        o_vec[5:6, :] = line[:, width:]
        for i in range(3):
            o_vec[6 + i : 7 + i, :] = jnp.sum(stats[i], axis=0, keepdims=True)
        lane = lax.broadcasted_iota(jnp.int32, (16 - 9, width), 1)
        digits = (count[0] >> (3 * jnp.minimum(lane, 8))) & 7
        o_vec[9:16, :] = jnp.where(lane < 8, digits, 0).astype(F32)


def branch_kernel(
    cfg,
    sec_ref,
    buckets,
    item_len,
    gskip_ref,
    dsent_ref,
    slope_ref,
    gate_ref,
    res_w,
    o_dpre,
    o_edge,
    o_vec,
    o_keep,
    o_give,
    g_res,
    res_t,
    sums,
):
    tile, slots, subs, tiles = cfg
    t = pl.program_id(0)
    section = sec_ref[0]
    size = subs * tile
    width = dsent_ref.shape[1]
    half = width // 2
    last = tiles // subs - 1

    @pl.when(t == 0)
    def _():
        res_t[...] = res_w[...].T
        g_res[...] = jnp.zeros_like(g_res)
        sums[...] = jnp.zeros_like(sums)

    row = rows_iota(size, width)
    limit = jnp.zeros((size, width), jnp.int32)
    for k in range(subs):
        lim = plan(section * tiles + t * subs + k, tile, slots, buckets, item_len)[2]
        limit = jnp.where(row >= k * tile, lim + k * tile, limit)
    d_res = (dsent_ref[...].astype(F32) * ISQ2).astype(BF16)
    gs = jnp.where(row < limit, gskip_ref[...].astype(F32), 0.0).astype(BF16)
    d_branch = jnp.concatenate([d_res, gs], axis=1)
    sums[1] += col_sums(d_branch.astype(F32))
    g_res[...] += tn(gate_ref[...], d_branch)
    d_gate = nn(d_branch, res_t[...])
    slope = slope_ref[...].astype(F32)
    d_pre = jnp.concatenate(
        [(d_gate * slope[:, :width]).astype(BF16), (d_gate * slope[:, width:]).astype(BF16)],
        axis=1,
    )
    sums[0] += col_sums(d_pre.astype(F32))
    o_dpre[...] = d_pre

    @pl.when(t == 0)
    def _():
        o_edge[:EDGE, :] = d_pre[:EDGE, :]

    @pl.when(t == last)
    def _():
        o_edge[EDGE:, :] = d_pre[size - EDGE :, :]
        mine = pl.multiple_of(section * half, half)
        theirs = pl.multiple_of(half - section * half, half)
        for side in range(2):
            o_keep[side] = g_res[pl.ds(mine, half), pl.ds(side * width, width)].astype(BF16)
            o_give[side] = g_res[pl.ds(theirs, half), pl.ds(side * width, width)].astype(BF16)
        for i in range(2):
            line = jnp.sum(sums[i], axis=0, keepdims=True)
            o_vec[2 * i : 2 * i + 1, :] = line[:, :width]
            o_vec[2 * i + 1 : 2 * i + 2, :] = line[:, width:]
        o_vec[4:16, :] = jnp.zeros((12, width), F32)


def weight_kernel(sec_ref, left_ref, dpre_ref, *refs):
    o_keep, o_give, acc = refs[-3:]
    section = sec_ref[0]
    width = acc.shape[0]
    half = width // 2
    acc[...] = tn(left_ref[...], dpre_ref[...])
    mine = pl.multiple_of(section * half, half)
    theirs = pl.multiple_of(half - section * half, half)
    for side in range(2):
        o_keep[side] = acc[pl.ds(mine, half), pl.ds(side * width, width)].astype(BF16)
        o_give[side] = acc[pl.ds(theirs, half), pl.ds(side * width, width)].astype(BF16)


def back_kernel(
    cfg,
    sec_ref,
    buckets,
    item_len,
    dpre_ref,
    other_ref,
    dsent_ref,
    conv_w,
    steps,
    vec_ref,
    vec_more,
    after_ref,
    o_keep,
    o_give,
    o_rows,
    acc,
    d_step,
):
    tile, slots, tiles, micro = cfg
    tap = pl.program_id(0)
    section = sec_ref[0]
    width = dsent_ref.shape[1]
    half = width // 2
    plans = [plan(section * tiles + k, tile, slots, buckets, item_len) for k in range(tiles)]
    spread = tile + 2 * EDGE

    def moved(offset):
        place = rows_iota(spread, 2 * width)
        pieces = []
        for k in range(tiles):
            lo = jnp.where(plans[k][3], 0, EDGE)
            hi = jnp.where(plans[k][4], spread, tile + EDGE)
            before = dpre_ref[k * tile - EDGE : k * tile, :] if k else other_ref[EDGE:, :]
            here = dpre_ref[k * tile : (k + 1) * tile, :]
            end = (k + 1) * tile
            after = dpre_ref[end : end + EDGE, :] if k < tiles - 1 else other_ref[:EDGE, :]
            part = jnp.concatenate([before, here, after], axis=0).astype(F32)
            part = jnp.where((place >= lo) & (place < hi), part, 0.0)
            part = pltpu.roll(part, (spread - offset) % spread, 0)
            pieces.append(part[EDGE : EDGE + tile].astype(BF16))
        return jnp.concatenate(pieces, axis=0)

    @pl.when(tap == 0)
    def _():
        acc[...] = nt(moved(SHIFT), conv_w[...])

    @pl.when(tap == 1)
    def _():
        acc[...] += nt(dpre_ref[...], conv_w[...])

    @pl.when(tap == 2)
    def _():
        acc[...] += nt(moved(-SHIFT), conv_w[...])
        items = micro * slots
        group = d_step.shape[0]
        d_step[...] = jnp.zeros_like(d_step)
        for k in range(tiles):
            mb, slot, lim = plans[k][:3]
            rows = slice(k * tile, (k + 1) * tile)
            d_mixed = dsent_ref[rows, :].astype(F32) * ISQ2 + acc[rows, :]
            d_mixed = jnp.where(rows_iota(tile, width) < lim, d_mixed, 0.0)
            line = jnp.sum(col_sums(d_mixed), axis=0, keepdims=True)
            d_step[pl.ds(mb * slots + slot, 1), :] += line
            low = d_mixed.astype(BF16)
            o_keep[rows, :] = jnp.where(section == 0, low[:, :half], low[:, half:])
            o_give[rows, :] = jnp.where(section == 0, low[:, half:], low[:, :half])
        lane = lax.broadcasted_iota(jnp.int32, (1, width), 1)
        index = jnp.zeros((1, width), jnp.int32)
        for i in range(items):
            index = jnp.where(lane == i, steps[i // slots, i % slots], index)
        index = jnp.where(section == 0, index, 0)
        d_step[items : items + 1, :] = (index >> 5).astype(F32)
        d_step[items + 1 : items + 2, :] = (index & 31).astype(F32)
        o_rows[:group, :] = d_step[...].astype(BF16)
        o_rows[group:, :] = (vec_ref[...] + vec_more[...]).astype(BF16)


SMALL = pl.CostEstimate(flops=1024, bytes_accessed=1024, transcendentals=0)
LARGE = pl.CostEstimate(flops=1 << 36, bytes_accessed=1024, transcendentals=0)
ANYWHERE = pl.BlockSpec(memory_space=pl.ANY)
PARAMS = pltpu.CompilerParams(vmem_limit_bytes=VMEM)


IN_VMEM = pl.BlockSpec(memory_space=pltpu.VMEM)
IN_SMEM = pl.BlockSpec(memory_space=pltpu.SMEM)
IN_HBM = pl.BlockSpec(memory_space=pltpu.HBM)


def struct(rows, width, dtype=BF16):
    return jax.ShapeDtypeStruct((rows, width), dtype)


def total(a, b):
    return (a.astype(F32) + b.astype(F32)).astype(BF16)


def at_bit(bit, rows):
    return pl.ds(pl.multiple_of(bit * rows, 16), rows)


def split_body(bit, held, got, keep, give):
    rows = keep.shape[0]
    keep[...] = total(held[at_bit(bit, rows), :], got[at_bit(bit, rows), :])
    give[...] = total(held[at_bit(1 - bit, rows), :], got[at_bit(1 - bit, rows), :])


def add_body(bit, held, got, out):
    out[...] = total(held[...], got[...])


def merge_body(bit, cur, got, out):
    rows = cur.shape[0]
    out[at_bit(bit, rows), :] = cur[...]
    out[at_bit(1 - bit, rows), :] = got[...]


def gather_body(bit, cur, got, out):
    rows = cur.shape[0] - EDGE
    out[at_bit(bit, rows), :] = cur[:rows, :]
    out[at_bit(1 - bit, rows), :] = got[:rows, :]
    out[2 * rows :, :] = total(cur[rows:, :], got[rows:, :])


def pair_kernel(bodies, outs, *refs):
    n = len(bodies)
    bits, arrays, results = refs[:n], refs[n : 3 * n], refs[3 * n + 1 :]
    for i, body in enumerate(bodies):
        count = outs[i]
        body(bits[i][0], arrays[2 * i], arrays[2 * i + 1], *results[:count])
        results = results[count:]


def pair_call(works, after, cost):
    outs = [len(w[4]) for w in works]
    shapes = [x for w in works for x in w[4]]
    return pl.pallas_call(
        functools.partial(pair_kernel, [w[0] for w in works], outs),
        in_specs=[IN_SMEM] * len(works) + [IN_VMEM] * (2 * len(works)) + [ANYWHERE],
        out_specs=[IN_VMEM] * len(shapes),
        out_shape=shapes,
        compiler_params=pltpu.CompilerParams(vmem_limit_bytes=24 * 1024 * 1024),
        cost_estimate=cost,
        name=works[0][0].__name__,
    )(*[w[1] for w in works], *[x for w in works for x in w[2:4]], after)


def then_kernel(x_ref, after_ref, out_ref):
    out_ref[...] = x_ref[...]


def then(x, after):
    return pl.pallas_call(
        then_kernel,
        in_specs=[IN_VMEM, ANYWHERE],
        out_specs=IN_VMEM,
        out_shape=jax.ShapeDtypeStruct(x.shape, x.dtype),
        compiler_params=pltpu.CompilerParams(vmem_limit_bytes=16 * 1024 * 1024),
        cost_estimate=SMALL,
        name="then",
    )(x, after)


def join_kernel(count, sec_ref, *refs):
    section = sec_ref[0]
    arrays, outs = refs[: 2 * count], refs[2 * count + 1 : 3 * count + 1]
    mark, sems = refs[-2:]
    mark[...] = jnp.zeros_like(mark)
    copies = []
    for i in range(count):
        rows = arrays[2 * i].shape[0]
        for j, place in enumerate((section, 1 - section)):
            copies.append(
                pltpu.make_async_copy(
                    arrays[2 * i + j], outs[i].at[at_bit(place, rows), :], sems.at[2 * i + j]
                )
            )
    for copy in copies:
        copy.start()
    for copy in copies:
        copy.wait()


def join(sec, after, *pairs):
    rows, width = pairs[0][0].shape
    count = len(pairs)
    return pl.pallas_call(
        functools.partial(join_kernel, count),
        in_specs=[IN_SMEM] + [IN_VMEM] * (2 * count) + [ANYWHERE],
        out_specs=[IN_HBM] * count + [IN_VMEM],
        out_shape=[struct(2 * rows, width)] * count + [struct(8, 128, F32)],
        scratch_shapes=[pltpu.SemaphoreType.DMA((2 * count,))],
        compiler_params=pltpu.CompilerParams(vmem_limit_bytes=16 * 1024 * 1024),
        cost_estimate=SMALL,
        name="join",
    )(sec, *[x for pair in pairs for x in pair], after)


def swap(x):
    return lax.ppermute(x, "section", [(0, 1), (1, 0)])


class Sum:
    def __init__(self, orders):
        self.chips = lax.axis_size("dp")
        self.section = lax.axis_index("section")
        self.chip = lax.axis_index("dp")
        self.orders = orders
        self.levels = len(orders[0])

    def bit_of(self, step, section):
        where = jnp.where(section == 0, self.orders[0][step], self.orders[1][step])
        return ((self.chip >> where) & 1).astype(jnp.int32)

    def bit(self, step):
        return self.bit_of(step, self.section).reshape(1)

    def send(self, x, step):
        chips = self.chips
        route = [
            (s * chips + d, s * chips + (d ^ (1 << self.orders[s][step])))
            for s in range(2)
            for d in range(chips)
        ]
        return lax.ppermute(x, ("section", "dp"), route)

    def runs(self):
        mine, theirs = self.section, 1 - self.section
        own, other = self.bit_of(0, mine), self.bit_of(0, theirs)
        return jnp.stack(
            [2 * mine + own, 2 * mine + 1 - own, 2 * theirs + other, 2 * theirs + 1 - other]
        ).astype(jnp.int32)


class Batch:
    def __init__(self, sums, keep, give):
        self.sums = sums
        self.held = keep
        self.got = swap(give)
        self.step = 0

    def turn(self, after, more=(), cost=LARGE):
        sums, last = self.sums, self.sums.levels - 1
        at = self.step
        self.step += 1
        rows, width = self.held.shape
        if at < last:
            work = (split_body, sums.bit(at), self.held, self.got, [struct(rows // 2, width)] * 2)
            self.held, give, *rest = pair_call([work, *more], after, cost)
            self.got = sums.send(give, at)
        elif at <= last + 1:
            work = (add_body, sums.bit(0), self.held, self.got, [struct(rows, width)])
            self.held, *rest = pair_call([work, *more], after, cost)
            self.got = sums.send(self.held, at if at == last else last - 1)
        else:
            back = 2 * last + 1 - at
            work = (merge_body, sums.bit(back), self.held, self.got, [struct(2 * rows, width)])
            self.held, *rest = pair_call([work, *more], after, cost)
            self.got = sums.send(self.held, back - 1)
        return (self.held, *rest)

    @property
    def turns(self):
        return 2 * self.sums.levels - 1

    def early(self, shapes, spots, after, outs=()):
        return place(self.sums.runs(), (0, 2), (self.held, swap(self.held)), shapes, spots, after, outs)

    def arrive(self, after):
        self.got = then(self.got, after)
        self.last = swap(self.got)
        return self.got

    def late(self, shapes, spots, after, outs):
        return place(self.sums.runs(), (1, 3), (self.got, self.last), shapes, spots, after, outs)


def place_kernel(which, spots, count, runs, p0, p1, after_ref, *refs):
    outs, (mark, buf, sems) = refs[-3 - count : -3], refs[-3:]
    mark[...] = jnp.zeros_like(mark)
    rows = buf.shape[1]
    per_run = p0.shape[0] // rows
    for wait in (False, True):
        for run in range(4):
            mine, theirs = runs[which[0]] == run, runs[which[1]] == run
            base = run * per_run

            @pl.when(mine | theirs)
            def _(run=run, mine=mine):
                slot = jnp.where(mine, 0, 1)
                for w in range(run * per_run, (run + 1) * per_run):
                    spot = spots[w]
                    if spot is None:
                        continue
                    j = w - base
                    k, row, col = spot
                    copy = pltpu.make_async_copy(
                        buf.at[slot * per_run + j],
                        outs[k].at[pl.ds(row, rows), pl.ds(col, buf.shape[2])],
                        sems.at[slot * per_run + j],
                    )
                    if wait:
                        copy.wait()
                    else:
                        part = slice(j * rows, (j + 1) * rows)
                        value = jnp.where(mine, p0[part, :], p1[part, :])
                        buf[slot * per_run + j] = value.astype(F32)
                        copy.start()


def spots_of(targets, width):
    quarter = width // 4
    spots = []
    for section in range(2):
        for k, row, col in targets:
            for u in range(2):
                spots.append((k, row + (2 * section + u) * quarter, col))
    return spots


def place(runs, which, pieces, shapes, spots, after, outs=()):
    length, width = pieces[0].shape
    quarter = width // 4
    per_run = length // quarter
    half = len(spots) // 2
    full = [None] * (4 * per_run)
    full[:half] = spots[:half]
    full[2 * per_run : 2 * per_run + half] = spots[half:]
    return pl.pallas_call(
        functools.partial(place_kernel, which, full, len(shapes)),
        in_specs=[IN_SMEM] + [IN_VMEM] * 2 + [ANYWHERE] + [IN_HBM] * len(outs),
        out_specs=[IN_HBM] * len(shapes) + [IN_VMEM],
        out_shape=list(shapes) + [struct(8, 128, F32)],
        input_output_aliases={4 + k: k for k in range(len(outs))},
        scratch_shapes=[
            pltpu.VMEM((2 * per_run, quarter, width), F32),
            pltpu.SemaphoreType.DMA((2 * per_run,)),
        ],
        compiler_params=pltpu.CompilerParams(vmem_limit_bytes=24 * 1024 * 1024),
        cost_estimate=SMALL,
        name="place",
    )(runs, *pieces, after, *outs)


def step_kernel(items, group, rows_ref, after_ref, out_ref, mark):
    mark[...] = jnp.zeros_like(mark)
    width = rows_ref.shape[1]
    half = width // 2
    rows = rows_ref[: rows_ref.shape[0] - EDGE, :].astype(F32).reshape(-1, group, width)
    lanes = (rows.shape[0], group, 128)
    index = 32.0 * rows[:, items : items + 1, :128] + rows[:, items + 1 : items + 2, :128]
    diagonal = lax.broadcasted_iota(jnp.int32, lanes, 1) == lax.broadcasted_iota(
        jnp.int32, lanes, 2
    )
    index = jnp.sum(jnp.where(diagonal, index, 0.0), axis=2, keepdims=True)
    index = index.reshape(-1, 1)
    lane = lax.broadcasted_iota(jnp.int32, (index.shape[0], half), 1).astype(F32)
    angle = index * jnp.exp(lane * F32(-math.log(10000.0) / half))
    emb = jnp.concatenate([jnp.sin(angle), jnp.cos(angle)], axis=1)
    used = lax.broadcasted_iota(jnp.int32, rows.shape, 1) < items
    sums = jnp.where(used, rows, 0.0).reshape(-1, width)
    out_ref[...] = tn(emb.astype(BF16), sums.astype(BF16))


def padded(x, rows):
    return x if x.shape[0] == rows else jnp.pad(x, ((0, rows - x.shape[0]), (0, 0)))


def on_device(
    input_rows,
    conditioning,
    prompt,
    buckets,
    item_len,
    step_index,
    output_gradient,
    grad_skip,
    step_w,
    conv_w,
    cond_w,
    conv_b,
    res_w,
    res_b,
    query_w,
    key_w,
    value_w,
    out_w,
    out_b,
):
    section = lax.axis_index("section")
    sec = section.astype(jnp.int32).reshape(1)
    total, width = input_rows.shape
    micro, slots = item_len.shape
    nq = prompt.shape[2]
    frames = total // micro
    tile = frames // slots
    own = total // 2
    tiles = own // tile
    subs = 2
    size = subs * tile
    grid = tiles // subs
    mb_own = -(-own // frames)
    items = mb_own * slots
    half = width // 2
    taps = conv_w.shape[0]
    per = size // EDGE
    last = total // EDGE - 1
    wide = 2 * width
    conv_flat = conv_w.reshape(taps * width, wide)
    flat_prompt = prompt.reshape(-1, width)
    head = width // HEADS
    mask = (
        jnp.arange(HEADS * nq)[:, None] // nq == jnp.arange(width)[None, :] // head
    ).astype(BF16)

    def whole(x):
        n = x.ndim
        return pl.BlockSpec(x.shape, lambda t, *_: (0,) * n, pipeline_mode=pl.Buffered(1))

    smem = pl.BlockSpec(memory_space=pltpu.SMEM)

    def chip_tile(cols):
        return pl.BlockSpec((size, cols), lambda t, s, *_: (s[0] * grid + t, 0))

    def own_tile(cols):
        return pl.BlockSpec((size, cols), lambda t, *_: (t, 0))

    def const(shape):
        return pl.BlockSpec(shape, lambda t, *_: (0,) * len(shape))

    prev_chip = pl.BlockSpec(
        (EDGE, width), lambda t, s, *_: (jnp.maximum((s[0] * grid + t) * per - 1, 0), 0)
    )
    next_chip = pl.BlockSpec(
        (EDGE, width), lambda t, s, *_: (jnp.minimum((s[0] * grid + t + 1) * per, last), 0)
    )
    vectors = [x.reshape(1, -1) for x in (conv_b, res_b, out_b)]
    weights = [
        step_w,
        conv_flat,
        cond_w,
        vectors[0],
        res_w,
        vectors[1],
        query_w,
        key_w,
        value_w,
        out_w,
        vectors[2],
    ]

    def shape(*dims, dtype=BF16):
        return jax.ShapeDtypeStruct(dims, dtype)

    def blocks_of(n):
        return const((n, half, width)), shape(n, half, width)

    film_blocks = 5
    film_spec, film_shape = blocks_of(film_blocks)
    (
        stack,
        slope,
        gate,
        d_sent,
        block_keep,
        block_give,
        skip_keep,
        skip_give,
        keep_a,
        give_a,
        vec,
        _,
    ) = pl.pallas_call(
        functools.partial(forward_kernel, (tile, slots, nq, subs, tiles, mb_own, micro)),
        grid_spec=pltpu.PrefetchScalarGridSpec(
            num_scalar_prefetch=1,
            grid=(grid,),
            in_specs=[smem, smem, smem, prev_chip, chip_tile(width), next_chip]
            + [chip_tile(width)] * 2
            + [whole(flat_prompt), whole(mask)]
            + [whole(w) for w in weights],
            out_specs=[own_tile(taps * width), own_tile(wide), own_tile(width), own_tile(width)]
            + [own_tile(half)] * 4
            + [film_spec, film_spec, const((16, width)), const((items, width))],
            scratch_shapes=[
                pltpu.VMEM((items, width), F32),
                pltpu.VMEM((items * nq, width), BF16),
                pltpu.VMEM((items * nq, width), BF16),
                pltpu.VMEM((items * nq, width), F32),
                pltpu.VMEM((items * nq, width), F32),
                pltpu.VMEM((width, wide), F32),
                pltpu.VMEM((width, width), F32),
                pltpu.VMEM((8, wide), F32),
                pltpu.VMEM((3, 8, width), F32),
                pltpu.SMEM((1,), jnp.int32),
                pltpu.VMEM((wide, width), BF16),
                pltpu.VMEM((width, width), BF16),
            ],
        ),
        out_shape=[
            shape(own, taps * width),
            shape(own, wide),
            shape(own, width),
            shape(own, width),
            shape(own, half),
            shape(own, half),
            shape(own, half),
            shape(own, half),
            film_shape,
            film_shape,
            shape(16, width, dtype=F32),
            shape(items, width, dtype=F32),
        ],
        compiler_params=pltpu.CompilerParams(vmem_limit_bytes=VMEM),
        cost_estimate=LARGE,
        name="forward",
    )(
        sec,
        buckets,
        item_len,
        step_index,
        input_rows,
        input_rows,
        input_rows,
        conditioning,
        output_gradient,
        flat_prompt,
        mask,
        *weights,
    )

    bits = list(range(lax.axis_size("dp").bit_length() - 1))
    other = [bits[1], bits[0]] + bits[2:]
    if len(other) > 3:
        other[-2], other[-1] = other[-1], other[-2]
    sums = Sum((bits, other))
    unit = 16 * lax.axis_size("dp") // 2

    def batch(keep, give):
        rows = keep.shape[0] * half
        rows = -(-rows // unit) * unit
        return Batch(
            sums, padded(keep.reshape(-1, width), rows), padded(give.reshape(-1, width), rows)
        )

    batch_a = batch(keep_a, give_a)
    block_got, skip_got = swap(block_give), swap(skip_give)

    side = pl.BlockSpec((2, half, width), lambda t, *_: (0, 0, 0))
    d_pre, edge, vec_more, keep_c, give_c = pl.pallas_call(
        functools.partial(branch_kernel, (tile, slots, subs, tiles)),
        grid_spec=pltpu.PrefetchScalarGridSpec(
            num_scalar_prefetch=1,
            grid=(grid,),
            in_specs=[smem, smem, chip_tile(width), own_tile(width), own_tile(wide)]
            + [own_tile(width), whole(res_w)],
            out_specs=[own_tile(wide), const((2 * EDGE, wide)), const((16, width)), side, side],
            scratch_shapes=[
                pltpu.VMEM((width, wide), F32),
                pltpu.VMEM((wide, width), BF16),
                pltpu.VMEM((2, 8, wide), F32),
            ],
        ),
        out_shape=[
            shape(own, wide),
            shape(2 * EDGE, wide),
            shape(16, width, dtype=F32),
            shape(4, half, width),
            shape(4, half, width),
        ],
        compiler_params=pltpu.CompilerParams(vmem_limit_bytes=KB_VMEM),
        cost_estimate=LARGE,
        name="branch",
    )(sec, buckets, item_len, grad_skip, d_sent, slope, gate, res_w)
    other_edge = swap(edge)
    (after,) = batch_a.turn(vec_more)

    def weight_grads(left, count, index, after, first=0, outs=(), total=0):
        spec = pl.BlockSpec((2, half, width), lambda i, *_: (first + i, 0, 0))
        return pl.pallas_call(
            weight_kernel,
            grid_spec=pltpu.PrefetchScalarGridSpec(
                num_scalar_prefetch=1,
                grid=(count,),
                in_specs=[pl.BlockSpec((own, width), index), whole(d_pre)]
                + [ANYWHERE] * (1 + len(outs)),
                out_specs=[spec, spec],
                scratch_shapes=[pltpu.VMEM((width, wide), F32)],
            ),
            out_shape=[shape(2 * (first + count), half, width)] * 2,
            input_output_aliases={4 + k: k for k in range(len(outs))},
            compiler_params=pltpu.CompilerParams(vmem_limit_bytes=KB_VMEM),
            cost_estimate=LARGE,
            name="weights",
        )(sec, left, d_pre, after, *outs)

    keep_b, give_b = weight_grads(stack, taps, lambda i, s: (0, i), after)
    batch_b = batch(keep_b, give_b)
    keep_c, give_c = weight_grads(
        conditioning, 1, lambda i, s: (s[0], 0), keep_b, 1, (keep_c, give_c)
    )
    batch_c = batch(keep_c, give_c)
    (after,) = batch_a.turn(keep_c)
    (after,) = batch_b.turn(after)
    (after,) = batch_c.turn(after)

    group = -(-(micro * slots + 2) // 16) * 16
    in_keep, in_give, rows_now = pl.pallas_call(
        functools.partial(back_kernel, (tile, slots, tiles, micro)),
        grid_spec=pltpu.PrefetchScalarGridSpec(
            num_scalar_prefetch=1,
            grid=(taps,),
            in_specs=[
                smem,
                smem,
                whole(d_pre),
                whole(edge),
                whole(d_sent),
                pl.BlockSpec((width, wide), lambda k, *_: (k, 0)),
                smem,
                whole(vec),
                whole(vec_more),
                ANYWHERE,
            ],
            out_specs=[const((own, half)), const((own, half)), const((group + EDGE, width))],
            scratch_shapes=[pltpu.VMEM((own, width), F32), pltpu.VMEM((group, width), F32)],
        ),
        out_shape=[shape(own, half), shape(own, half), shape(group + EDGE, width)],
        compiler_params=pltpu.CompilerParams(vmem_limit_bytes=KC_VMEM),
        cost_estimate=LARGE,
        name="back",
    )(
        sec,
        buckets,
        item_len,
        d_pre,
        other_edge,
        d_sent,
        conv_flat,
        step_index,
        vec,
        vec_more,
        after,
    )
    in_got = swap(in_give)

    block_out, skip_out, after = join(
        sec, rows_now, (block_keep, block_got), (skip_keep, skip_got)
    )
    rows_got, rows_bit, gathered = swap(rows_now), sec, 0
    batches = {"a": batch_a, "b": batch_b, "c": batch_c}
    first = True
    for name in "ab-c" * (batch_a.turns - 3) + "abcTbc":
        if name == "T":
            after = batch_a.arrive(after)
            continue
        if name == "-":
            first = False
            continue
        turner = batches[name]
        if name == "c" and gathered <= sums.levels:
            n = rows_now.shape[0]
            work = (add_body, rows_bit, rows_now, rows_got, [struct(n, width)])
            if gathered:
                work = (gather_body, rows_bit, rows_now, rows_got, [struct(2 * n - EDGE, width)])
            after, rows_now = turner.turn(after, [work])
            if gathered < sums.levels:
                route = [(d, d ^ (1 << gathered)) for d in range(sums.chips)]
                rows_got = lax.ppermute(rows_now, "dp", route)
                rows_bit = ((sums.chip >> gathered) & 1).astype(jnp.int32).reshape(1)
            gathered += 1
        else:
            (after,) = turner.turn(after, cost=SMALL if first else LARGE)

    in_grad, mark = join(sec, after, (in_keep, in_got))
    g_step, mark = pl.pallas_call(
        functools.partial(step_kernel, micro * slots, group),
        in_specs=[IN_VMEM, ANYWHERE],
        out_specs=[IN_VMEM, IN_VMEM],
        out_shape=[struct(width, width, F32), struct(8, 128, F32)],
        compiler_params=pltpu.CompilerParams(vmem_limit_bytes=24 * 1024 * 1024),
        cost_estimate=SMALL,
        name="step_grad",
    )(rows_now, mark)

    def pairs(k, count, base=0):
        return [(k, base + i * width, col) for i in range(count) for col in (0, width)]

    square, tall = struct(width, width, F32), struct(width, wide, F32)
    shapes_a = [tall, square, square, square]
    spots_a = spots_of(pairs(0, 1) + [(k, 0, 0) for k in (1, 2, 3)], width)
    shapes_b, spots_b = [struct(taps * width, wide, F32)], spots_of(pairs(0, taps), width)
    shapes_c, spots_c = [tall, tall], spots_of(pairs(0, 1) + pairs(1, 1), width)
    *outs_a, mark = batch_a.early(shapes_a, spots_a, mark)
    *outs_a, mark = batch_a.late(shapes_a, spots_a, mark, outs_a)
    *outs_b, mark = batch_b.early(shapes_b, spots_b, mark)
    *outs_c, mark = batch_c.early(shapes_c, spots_c, mark)
    mark = batch_c.arrive(batch_b.arrive(mark))
    *outs_b, mark = batch_b.late(shapes_b, spots_b, mark, outs_b)
    *outs_c, mark = batch_c.late(shapes_c, spots_c, mark, outs_c)
    g_out, g_query, g_key, g_value = outs_a
    g_conv = outs_b[0].reshape(conv_w.shape)
    g_res, g_cond = outs_c
    vec = rows_now[rows_now.shape[0] - EDGE :].astype(F32)
    g_convb, g_resb, g_outb = (vec[2 * i : 2 * i + 2].reshape(wide) for i in range(3))
    sizes = jnp.sum(vec[6:9], axis=1)
    frames_valid = sum(vec[9, i] * (1 << 3 * i) for i in range(8))
    levels = jnp.sqrt(sizes / (frames_valid * width))
    return (
        block_out,
        skip_out,
        in_grad,
        g_step,
        g_conv,
        g_cond,
        g_convb,
        g_res,
        g_resb,
        g_query,
        g_key,
        g_value,
        g_out,
        g_outb,
        levels,
    )


def solution(mesh):
    rows = P("dp", None)
    split = P("dp", "section")
    return jax.shard_map(
        on_device,
        mesh=mesh,
        in_specs=(rows, rows, P("dp", None, None, None), P("dp"), rows, rows, rows, rows)
        + (P(),) * 11,
        out_specs=(split,) * 3 + (P(),) * 12,
        check_vma=False,
    )
```

```python
import functools
import math

import jax
import jax.numpy as jnp
from jax import lax
from jax.experimental import pallas as pl
from jax.experimental.pallas import tpu as pltpu
from jax.sharding import PartitionSpec as P

HEADS = 8
SHIFT = 2
EDGE = 16
ISQ2 = 0.7071067811865476
F32 = jnp.float32
BF16 = jnp.bfloat16
VMEM = 56 * 1024 * 1024
KB_VMEM = 48 * 1024 * 1024
KC_VMEM = 48 * 1024 * 1024


def nn(a, b):
    return lax.dot_general(a, b, (((1,), (0,)), ((), ())), preferred_element_type=F32)


def nt(a, b):
    return lax.dot_general(a, b, (((1,), (1,)), ((), ())), preferred_element_type=F32)


def tn(a, b):
    return lax.dot_general(a, b, (((0,), (0,)), ((), ())), preferred_element_type=F32)


def rows_iota(rows, cols):
    return lax.broadcasted_iota(jnp.int32, (rows, cols), 0)


def col_sums(x):
    rows, cols = x.shape
    return jnp.sum(x.reshape(rows // 8, 8, cols), axis=0)


def plan(g, tile, slots, buckets, item_len):
    mb = g // slots
    q = g - mb * slots
    span = slots >> buckets[mb]
    slot = q // span
    off = q - slot * span
    lim = item_len[mb, slot] - off * tile
    return mb, slot, lim, off > 0, off < span - 1


def forward_kernel(
    cfg,
    sec_ref,
    buckets,
    item_len,
    steps,
    prev_ref,
    rows_ref,
    next_ref,
    cond_ref,
    gout_ref,
    gskip_ref,
    prompt_ref,
    step_w,
    conv_w,
    cond_w,
    conv_b,
    res_w,
    res_b,
    query_w,
    key_w,
    value_w,
    out_w,
    out_b,
    o_stack,
    o_dpre,
    o_edge,
    o_dsent,
    o_block_keep,
    o_block_give,
    o_skip_keep,
    o_skip_give,
    o_keep,
    o_give,
    o_keep_c,
    o_give_c,
    o_vec,
    proj,
    keys,
    values,
    d_keys,
    d_values,
    g_out,
    g_query,
    sums,
    stats,
    count,
    out_t,
    query_t,
    res_t,
    g_res,
    g_cond,
    own_head,
):
    tile, slots, nq, subs, tiles, mb_own, micro = cfg
    t = pl.program_id(0)
    section = sec_ref[0]
    size = subs * tile
    width = rows_ref.shape[1]
    half = width // 2
    head = width // HEADS
    mb0 = section * (micro - mb_own)
    items = mb_own * slots
    keep_left = section == 0

    @pl.when(t == 0)
    def _():
        row = rows_iota(items, half)
        when = jnp.zeros((items, half), F32)
        for i in range(items):
            s = steps[mb0 + i // slots, i % slots].astype(F32)
            when = jnp.where(row == i, s, when)
        lane = lax.broadcasted_iota(jnp.int32, (items, half), 1).astype(F32)
        angle = when * jnp.exp(lane * F32(-math.log(10000.0) / half))
        emb = jnp.concatenate([jnp.sin(angle), jnp.cos(angle)], axis=1)
        proj[...] = nn(emb.astype(BF16), step_w[...])
        here = prompt_ref[pl.ds(pl.multiple_of(mb0 * slots * nq, 16), items * nq), :]
        factor = head ** (-0.5)
        keys[...] = (nn(here, key_w[...]).astype(BF16) * BF16(factor)).astype(BF16)
        values[...] = nn(here, value_w[...]).astype(BF16)
        d_keys[...] = jnp.zeros_like(d_keys)
        d_values[...] = jnp.zeros_like(d_values)
        g_out[...] = jnp.zeros_like(g_out)
        out_t[...] = out_w[...].T
        query_t[...] = query_w[...].T
        res_t[...] = res_w[...].T
        g_res[...] = jnp.zeros_like(g_res)
        g_cond[...] = jnp.zeros_like(g_cond)
        at_row = rows_iota(HEADS * nq, width) // nq
        at_lane = lax.broadcasted_iota(jnp.int32, (HEADS * nq, width), 1) // head
        own_head[...] = jnp.where(at_row == at_lane, 1.0, 0.0).astype(BF16)
        g_query[...] = jnp.zeros_like(g_query)
        sums[...] = jnp.zeros_like(sums)
        stats[...] = jnp.zeros_like(stats)
        count[0] = 0

    ext = jnp.concatenate([prev_ref[...], rows_ref[...], next_ref[...]], axis=0)
    spread = tile + 2 * EDGE
    place = rows_iota(spread, 128)

    def lanes(mask):
        return jnp.concatenate([mask] * (width // 128), axis=1)

    mixed, behind, ahead, at = [], [], [], []
    valid = []
    row = rows_iota(tile, 128)
    for k in range(subs):
        mb, slot, lim, prev_in, next_in = plan(
            section * tiles + t * subs + k, tile, slots, buckets, item_len
        )
        item = (mb - mb0) * slots + slot
        at.append(pl.multiple_of(item * nq, nq))
        lo = jnp.where(prev_in, 0, EDGE)
        hi = jnp.where(next_in, tile + 2 * EDGE, tile + EDGE)
        hi = jnp.minimum(hi, lim + EDGE)
        part = ext[k * tile : k * tile + spread].astype(F32) + proj[pl.ds(item, 1), :]
        part = part * lanes(jnp.where((place >= lo) & (place < hi), 1.0, 0.0))
        mixed.append(part[EDGE : EDGE + tile])
        behind.append(pltpu.roll(part, SHIFT, 0)[EDGE : EDGE + tile].astype(BF16))
        ahead.append(pltpu.roll(part, spread - SHIFT, 0)[EDGE : EDGE + tile].astype(BF16))
        valid.append(jnp.where(row < lim, 1.0, 0.0))
        count[0] += jnp.clip(lim, 0, tile)
    mixed = jnp.concatenate(mixed, axis=0)
    valid = lanes(jnp.concatenate(valid, axis=0))
    stacked = jnp.concatenate(
        [jnp.concatenate(behind, axis=0), mixed.astype(BF16), jnp.concatenate(ahead, axis=0)],
        axis=1,
    )
    o_stack[...] = stacked
    pre = nn(stacked, conv_w[...]) + nn(cond_ref[...], cond_w[...]) + conv_b[...]
    a = jnp.tanh(pre[:, :width])
    s = 0.5 * jnp.tanh(0.5 * pre[:, width:]) + 0.5
    both = a * s
    gate = both.astype(BF16)
    slope_a = s - both * a
    slope_s = both - both * s
    branch = nn(gate, res_w[...]) + res_b[...]
    res_part = branch[:, :width] * valid
    skip = (branch[:, width:] * valid).astype(BF16)
    o_skip_keep[...] = jnp.where(keep_left, skip[:, :half], skip[:, half:])
    o_skip_give[...] = jnp.where(keep_left, skip[:, half:], skip[:, :half])
    hidden = (mixed + res_part) * ISQ2
    sent = hidden.astype(BF16)
    sent_f = sent.astype(F32)
    stats[0] += col_sums(hidden * hidden)
    stats[1] += col_sums(res_part * res_part)

    query = nn(sent, query_w[...]).astype(BF16)
    mask = own_head[...]
    probs, probs_low, key_bd, value_bd, attended = [], [], [], [], []
    for k in range(subs):
        key_bd.append(jnp.concatenate([keys[pl.ds(at[k], nq), :]] * HEADS, axis=0) * mask)
        value_bd.append(jnp.concatenate([values[pl.ds(at[k], nq), :]] * HEADS, axis=0) * mask)
        scores = nt(key_bd[k], query[k * tile : (k + 1) * tile]).reshape(HEADS, nq, tile)
        expo = jnp.exp(scores - jnp.max(scores, axis=1, keepdims=True))
        probs.append(expo * (1.0 / jnp.sum(expo, axis=1, keepdims=True)))
        probs_low.append(probs[k].astype(BF16).reshape(HEADS * nq, tile))
        attended.append(tn(probs_low[k], value_bd[k]).astype(BF16))
    attended = jnp.concatenate(attended, axis=0)
    film = nn(attended, out_w[...]) + out_b[...]
    scale = film[:, :width]
    change = (sent_f * scale + film[:, width:]) * valid
    block = (sent_f + change).astype(BF16)
    o_block_keep[...] = jnp.where(keep_left, block[:, :half], block[:, half:])
    o_block_give[...] = jnp.where(keep_left, block[:, half:], block[:, :half])
    stats[2] += col_sums(change * change)

    gy = gout_ref[...].astype(F32) * valid
    d_film = jnp.concatenate([(gy * sent_f).astype(BF16), gy.astype(BF16)], axis=1)
    sums[2] += col_sums(d_film.astype(F32))
    g_out[...] += tn(attended, d_film)
    d_att = nn(d_film, out_t[...]).astype(BF16)
    low_lane = lax.broadcasted_iota(jnp.int32, (nq, 2 * head), 1) < head

    def own_heads(x):
        pieces = []
        for p in range(HEADS // 2):
            at_row, at_lane = 2 * p * nq, 2 * p * head
            first = x[at_row : at_row + nq, at_lane : at_lane + 2 * head]
            second = x[at_row + nq : at_row + 2 * nq, at_lane : at_lane + 2 * head]
            pieces.append(jnp.where(low_lane, first, second))
        return jnp.concatenate(pieces, axis=1)

    d_query = []
    for k in range(subs):
        here = slice(k * tile, (k + 1) * tile)
        d_probs = nt(value_bd[k], d_att[here]).reshape(HEADS, nq, tile)
        weighted = probs[k] * d_probs
        inner = jnp.sum(weighted, axis=1, keepdims=True)
        d_scores = (weighted - probs[k] * inner).astype(BF16).reshape(HEADS * nq, tile)
        d_values[pl.ds(at[k], nq), :] += own_heads(nn(probs_low[k], d_att[here]))
        d_keys[pl.ds(at[k], nq), :] += own_heads(nn(d_scores, query[here]))
        d_query.append(tn(d_scores, key_bd[k]).astype(BF16))
    d_query = jnp.concatenate(d_query, axis=0)
    g_query[...] += tn(sent, d_query)
    d_sent = (gy * (1.0 + scale) + nn(d_query, query_t[...])).astype(BF16)
    o_dsent[...] = d_sent

    d_res = (d_sent.astype(F32) * ISQ2).astype(BF16)
    gs = (gskip_ref[...].astype(F32) * valid).astype(BF16)
    d_branch = jnp.concatenate([d_res, gs], axis=1)
    sums[1] += col_sums(d_branch.astype(F32))
    g_res[...] += tn(gate, d_branch)
    d_gate = nn(d_branch, res_t[...])
    d_pre = jnp.concatenate(
        [(d_gate * slope_a).astype(BF16), (d_gate * slope_s).astype(BF16)], axis=1
    )
    sums[0] += col_sums(d_pre.astype(F32))
    o_dpre[...] = d_pre
    g_cond[...] += tn(cond_ref[...], d_pre)

    @pl.when(t == 0)
    def _():
        o_edge[:EDGE, :] = d_pre[:EDGE, :]

    @pl.when(t == tiles // subs - 1)
    def _():
        here = prompt_ref[pl.ds(pl.multiple_of(mb0 * slots * nq, 16), items * nq), :]
        factor = head ** (-0.5)
        mine = pl.multiple_of(section * half, half)
        theirs = pl.multiple_of(half - section * half, half)

        o_edge[EDGE:, :] = d_pre[size - EDGE :, :]

        def put(i, ref, left, keep=o_keep, give=o_give):
            keep[i] = ref[pl.ds(mine, half), pl.ds(left, width)].astype(BF16)
            give[i] = ref[pl.ds(theirs, half), pl.ds(left, width)].astype(BF16)

        put(0, g_out, 0)
        put(1, g_out, width)
        put(2, g_query, 0)
        g_query[...] = tn(here, (d_keys[...] * factor).astype(BF16))
        put(3, g_query, 0)
        g_query[...] = tn(here, d_values[...].astype(BF16))
        put(4, g_query, 0)
        put(0, g_res, 0, o_keep_c, o_give_c)
        put(1, g_res, width, o_keep_c, o_give_c)
        put(2, g_cond, 0, o_keep_c, o_give_c)
        put(3, g_cond, width, o_keep_c, o_give_c)
        for i in range(3):
            line = jnp.sum(sums[i], axis=0, keepdims=True)
            o_vec[2 * i : 2 * i + 1, :] = line[:, :width]
            o_vec[2 * i + 1 : 2 * i + 2, :] = line[:, width:]
        for i in range(3):
            o_vec[6 + i : 7 + i, :] = jnp.sum(stats[i], axis=0, keepdims=True)
        lane = lax.broadcasted_iota(jnp.int32, (16 - 9, width), 1)
        digits = (count[0] >> (3 * jnp.minimum(lane, 8))) & 7
        o_vec[9:16, :] = jnp.where(lane < 8, digits, 0).astype(F32)


def weight_kernel(sec_ref, left_ref, dpre_ref, *refs):
    o_keep, o_give, acc = refs[-3:]
    section = sec_ref[0]
    width = acc.shape[0]
    half = width // 2
    acc[...] = tn(left_ref[...], dpre_ref[...])
    mine = pl.multiple_of(section * half, half)
    theirs = pl.multiple_of(half - section * half, half)
    for side in range(2):
        o_keep[side] = acc[pl.ds(mine, half), pl.ds(side * width, width)].astype(BF16)
        o_give[side] = acc[pl.ds(theirs, half), pl.ds(side * width, width)].astype(BF16)


def back_kernel(
    cfg,
    sec_ref,
    buckets,
    item_len,
    prev_ref,
    dpre_ref,
    next_ref,
    other_ref,
    dsent_ref,
    conv_w,
    steps,
    vec_ref,
    after_ref,
    o_keep,
    o_give,
    o_rows,
    d_step,
):
    tile, slots, subs, tiles, micro = cfg
    t = pl.program_id(0)
    section = sec_ref[0]
    width = dsent_ref.shape[1]
    half = width // 2
    count = tiles // subs

    @pl.when(t == 0)
    def _():
        d_step[...] = jnp.zeros_like(d_step)

    before = jnp.where(t == 0, other_ref[EDGE:, :], prev_ref[...])
    after = jnp.where(t == count - 1, other_ref[:EDGE, :], next_ref[...])
    ext = jnp.concatenate([before, dpre_ref[...], after], axis=0)
    spread = tile + 2 * EDGE
    place = rows_iota(spread, 128)
    row = rows_iota(tile, 128)
    ahead, behind, valid, item = [], [], [], []
    for k in range(subs):
        mb, slot, lim, prev_in, next_in = plan(
            section * tiles + t * subs + k, tile, slots, buckets, item_len
        )
        item.append(mb * slots + slot)
        lo = jnp.where(prev_in, 0, EDGE)
        hi = jnp.where(next_in, spread, tile + EDGE)
        here = jnp.where((place >= lo) & (place < hi), 1.0, 0.0)
        part = ext[k * tile : k * tile + spread].astype(F32)
        part = part * jnp.concatenate([here] * (2 * width // 128), axis=1)
        ahead.append(pltpu.roll(part, spread - SHIFT, 0)[EDGE : EDGE + tile].astype(BF16))
        behind.append(pltpu.roll(part, SHIFT, 0)[EDGE : EDGE + tile].astype(BF16))
        valid.append(jnp.where(row < lim, 1.0, 0.0))
    valid = jnp.concatenate([jnp.concatenate(valid, axis=0)] * (width // 128), axis=1)
    d_in = nt(jnp.concatenate(ahead, axis=0), conv_w[:width, :])
    d_in += nt(dpre_ref[...], conv_w[width : 2 * width, :])
    d_in += nt(jnp.concatenate(behind, axis=0), conv_w[2 * width :, :])
    d_mixed = (dsent_ref[...].astype(F32) * ISQ2 + d_in) * valid
    for k in range(subs):
        line = jnp.sum(col_sums(d_mixed[k * tile : (k + 1) * tile]), axis=0, keepdims=True)
        d_step[pl.ds(item[k], 1), :] += line
    low = d_mixed.astype(BF16)
    o_keep[...] = jnp.where(section == 0, low[:, :half], low[:, half:])
    o_give[...] = jnp.where(section == 0, low[:, half:], low[:, :half])

    @pl.when(t == count - 1)
    def _():
        items = micro * slots
        group = d_step.shape[0]
        lane = lax.broadcasted_iota(jnp.int32, (1, width), 1)
        index = jnp.zeros((1, width), jnp.int32)
        for i in range(items):
            index = jnp.where(lane == i, steps[i // slots, i % slots], index)
        index = jnp.where(section == 0, index, 0)
        d_step[items : items + 1, :] = (index >> 5).astype(F32)
        d_step[items + 1 : items + 2, :] = (index & 31).astype(F32)
        o_rows[:group, :] = d_step[...].astype(BF16)
        o_rows[group:, :] = vec_ref[...].astype(BF16)


SMALL = pl.CostEstimate(flops=1024, bytes_accessed=1024, transcendentals=0)
LARGE = pl.CostEstimate(flops=1 << 36, bytes_accessed=1024, transcendentals=0)
ANYWHERE = pl.BlockSpec(memory_space=pl.ANY)
PARAMS = pltpu.CompilerParams(vmem_limit_bytes=VMEM)


IN_VMEM = pl.BlockSpec(memory_space=pltpu.VMEM)
IN_SMEM = pl.BlockSpec(memory_space=pltpu.SMEM)
IN_HBM = pl.BlockSpec(memory_space=pltpu.HBM)


def struct(rows, width, dtype=BF16):
    return jax.ShapeDtypeStruct((rows, width), dtype)


def total(a, b):
    return (a.astype(F32) + b.astype(F32)).astype(BF16)


def at_bit(bit, rows):
    return pl.ds(pl.multiple_of(bit * rows, 16), rows)


def split_body(bit, held, got, keep, give):
    rows = keep.shape[0]
    keep[...] = total(held[at_bit(bit, rows), :], got[at_bit(bit, rows), :])
    give[...] = total(held[at_bit(1 - bit, rows), :], got[at_bit(1 - bit, rows), :])


def add_body(bit, held, got, out):
    out[...] = total(held[...], got[...])


def merge_body(bit, cur, got, out):
    rows = cur.shape[0]
    out[at_bit(bit, rows), :] = cur[...]
    out[at_bit(1 - bit, rows), :] = got[...]


def gather_body(bit, cur, got, out):
    rows = cur.shape[0] - EDGE
    out[at_bit(bit, rows), :] = cur[:rows, :]
    out[at_bit(1 - bit, rows), :] = got[:rows, :]
    out[2 * rows :, :] = total(cur[rows:, :], got[rows:, :])


def pair_kernel(bodies, outs, *refs):
    n = len(bodies)
    bits, arrays, results = refs[:n], refs[n : 3 * n], refs[3 * n + 1 :]
    for i, body in enumerate(bodies):
        count = outs[i]
        body(bits[i][0], arrays[2 * i], arrays[2 * i + 1], *results[:count])
        results = results[count:]


def pair_call(works, after, cost):
    outs = [len(w[4]) for w in works]
    shapes = [x for w in works for x in w[4]]
    return pl.pallas_call(
        functools.partial(pair_kernel, [w[0] for w in works], outs),
        in_specs=[IN_SMEM] * len(works) + [IN_VMEM] * (2 * len(works)) + [ANYWHERE],
        out_specs=[IN_VMEM] * len(shapes),
        out_shape=shapes,
        compiler_params=pltpu.CompilerParams(vmem_limit_bytes=24 * 1024 * 1024),
        cost_estimate=cost,
        name=works[0][0].__name__,
    )(*[w[1] for w in works], *[x for w in works for x in w[2:4]], after)


def then_kernel(x_ref, after_ref, out_ref):
    out_ref[...] = x_ref[...]


def then(x, after):
    return pl.pallas_call(
        then_kernel,
        in_specs=[IN_VMEM, ANYWHERE],
        out_specs=IN_VMEM,
        out_shape=jax.ShapeDtypeStruct(x.shape, x.dtype),
        compiler_params=pltpu.CompilerParams(vmem_limit_bytes=16 * 1024 * 1024),
        cost_estimate=SMALL,
        name="then",
    )(x, after)


def join_kernel(count, sec_ref, *refs):
    section = sec_ref[0]
    arrays, outs = refs[: 2 * count], refs[2 * count + 1 : 3 * count + 1]
    mark, sems = refs[-2:]
    mark[...] = jnp.zeros_like(mark)
    copies = []
    for i in range(count):
        rows = arrays[2 * i].shape[0]
        for j, place in enumerate((section, 1 - section)):
            copies.append(
                pltpu.make_async_copy(
                    arrays[2 * i + j], outs[i].at[at_bit(place, rows), :], sems.at[2 * i + j]
                )
            )
    for copy in copies:
        copy.start()
    for copy in copies:
        copy.wait()


def join(sec, after, *pairs):
    rows, width = pairs[0][0].shape
    count = len(pairs)
    return pl.pallas_call(
        functools.partial(join_kernel, count),
        in_specs=[IN_SMEM] + [IN_VMEM] * (2 * count) + [ANYWHERE],
        out_specs=[IN_HBM] * count + [IN_VMEM],
        out_shape=[struct(2 * rows, width)] * count + [struct(8, 128, F32)],
        scratch_shapes=[pltpu.SemaphoreType.DMA((2 * count,))],
        compiler_params=pltpu.CompilerParams(vmem_limit_bytes=16 * 1024 * 1024),
        cost_estimate=SMALL,
        name="join",
    )(sec, *[x for pair in pairs for x in pair], after)


def swap(x):
    return lax.ppermute(x, "section", [(0, 1), (1, 0)])


class Sum:
    def __init__(self, orders):
        self.chips = lax.axis_size("dp")
        self.section = lax.axis_index("section")
        self.chip = lax.axis_index("dp")
        self.orders = orders
        self.levels = len(orders[0])

    def bit_of(self, step, section):
        where = jnp.where(section == 0, self.orders[0][step], self.orders[1][step])
        return ((self.chip >> where) & 1).astype(jnp.int32)

    def bit(self, step):
        return self.bit_of(step, self.section).reshape(1)

    def send(self, x, step):
        chips = self.chips
        route = [
            (s * chips + d, s * chips + (d ^ (1 << self.orders[s][step])))
            for s in range(2)
            for d in range(chips)
        ]
        return lax.ppermute(x, ("section", "dp"), route)

    def runs(self):
        mine, theirs = self.section, 1 - self.section
        own, other = self.bit_of(0, mine), self.bit_of(0, theirs)
        return jnp.stack(
            [2 * mine + own, 2 * mine + 1 - own, 2 * theirs + other, 2 * theirs + 1 - other]
        ).astype(jnp.int32)


class Batch:
    def __init__(self, sums, keep, give):
        self.sums = sums
        self.held = keep
        self.got = swap(give)
        self.step = 0

    def turn(self, after, more=(), cost=LARGE):
        sums = self.sums
        halved = sums.levels - 2
        at = self.step
        self.step += 1
        rows, width = self.held.shape
        if at < halved:
            work = (split_body, sums.bit(at), self.held, self.got, [struct(rows // 2, width)] * 2)
            self.held, give, *rest = pair_call([work, *more], after, cost)
            self.got = sums.send(give, at)
        elif at <= halved + 2:
            work = (add_body, sums.bit(0), self.held, self.got, [struct(rows, width)])
            self.held, *rest = pair_call([work, *more], after, cost)
            self.got = sums.send(self.held, at if at < halved + 2 else halved - 1)
        else:
            back = 2 * halved + 2 - at
            work = (merge_body, sums.bit(back), self.held, self.got, [struct(2 * rows, width)])
            self.held, *rest = pair_call([work, *more], after, cost)
            self.got = sums.send(self.held, back - 1)
        return (self.held, *rest)

    @property
    def turns(self):
        return 2 * self.sums.levels - 2

    def early(self, shapes, spots, after, outs=()):
        return place(self.sums.runs(), (0, 2), (self.held, swap(self.held)), shapes, spots, after, outs)

    def arrive(self, after):
        self.got = then(self.got, after)
        self.last = swap(self.got)
        return self.got

    def late(self, shapes, spots, after, outs):
        return place(self.sums.runs(), (1, 3), (self.got, self.last), shapes, spots, after, outs)


def place_kernel(which, spots, count, runs, p0, p1, after_ref, *refs):
    outs, (mark, buf, sems) = refs[-3 - count : -3], refs[-3:]
    mark[...] = jnp.zeros_like(mark)
    rows = buf.shape[1]
    per_run = p0.shape[0] // rows
    for wait in (False, True):
        for run in range(4):
            mine, theirs = runs[which[0]] == run, runs[which[1]] == run
            base = run * per_run

            @pl.when(mine | theirs)
            def _(run=run, mine=mine):
                slot = jnp.where(mine, 0, 1)
                for w in range(run * per_run, (run + 1) * per_run):
                    spot = spots[w]
                    if spot is None:
                        continue
                    j = w - base
                    k, row, col = spot
                    copy = pltpu.make_async_copy(
                        buf.at[slot * per_run + j],
                        outs[k].at[pl.ds(row, rows), pl.ds(col, buf.shape[2])],
                        sems.at[slot * per_run + j],
                    )
                    if wait:
                        copy.wait()
                    else:
                        part = slice(j * rows, (j + 1) * rows)
                        value = jnp.where(mine, p0[part, :], p1[part, :])
                        buf[slot * per_run + j] = value.astype(F32)
                        copy.start()


def spots_of(targets, width):
    quarter = width // 4
    spots = []
    for section in range(2):
        for k, row, col in targets:
            for u in range(2):
                spots.append((k, row + (2 * section + u) * quarter, col))
    return spots


def place(runs, which, pieces, shapes, spots, after, outs=()):
    length, width = pieces[0].shape
    quarter = width // 4
    per_run = length // quarter
    half = len(spots) // 2
    full = [None] * (4 * per_run)
    full[:half] = spots[:half]
    full[2 * per_run : 2 * per_run + half] = spots[half:]
    return pl.pallas_call(
        functools.partial(place_kernel, which, full, len(shapes)),
        in_specs=[IN_SMEM] + [IN_VMEM] * 2 + [ANYWHERE] + [IN_HBM] * len(outs),
        out_specs=[IN_HBM] * len(shapes) + [IN_VMEM],
        out_shape=list(shapes) + [struct(8, 128, F32)],
        input_output_aliases={4 + k: k for k in range(len(outs))},
        scratch_shapes=[
            pltpu.VMEM((2 * per_run, quarter, width), F32),
            pltpu.SemaphoreType.DMA((2 * per_run,)),
        ],
        compiler_params=pltpu.CompilerParams(vmem_limit_bytes=24 * 1024 * 1024),
        cost_estimate=SMALL,
        name="place",
    )(runs, *pieces, after, *outs)


def step_kernel(items, group, rows_ref, after_ref, out_ref, o_low, o_res, o_out, o_levels, mark):
    mark[...] = jnp.zeros_like(mark)
    width = rows_ref.shape[1]
    half = width // 2
    rows = rows_ref[: rows_ref.shape[0] - EDGE, :].astype(F32).reshape(-1, group, width)
    lanes = (rows.shape[0], group, 128)
    index = 32.0 * rows[:, items : items + 1, :128] + rows[:, items + 1 : items + 2, :128]
    diagonal = lax.broadcasted_iota(jnp.int32, lanes, 1) == lax.broadcasted_iota(
        jnp.int32, lanes, 2
    )
    index = jnp.sum(jnp.where(diagonal, index, 0.0), axis=2, keepdims=True)
    index = index.reshape(-1, 1)
    lane = lax.broadcasted_iota(jnp.int32, (index.shape[0], half), 1).astype(F32)
    angle = index * jnp.exp(lane * F32(-math.log(10000.0) / half))
    emb = jnp.concatenate([jnp.sin(angle), jnp.cos(angle)], axis=1)
    used = lax.broadcasted_iota(jnp.int32, rows.shape, 1) < items
    sums = jnp.where(used, rows, 0.0).reshape(-1, width)
    out_ref[...] = tn(emb.astype(BF16), sums.astype(BF16))
    vec = rows_ref[rows_ref.shape[0] - EDGE :, :].astype(F32)
    for i, out in enumerate((o_low, o_res, o_out)):
        out[:, :width] = vec[2 * i : 2 * i + 1, :]
        out[:, width:] = vec[2 * i + 1 : 2 * i + 2, :]
    digit = lax.broadcasted_iota(jnp.int32, (1, width), 1)
    weight = jnp.where(digit < 8, 1 << (3 * jnp.minimum(digit, 8)), 0).astype(F32)
    frames = jnp.sum(vec[9:10, :] * weight, axis=1, keepdims=True) * width
    sizes = jnp.sum(vec[6:9, :], axis=1, keepdims=True)
    o_levels[...] = jnp.broadcast_to(jnp.sqrt(sizes / frames), o_levels.shape)


def padded(x, rows):
    return x if x.shape[0] == rows else jnp.pad(x, ((0, rows - x.shape[0]), (0, 0)))


def on_device(
    input_rows,
    conditioning,
    prompt,
    buckets,
    item_len,
    step_index,
    output_gradient,
    grad_skip,
    step_w,
    conv_w,
    cond_w,
    conv_b,
    res_w,
    res_b,
    query_w,
    key_w,
    value_w,
    out_w,
    out_b,
):
    section = lax.axis_index("section")
    sec = section.astype(jnp.int32).reshape(1)
    total, width = input_rows.shape
    micro, slots = item_len.shape
    nq = prompt.shape[2]
    frames = total // micro
    tile = frames // slots
    own = total // 2
    tiles = own // tile
    subs = 2
    size = subs * tile
    grid = tiles // subs
    mb_own = -(-own // frames)
    items = mb_own * slots
    half = width // 2
    taps = conv_w.shape[0]
    per = size // EDGE
    last = total // EDGE - 1
    wide = 2 * width
    conv_flat = conv_w.reshape(taps * width, wide)
    flat_prompt = prompt.reshape(-1, width)

    def whole(x):
        n = x.ndim
        return pl.BlockSpec(x.shape, lambda t, *_: (0,) * n, pipeline_mode=pl.Buffered(1))

    smem = pl.BlockSpec(memory_space=pltpu.SMEM)

    def chip_tile(cols):
        return pl.BlockSpec((size, cols), lambda t, s, *_: (s[0] * grid + t, 0))

    def own_tile(cols):
        return pl.BlockSpec((size, cols), lambda t, *_: (t, 0))

    def const(shape):
        return pl.BlockSpec(shape, lambda t, *_: (0,) * len(shape))

    prev_chip = pl.BlockSpec(
        (EDGE, width), lambda t, s, *_: (jnp.maximum((s[0] * grid + t) * per - 1, 0), 0)
    )
    next_chip = pl.BlockSpec(
        (EDGE, width), lambda t, s, *_: (jnp.minimum((s[0] * grid + t + 1) * per, last), 0)
    )
    vectors = [x.reshape(1, -1) for x in (conv_b, res_b, out_b)]
    weights = [
        step_w,
        conv_flat,
        cond_w,
        vectors[0],
        res_w,
        vectors[1],
        query_w,
        key_w,
        value_w,
        out_w,
        vectors[2],
    ]

    def shape(*dims, dtype=BF16):
        return jax.ShapeDtypeStruct(dims, dtype)

    def blocks_of(n):
        return const((n, half, width)), shape(n, half, width)

    film_spec, film_shape = blocks_of(5)
    side_spec, side_shape = blocks_of(4)
    (
        stack,
        d_pre,
        edge,
        d_sent,
        block_keep,
        block_give,
        skip_keep,
        skip_give,
        keep_a,
        give_a,
        keep_c,
        give_c,
        vec,
    ) = pl.pallas_call(
        functools.partial(forward_kernel, (tile, slots, nq, subs, tiles, mb_own, micro)),
        grid_spec=pltpu.PrefetchScalarGridSpec(
            num_scalar_prefetch=1,
            grid=(grid,),
            in_specs=[smem, smem, smem, prev_chip, chip_tile(width), next_chip]
            + [chip_tile(width)] * 3
            + [whole(flat_prompt)]
            + [whole(w) for w in weights],
            out_specs=[own_tile(taps * width), own_tile(wide), const((2 * EDGE, wide))]
            + [own_tile(width)]
            + [own_tile(half)] * 4
            + [film_spec, film_spec, side_spec, side_spec, const((16, width))],
            scratch_shapes=[
                pltpu.VMEM((items, width), F32),
                pltpu.VMEM((items * nq, width), BF16),
                pltpu.VMEM((items * nq, width), BF16),
                pltpu.VMEM((items * nq, width), F32),
                pltpu.VMEM((items * nq, width), F32),
                pltpu.VMEM((width, wide), F32),
                pltpu.VMEM((width, width), F32),
                pltpu.VMEM((3, 8, wide), F32),
                pltpu.VMEM((3, 8, width), F32),
                pltpu.SMEM((1,), jnp.int32),
                pltpu.VMEM((wide, width), BF16),
                pltpu.VMEM((width, width), BF16),
                pltpu.VMEM((wide, width), BF16),
                pltpu.VMEM((width, wide), F32),
                pltpu.VMEM((width, wide), F32),
                pltpu.VMEM((HEADS * nq, width), BF16),
            ],
        ),
        out_shape=[
            shape(own, taps * width),
            shape(own, wide),
            shape(2 * EDGE, wide),
            shape(own, width),
            shape(own, half),
            shape(own, half),
            shape(own, half),
            shape(own, half),
            film_shape,
            film_shape,
            side_shape,
            side_shape,
            shape(16, width, dtype=F32),
        ],
        compiler_params=pltpu.CompilerParams(vmem_limit_bytes=VMEM),
        cost_estimate=LARGE,
        name="forward",
    )(
        sec,
        buckets,
        item_len,
        step_index,
        input_rows,
        input_rows,
        input_rows,
        conditioning,
        output_gradient,
        grad_skip,
        flat_prompt,
        *weights,
    )

    bits = list(range(lax.axis_size("dp").bit_length() - 1))
    other = [bits[1], bits[0]] + bits[2:]
    if len(other) > 3:
        other[-2], other[-1] = other[-1], other[-2]
    sums = Sum((bits, other))
    unit = 16 * lax.axis_size("dp") // 4

    def batch(keep, give):
        rows = keep.shape[0] * half
        rows = -(-rows // unit) * unit
        return Batch(
            sums, padded(keep.reshape(-1, width), rows), padded(give.reshape(-1, width), rows)
        )

    batch_a, batch_c = batch(keep_a, give_a), batch(keep_c, give_c)
    block_got, skip_got, other_edge = swap(block_give), swap(skip_give), swap(edge)
    spec = pl.BlockSpec((2, half, width), lambda i, *_: (i, 0, 0))
    keep_b, give_b = pl.pallas_call(
        weight_kernel,
        grid_spec=pltpu.PrefetchScalarGridSpec(
            num_scalar_prefetch=1,
            grid=(taps,),
            in_specs=[pl.BlockSpec((own, width), lambda i, *_: (0, i)), whole(d_pre)],
            out_specs=[spec, spec],
            scratch_shapes=[pltpu.VMEM((width, wide), F32)],
        ),
        out_shape=[shape(2 * taps, half, width)] * 2,
        compiler_params=pltpu.CompilerParams(vmem_limit_bytes=KB_VMEM),
        cost_estimate=LARGE,
        name="weights",
    )(sec, stack, d_pre)
    batch_b = batch(keep_b, give_b)
    (after,) = batch_a.turn(keep_b)
    (after,) = batch_c.turn(after)
    (after,) = batch_b.turn(after)

    group = -(-(micro * slots + 2) // 16) * 16
    rows_last = own // EDGE - 1
    in_keep, in_give, rows_now = pl.pallas_call(
        functools.partial(back_kernel, (tile, slots, subs, tiles, micro)),
        grid_spec=pltpu.PrefetchScalarGridSpec(
            num_scalar_prefetch=1,
            grid=(grid,),
            in_specs=[
                smem,
                smem,
                pl.BlockSpec((EDGE, wide), lambda t, *_: (jnp.maximum(t * per - 1, 0), 0)),
                own_tile(wide),
                pl.BlockSpec(
                    (EDGE, wide), lambda t, *_: (jnp.minimum((t + 1) * per, rows_last), 0)
                ),
                whole(other_edge),
                own_tile(width),
                whole(conv_flat),
                smem,
                whole(vec),
                ANYWHERE,
            ],
            out_specs=[own_tile(half), own_tile(half), const((group + EDGE, width))],
            scratch_shapes=[pltpu.VMEM((group, width), F32)],
        ),
        out_shape=[shape(own, half), shape(own, half), shape(group + EDGE, width)],
        compiler_params=pltpu.CompilerParams(vmem_limit_bytes=KC_VMEM),
        cost_estimate=LARGE,
        name="back",
    )(
        sec,
        buckets,
        item_len,
        d_pre,
        d_pre,
        d_pre,
        other_edge,
        d_sent,
        conv_flat,
        step_index,
        vec,
        after,
    )
    in_got = swap(in_give)

    block_out, skip_out, after = join(
        sec, rows_now, (block_keep, block_got), (skip_keep, skip_got)
    )
    rows_got, rows_bit, gathered = swap(rows_now), sec, 0
    batches = {"a": batch_a, "b": batch_b, "c": batch_c}
    first = True
    for name in "ac-b" * (batch_a.turns - 1):
        if name == "-":
            first = False
            continue
        turner = batches[name]
        if name == "b" and gathered <= sums.levels:
            n = rows_now.shape[0]
            work = (add_body, rows_bit, rows_now, rows_got, [struct(n, width)])
            if gathered:
                work = (gather_body, rows_bit, rows_now, rows_got, [struct(2 * n - EDGE, width)])
            after, rows_now = turner.turn(after, [work])
            if gathered < sums.levels:
                route = [(d, d ^ (1 << gathered)) for d in range(sums.chips)]
                rows_got = lax.ppermute(rows_now, "dp", route)
                rows_bit = ((sums.chip >> gathered) & 1).astype(jnp.int32).reshape(1)
            gathered += 1
        else:
            (after,) = turner.turn(after, cost=SMALL if first else LARGE)

    line = struct(1, wide, F32)
    g_step, g_convb, g_resb, g_outb, levels, mark = pl.pallas_call(
        functools.partial(step_kernel, micro * slots, group),
        in_specs=[IN_VMEM, ANYWHERE],
        out_specs=[IN_VMEM] * 6,
        out_shape=[struct(width, width, F32), line, line, line]
        + [struct(3, 128, F32), struct(8, 128, F32)],
        compiler_params=pltpu.CompilerParams(vmem_limit_bytes=24 * 1024 * 1024),
        cost_estimate=LARGE,
        name="step_grad",
    )(rows_now, after)
    in_grad, mark = join(sec, mark, (in_keep, in_got))

    def pairs(k, count, base=0):
        return [(k, base + i * width, col) for i in range(count) for col in (0, width)]

    square, tall = struct(width, width, F32), struct(width, wide, F32)
    shapes_a = [tall, square, square, square]
    spots_a = spots_of(pairs(0, 1) + [(k, 0, 0) for k in (1, 2, 3)], width)
    shapes_b, spots_b = [struct(taps * width, wide, F32)], spots_of(pairs(0, taps), width)
    shapes_c, spots_c = [tall, tall], spots_of(pairs(0, 1) + pairs(1, 1), width)
    *outs_a, mark = batch_a.early(shapes_a, spots_a, mark)
    *outs_c, mark = batch_c.early(shapes_c, spots_c, mark)
    *outs_b, mark = batch_b.early(shapes_b, spots_b, mark)
    mark = batch_b.arrive(batch_c.arrive(batch_a.arrive(mark)))
    *outs_a, mark = batch_a.late(shapes_a, spots_a, mark, outs_a)
    *outs_c, mark = batch_c.late(shapes_c, spots_c, mark, outs_c)
    *outs_b, mark = batch_b.late(shapes_b, spots_b, mark, outs_b)
    g_out, g_query, g_key, g_value = outs_a
    g_conv = outs_b[0].reshape(conv_w.shape)
    g_res, g_cond = outs_c
    g_convb, g_resb, g_outb = (x.reshape(wide) for x in (g_convb, g_resb, g_outb))
    levels = levels[:, 0]
    return (
        block_out,
        skip_out,
        in_grad,
        g_step,
        g_conv,
        g_cond,
        g_convb,
        g_res,
        g_resb,
        g_query,
        g_key,
        g_value,
        g_out,
        g_outb,
        levels,
    )


def solution(mesh):
    rows = P("dp", None)
    split = P("dp", "section")
    return jax.shard_map(
        on_device,
        mesh=mesh,
        in_specs=(rows, rows, P("dp", None, None, None), P("dp"), rows, rows, rows, rows)
        + (P(),) * 11,
        out_specs=(split,) * 3 + (P(),) * 12,
        check_vma=False,
    )
```

```python
import functools
import math

import jax
import jax.numpy as jnp
from jax import lax
from jax.experimental import pallas as pl
from jax.experimental.pallas import tpu as pltpu
from jax.sharding import PartitionSpec as P

HEADS = 8
SHIFT = 2
EDGE = 16
ISQ2 = 0.7071067811865476
F32 = jnp.float32
BF16 = jnp.bfloat16
VMEM = 56 * 1024 * 1024
KB_VMEM = 56 * 1024 * 1024
KC_VMEM = 32 * 1024 * 1024


def nn(a, b):
    return lax.dot_general(a, b, (((1,), (0,)), ((), ())), preferred_element_type=F32)


def nt(a, b):
    return lax.dot_general(a, b, (((1,), (1,)), ((), ())), preferred_element_type=F32)


def tn(a, b):
    return lax.dot_general(a, b, (((0,), (0,)), ((), ())), preferred_element_type=F32)


def rows_iota(rows, cols):
    return lax.broadcasted_iota(jnp.int32, (rows, cols), 0)


def col_sums(x):
    rows, cols = x.shape
    return jnp.sum(x.reshape(rows // 8, 8, cols), axis=0)


def plan(g, tile, slots, buckets, item_len):
    mb = g // slots
    q = g - mb * slots
    span = slots >> buckets[mb]
    slot = q // span
    off = q - slot * span
    lim = item_len[mb, slot] - off * tile
    return mb, slot, lim, off > 0, off < span - 1


def forward_kernel(
    cfg,
    sec_ref,
    buckets,
    item_len,
    steps,
    prev_ref,
    rows_ref,
    next_ref,
    cond_ref,
    gout_ref,
    gskip_ref,
    prompt_ref,
    step_w,
    conv_w,
    cond_w,
    conv_b,
    res_w,
    res_b,
    query_w,
    key_w,
    value_w,
    out_w,
    out_b,
    o_stack,
    o_dpre,
    o_edge,
    o_dsent,
    o_block_keep,
    o_block_give,
    o_skip_keep,
    o_skip_give,
    o_keep,
    o_give,
    o_keep_c,
    o_give_c,
    o_vec,
    proj,
    keys,
    values,
    d_keys,
    d_values,
    g_out,
    g_query,
    sums,
    stats,
    count,
    out_t,
    query_t,
    res_t,
    g_res,
    g_cond,
    own_head,
):
    tile, slots, nq, subs, tiles, mb_own, micro = cfg
    t = pl.program_id(0)
    section = sec_ref[0]
    size = subs * tile
    width = rows_ref.shape[1]
    half = width // 2
    head = width // HEADS
    mb0 = section * (micro - mb_own)
    items = mb_own * slots
    keep_left = section == 0

    @pl.when(t == 0)
    def _():
        row = rows_iota(items, half)
        when = jnp.zeros((items, half), F32)
        for i in range(items):
            s = steps[mb0 + i // slots, i % slots].astype(F32)
            when = jnp.where(row == i, s, when)
        lane = lax.broadcasted_iota(jnp.int32, (items, half), 1).astype(F32)
        angle = when * jnp.exp(lane * F32(-math.log(10000.0) / half))
        emb = jnp.concatenate([jnp.sin(angle), jnp.cos(angle)], axis=1)
        proj[...] = nn(emb.astype(BF16), step_w[...])
        here = prompt_ref[pl.ds(pl.multiple_of(mb0 * slots * nq, 16), items * nq), :]
        factor = head ** (-0.5)
        keys[...] = (nn(here, key_w[...]).astype(BF16) * BF16(factor)).astype(BF16)
        values[...] = nn(here, value_w[...]).astype(BF16)
        d_keys[...] = jnp.zeros_like(d_keys)
        d_values[...] = jnp.zeros_like(d_values)
        g_out[...] = jnp.zeros_like(g_out)
        out_t[...] = out_w[...].T
        query_t[...] = query_w[...].T
        res_t[...] = res_w[...].T
        g_res[...] = jnp.zeros_like(g_res)
        g_cond[...] = jnp.zeros_like(g_cond)
        at_row = rows_iota(HEADS * nq, width) // nq
        at_lane = lax.broadcasted_iota(jnp.int32, (HEADS * nq, width), 1) // head
        own_head[...] = jnp.where(at_row == at_lane, 1.0, 0.0).astype(BF16)
        g_query[...] = jnp.zeros_like(g_query)
        sums[...] = jnp.zeros_like(sums)
        stats[...] = jnp.zeros_like(stats)
        count[0] = 0

    ext = jnp.concatenate([prev_ref[...], rows_ref[...], next_ref[...]], axis=0)
    spread = tile + 2 * EDGE
    place = rows_iota(spread, 128)

    def lanes(mask):
        return jnp.concatenate([mask] * (width // 128), axis=1)

    mixed, behind, ahead, at = [], [], [], []
    valid = []
    row = rows_iota(tile, 128)
    for k in range(subs):
        mb, slot, lim, prev_in, next_in = plan(
            section * tiles + t * subs + k, tile, slots, buckets, item_len
        )
        item = (mb - mb0) * slots + slot
        at.append(pl.multiple_of(item * nq, nq))
        lo = jnp.where(prev_in, 0, EDGE)
        hi = jnp.where(next_in, tile + 2 * EDGE, tile + EDGE)
        hi = jnp.minimum(hi, lim + EDGE)
        part = ext[k * tile : k * tile + spread].astype(F32) + proj[pl.ds(item, 1), :]
        part = part * lanes(jnp.where((place >= lo) & (place < hi), 1.0, 0.0))
        mixed.append(part[EDGE : EDGE + tile])
        behind.append(pltpu.roll(part, SHIFT, 0)[EDGE : EDGE + tile].astype(BF16))
        ahead.append(pltpu.roll(part, spread - SHIFT, 0)[EDGE : EDGE + tile].astype(BF16))
        valid.append(jnp.where(row < lim, 1.0, 0.0))
        count[0] += jnp.clip(lim, 0, tile)
    mixed = jnp.concatenate(mixed, axis=0)
    valid = lanes(jnp.concatenate(valid, axis=0))
    stacked = jnp.concatenate(
        [jnp.concatenate(behind, axis=0), mixed.astype(BF16), jnp.concatenate(ahead, axis=0)],
        axis=1,
    )
    o_stack[...] = stacked
    pre = nn(stacked, conv_w[...]) + nn(cond_ref[...], cond_w[...]) + conv_b[...]
    a = jnp.tanh(pre[:, :width])
    s = 0.5 * jnp.tanh(0.5 * pre[:, width:]) + 0.5
    both = a * s
    gate = both.astype(BF16)
    slope_a = s - both * a
    slope_s = both - both * s
    branch = nn(gate, res_w[...]) + res_b[...]
    res_part = branch[:, :width] * valid
    skip = (branch[:, width:] * valid).astype(BF16)
    o_skip_keep[...] = jnp.where(keep_left, skip[:, :half], skip[:, half:])
    o_skip_give[...] = jnp.where(keep_left, skip[:, half:], skip[:, :half])
    hidden = (mixed + res_part) * ISQ2
    sent = hidden.astype(BF16)
    sent_f = sent.astype(F32)
    stats[0] += col_sums(hidden * hidden)
    stats[1] += col_sums(res_part * res_part)

    query = nn(sent, query_w[...]).astype(BF16)
    mask = own_head[...]
    probs, probs_low, key_bd, value_bd, attended = [], [], [], [], []
    for k in range(subs):
        key_bd.append(jnp.concatenate([keys[pl.ds(at[k], nq), :]] * HEADS, axis=0) * mask)
        value_bd.append(jnp.concatenate([values[pl.ds(at[k], nq), :]] * HEADS, axis=0) * mask)
        scores = nt(key_bd[k], query[k * tile : (k + 1) * tile]).reshape(HEADS, nq, tile)
        expo = jnp.exp(scores - jnp.max(scores, axis=1, keepdims=True))
        probs.append(expo * (1.0 / jnp.sum(expo, axis=1, keepdims=True)))
        probs_low.append(probs[k].astype(BF16).reshape(HEADS * nq, tile))
        attended.append(tn(probs_low[k], value_bd[k]).astype(BF16))
    attended = jnp.concatenate(attended, axis=0)
    film = nn(attended, out_w[...]) + out_b[...]
    scale = film[:, :width]
    change = (sent_f * scale + film[:, width:]) * valid
    block = (sent_f + change).astype(BF16)
    o_block_keep[...] = jnp.where(keep_left, block[:, :half], block[:, half:])
    o_block_give[...] = jnp.where(keep_left, block[:, half:], block[:, :half])
    stats[2] += col_sums(change * change)

    gy = gout_ref[...].astype(F32) * valid
    d_film = jnp.concatenate([(gy * sent_f).astype(BF16), gy.astype(BF16)], axis=1)
    sums[2] += col_sums(d_film.astype(F32))
    g_out[...] += tn(attended, d_film)
    d_att = nn(d_film, out_t[...]).astype(BF16)
    low_lane = lax.broadcasted_iota(jnp.int32, (nq, 2 * head), 1) < head

    def own_heads(x):
        pieces = []
        for p in range(HEADS // 2):
            at_row, at_lane = 2 * p * nq, 2 * p * head
            first = x[at_row : at_row + nq, at_lane : at_lane + 2 * head]
            second = x[at_row + nq : at_row + 2 * nq, at_lane : at_lane + 2 * head]
            pieces.append(jnp.where(low_lane, first, second))
        return jnp.concatenate(pieces, axis=1)

    d_query = []
    for k in range(subs):
        here = slice(k * tile, (k + 1) * tile)
        d_probs = nt(value_bd[k], d_att[here]).reshape(HEADS, nq, tile)
        weighted = probs[k] * d_probs
        inner = jnp.sum(weighted, axis=1, keepdims=True)
        d_scores = (weighted - probs[k] * inner).astype(BF16).reshape(HEADS * nq, tile)
        d_values[pl.ds(at[k], nq), :] += own_heads(nn(probs_low[k], d_att[here]))
        d_keys[pl.ds(at[k], nq), :] += own_heads(nn(d_scores, query[here]))
        d_query.append(tn(d_scores, key_bd[k]).astype(BF16))
    d_query = jnp.concatenate(d_query, axis=0)
    g_query[...] += tn(sent, d_query)
    d_sent = (gy * (1.0 + scale) + nn(d_query, query_t[...])).astype(BF16)
    o_dsent[...] = d_sent

    d_res = (d_sent.astype(F32) * ISQ2).astype(BF16)
    gs = (gskip_ref[...].astype(F32) * valid).astype(BF16)
    d_branch = jnp.concatenate([d_res, gs], axis=1)
    sums[1] += col_sums(d_branch.astype(F32))
    g_res[...] += tn(gate, d_branch)
    d_gate = nn(d_branch, res_t[...])
    d_pre = jnp.concatenate(
        [(d_gate * slope_a).astype(BF16), (d_gate * slope_s).astype(BF16)], axis=1
    )
    sums[0] += col_sums(d_pre.astype(F32))
    o_dpre[...] = d_pre
    g_cond[...] += tn(cond_ref[...], d_pre)

    @pl.when(t == 0)
    def _():
        o_edge[:EDGE, :] = d_pre[:EDGE, :]

    @pl.when(t == tiles // subs - 1)
    def _():
        here = prompt_ref[pl.ds(pl.multiple_of(mb0 * slots * nq, 16), items * nq), :]
        factor = head ** (-0.5)
        mine = pl.multiple_of(section * half, half)
        theirs = pl.multiple_of(half - section * half, half)

        o_edge[EDGE:, :] = d_pre[size - EDGE :, :]

        def put(i, ref, left, keep=o_keep, give=o_give):
            keep[i] = ref[pl.ds(mine, half), pl.ds(left, width)].astype(BF16)
            give[i] = ref[pl.ds(theirs, half), pl.ds(left, width)].astype(BF16)

        put(0, g_out, 0)
        put(1, g_out, width)
        put(2, g_query, 0)
        g_query[...] = tn(here, (d_keys[...] * factor).astype(BF16))
        put(3, g_query, 0)
        g_query[...] = tn(here, d_values[...].astype(BF16))
        put(4, g_query, 0)
        put(0, g_res, 0, o_keep_c, o_give_c)
        put(1, g_res, width, o_keep_c, o_give_c)
        put(2, g_cond, 0, o_keep_c, o_give_c)
        put(3, g_cond, width, o_keep_c, o_give_c)
        for i in range(3):
            line = jnp.sum(sums[i], axis=0, keepdims=True)
            o_vec[2 * i : 2 * i + 1, :] = line[:, :width]
            o_vec[2 * i + 1 : 2 * i + 2, :] = line[:, width:]
        for i in range(3):
            o_vec[6 + i : 7 + i, :] = jnp.sum(stats[i], axis=0, keepdims=True)
        lane = lax.broadcasted_iota(jnp.int32, (16 - 9, width), 1)
        digits = (count[0] >> (3 * jnp.minimum(lane, 8))) & 7
        o_vec[9:16, :] = jnp.where(lane < 8, digits, 0).astype(F32)


def weight_kernel(sec_ref, left_ref, dpre_ref, *refs):
    o_keep, o_give, acc = refs[-3:]
    section = sec_ref[0]
    width = acc.shape[0]
    half = width // 2
    acc[...] = tn(left_ref[...], dpre_ref[...])
    mine = pl.multiple_of(section * half, half)
    theirs = pl.multiple_of(half - section * half, half)
    for side in range(2):
        o_keep[side] = acc[pl.ds(mine, half), pl.ds(side * width, width)].astype(BF16)
        o_give[side] = acc[pl.ds(theirs, half), pl.ds(side * width, width)].astype(BF16)


def back_kernel(
    cfg,
    sec_ref,
    buckets,
    item_len,
    prev_ref,
    dpre_ref,
    next_ref,
    other_ref,
    dsent_ref,
    conv_w,
    steps,
    vec_ref,
    after_ref,
    o_keep,
    o_give,
    o_rows,
    d_step,
):
    tile, slots, subs, tiles, micro = cfg
    t = pl.program_id(0)
    section = sec_ref[0]
    width = dsent_ref.shape[1]
    half = width // 2
    count = tiles // subs

    @pl.when(t == 0)
    def _():
        d_step[...] = jnp.zeros_like(d_step)

    before = jnp.where(t == 0, other_ref[EDGE:, :], prev_ref[...])
    after = jnp.where(t == count - 1, other_ref[:EDGE, :], next_ref[...])
    ext = jnp.concatenate([before, dpre_ref[...], after], axis=0)
    spread = tile + 2 * EDGE
    place = rows_iota(spread, 128)
    row = rows_iota(tile, 128)
    ahead, behind, valid, item = [], [], [], []
    for k in range(subs):
        mb, slot, lim, prev_in, next_in = plan(
            section * tiles + t * subs + k, tile, slots, buckets, item_len
        )
        item.append(mb * slots + slot)
        lo = jnp.where(prev_in, 0, EDGE)
        hi = jnp.where(next_in, spread, tile + EDGE)
        here = jnp.where((place >= lo) & (place < hi), 1.0, 0.0)
        part = ext[k * tile : k * tile + spread].astype(F32)
        part = part * jnp.concatenate([here] * (2 * width // 128), axis=1)
        ahead.append(pltpu.roll(part, spread - SHIFT, 0)[EDGE : EDGE + tile].astype(BF16))
        behind.append(pltpu.roll(part, SHIFT, 0)[EDGE : EDGE + tile].astype(BF16))
        valid.append(jnp.where(row < lim, 1.0, 0.0))
    valid = jnp.concatenate([jnp.concatenate(valid, axis=0)] * (width // 128), axis=1)
    d_in = nt(jnp.concatenate(ahead, axis=0), conv_w[:width, :])
    d_in += nt(dpre_ref[...], conv_w[width : 2 * width, :])
    d_in += nt(jnp.concatenate(behind, axis=0), conv_w[2 * width :, :])
    d_mixed = (dsent_ref[...].astype(F32) * ISQ2 + d_in) * valid
    for k in range(subs):
        line = jnp.sum(col_sums(d_mixed[k * tile : (k + 1) * tile]), axis=0, keepdims=True)
        d_step[pl.ds(item[k], 1), :] += line
    low = d_mixed.astype(BF16)
    o_keep[...] = jnp.where(section == 0, low[:, :half], low[:, half:])
    o_give[...] = jnp.where(section == 0, low[:, half:], low[:, :half])

    @pl.when(t == count - 1)
    def _():
        items = micro * slots
        group = d_step.shape[0]
        lane = lax.broadcasted_iota(jnp.int32, (1, width), 1)
        index = jnp.zeros((1, width), jnp.int32)
        for i in range(items):
            index = jnp.where(lane == i, steps[i // slots, i % slots], index)
        index = jnp.where(section == 0, index, 0)
        d_step[items : items + 1, :] = (index >> 5).astype(F32)
        d_step[items + 1 : items + 2, :] = (index & 31).astype(F32)
        o_rows[:group, :] = d_step[...].astype(BF16)
        o_rows[group:, :] = vec_ref[...].astype(BF16)


SMALL = pl.CostEstimate(flops=1024, bytes_accessed=1024, transcendentals=0)
LARGE = pl.CostEstimate(flops=1 << 36, bytes_accessed=1024, transcendentals=0)
ANYWHERE = pl.BlockSpec(memory_space=pl.ANY)
PARAMS = pltpu.CompilerParams(vmem_limit_bytes=VMEM)


IN_VMEM = pl.BlockSpec(memory_space=pltpu.VMEM)
IN_SMEM = pl.BlockSpec(memory_space=pltpu.SMEM)
IN_HBM = pl.BlockSpec(memory_space=pltpu.HBM)


def struct(rows, width, dtype=BF16):
    return jax.ShapeDtypeStruct((rows, width), dtype)


def total(a, b):
    return (a.astype(F32) + b.astype(F32)).astype(BF16)


def at_bit(bit, rows):
    return pl.ds(pl.multiple_of(bit * rows, 16), rows)


def split_body(bit, held, got, keep, give):
    rows = keep.shape[0]
    keep[...] = total(held[at_bit(bit, rows), :], got[at_bit(bit, rows), :])
    give[...] = total(held[at_bit(1 - bit, rows), :], got[at_bit(1 - bit, rows), :])


def add_body(bit, held, got, out):
    out[...] = total(held[...], got[...])


def merge_body(bit, cur, got, out):
    rows = cur.shape[0]
    out[at_bit(bit, rows), :] = cur[...]
    out[at_bit(1 - bit, rows), :] = got[...]


def gather_body(bit, cur, got, out):
    rows = cur.shape[0] - EDGE
    out[at_bit(bit, rows), :] = cur[:rows, :]
    out[at_bit(1 - bit, rows), :] = got[:rows, :]
    out[2 * rows :, :] = total(cur[rows:, :], got[rows:, :])


def pair_kernel(bodies, outs, *refs):
    n = len(bodies)
    bits, arrays, results = refs[:n], refs[n : 3 * n], refs[3 * n + 1 :]
    for i, body in enumerate(bodies):
        count = outs[i]
        body(bits[i][0], arrays[2 * i], arrays[2 * i + 1], *results[:count])
        results = results[count:]


def pair_call(works, after, cost):
    outs = [len(w[4]) for w in works]
    shapes = [x for w in works for x in w[4]]
    return pl.pallas_call(
        functools.partial(pair_kernel, [w[0] for w in works], outs),
        in_specs=[IN_SMEM] * len(works) + [IN_VMEM] * (2 * len(works)) + [ANYWHERE],
        out_specs=[IN_VMEM] * len(shapes),
        out_shape=shapes,
        compiler_params=pltpu.CompilerParams(vmem_limit_bytes=24 * 1024 * 1024),
        cost_estimate=cost,
        name=works[0][0].__name__,
    )(*[w[1] for w in works], *[x for w in works for x in w[2:4]], after)


def first_kernel(bit_ref, held, got, after_ref, keep, give, bufs, sems):
    rows = keep.shape[0]
    bit = bit_ref[0]
    copies = []
    for i, half in enumerate((1 - bit, bit)):
        for j, array in enumerate((held, got)):
            copies.append(
                pltpu.make_async_copy(
                    array.at[at_bit(half, rows), :], bufs.at[2 * i + j], sems.at[2 * i + j]
                )
            )
    for copy in copies:
        copy.start()
    for i, out in enumerate((give, keep)):
        copies[2 * i].wait()
        copies[2 * i + 1].wait()
        out[...] = total(bufs[2 * i], bufs[2 * i + 1])


def split_first(held, got, bit, after, cost):
    rows, width = held.shape[0] // 2, held.shape[1]
    return pl.pallas_call(
        first_kernel,
        in_specs=[IN_SMEM, IN_HBM, IN_HBM, ANYWHERE],
        out_specs=[IN_VMEM] * 2,
        out_shape=[struct(rows, width)] * 2,
        scratch_shapes=[pltpu.VMEM((4, rows, width), BF16), pltpu.SemaphoreType.DMA((4,))],
        compiler_params=pltpu.CompilerParams(vmem_limit_bytes=24 * 1024 * 1024),
        cost_estimate=cost,
        name="split_first",
    )(bit, held, got, after)


def then_kernel(x_ref, after_ref, out_ref):
    out_ref[...] = x_ref[...]


def then(x, after):
    return pl.pallas_call(
        then_kernel,
        in_specs=[IN_VMEM, ANYWHERE],
        out_specs=IN_VMEM,
        out_shape=jax.ShapeDtypeStruct(x.shape, x.dtype),
        compiler_params=pltpu.CompilerParams(vmem_limit_bytes=16 * 1024 * 1024),
        cost_estimate=SMALL,
        name="then",
    )(x, after)


def join_kernel(count, sec_ref, *refs):
    section = sec_ref[0]
    arrays, outs = refs[: 2 * count], refs[2 * count + 1 : 3 * count + 1]
    mark, sems = refs[-2:]
    mark[...] = jnp.zeros_like(mark)
    copies = []
    for i in range(count):
        rows = arrays[2 * i].shape[0]
        for j, place in enumerate((section, 1 - section)):
            copies.append(
                pltpu.make_async_copy(
                    arrays[2 * i + j], outs[i].at[at_bit(place, rows), :], sems.at[2 * i + j]
                )
            )
    for copy in copies:
        copy.start()
    for copy in copies:
        copy.wait()


def join(sec, after, *pairs):
    rows, width = pairs[0][0].shape
    count = len(pairs)
    return pl.pallas_call(
        functools.partial(join_kernel, count),
        in_specs=[IN_SMEM] + [IN_VMEM] * (2 * count) + [ANYWHERE],
        out_specs=[IN_HBM] * count + [IN_VMEM],
        out_shape=[struct(2 * rows, width)] * count + [struct(8, 128, F32)],
        scratch_shapes=[pltpu.SemaphoreType.DMA((2 * count,))],
        compiler_params=pltpu.CompilerParams(vmem_limit_bytes=16 * 1024 * 1024),
        cost_estimate=SMALL,
        name="join",
    )(sec, *[x for pair in pairs for x in pair], after)


def swap(x):
    return lax.ppermute(x, "section", [(0, 1), (1, 0)])


class Sum:
    def __init__(self, orders):
        self.chips = lax.axis_size("dp")
        self.section = lax.axis_index("section")
        self.chip = lax.axis_index("dp")
        self.orders = orders
        self.levels = len(orders[0])

    def bit_of(self, step, section):
        where = jnp.where(section == 0, self.orders[0][step], self.orders[1][step])
        return ((self.chip >> where) & 1).astype(jnp.int32)

    def bit(self, step):
        return self.bit_of(step, self.section).reshape(1)

    def send(self, x, step):
        chips = self.chips
        route = [
            (s * chips + d, s * chips + (d ^ (1 << self.orders[s][step])))
            for s in range(2)
            for d in range(chips)
        ]
        return lax.ppermute(x, ("section", "dp"), route)

    def runs(self):
        mine, theirs = self.section, 1 - self.section
        own, other = self.bit_of(0, mine), self.bit_of(0, theirs)
        return jnp.stack(
            [2 * mine + own, 2 * mine + 1 - own, 2 * theirs + other, 2 * theirs + 1 - other]
        ).astype(jnp.int32)


class Batch:
    def __init__(self, sums, keep, give):
        self.sums = sums
        self.held = keep
        self.got = swap(give)
        self.step = 0

    def turn(self, after, more=(), cost=LARGE):
        sums, last = self.sums, self.sums.levels - 1
        at = self.step
        self.step += 1
        rows, width = self.held.shape
        if at == 0:
            self.held, give = split_first(self.held, self.got, sums.bit(0), after, cost)
            self.got, rest = sums.send(give, 0), []
        elif at < last:
            work = (split_body, sums.bit(at), self.held, self.got, [struct(rows // 2, width)] * 2)
            self.held, give, *rest = pair_call([work, *more], after, cost)
            self.got = sums.send(give, at)
        elif at <= last + 1:
            work = (add_body, sums.bit(0), self.held, self.got, [struct(rows, width)])
            self.held, *rest = pair_call([work, *more], after, cost)
            self.got = sums.send(self.held, at if at == last else last - 1)
        else:
            back = 2 * last + 1 - at
            work = (merge_body, sums.bit(back), self.held, self.got, [struct(2 * rows, width)])
            self.held, *rest = pair_call([work, *more], after, cost)
            self.got = sums.send(self.held, back - 1)
        return (self.held, *rest)

    @property
    def turns(self):
        return 2 * self.sums.levels - 1

    def early(self, shapes, spots, after, outs=()):
        return place(self.sums.runs(), (0, 2), (self.held, swap(self.held)), shapes, spots, after, outs)

    def arrive(self, after):
        self.got = then(self.got, after)
        self.last = swap(self.got)
        return self.got

    def late(self, shapes, spots, after, outs):
        return place(self.sums.runs(), (1, 3), (self.got, self.last), shapes, spots, after, outs)


def place_kernel(which, spots, count, runs, p0, p1, after_ref, *refs):
    outs, (mark, buf, sems) = refs[-3 - count : -3], refs[-3:]
    mark[...] = jnp.zeros_like(mark)
    rows = buf.shape[1]
    per_run = p0.shape[0] // rows
    for wait in (False, True):
        for run in range(4):
            mine, theirs = runs[which[0]] == run, runs[which[1]] == run
            base = run * per_run

            @pl.when(mine | theirs)
            def _(run=run, mine=mine):
                slot = jnp.where(mine, 0, 1)
                for w in range(run * per_run, (run + 1) * per_run):
                    spot = spots[w]
                    if spot is None:
                        continue
                    j = w - base
                    k, row, col = spot
                    copy = pltpu.make_async_copy(
                        buf.at[slot * per_run + j],
                        outs[k].at[pl.ds(row, rows), pl.ds(col, buf.shape[2])],
                        sems.at[slot * per_run + j],
                    )
                    if wait:
                        copy.wait()
                    else:
                        part = slice(j * rows, (j + 1) * rows)
                        value = jnp.where(mine, p0[part, :], p1[part, :])
                        buf[slot * per_run + j] = value.astype(F32)
                        copy.start()


def spots_of(targets, width):
    quarter = width // 4
    spots = []
    for section in range(2):
        for k, row, col in targets:
            for u in range(2):
                spots.append((k, row + (2 * section + u) * quarter, col))
    return spots


def place(runs, which, pieces, shapes, spots, after, outs=()):
    length, width = pieces[0].shape
    quarter = width // 4
    per_run = length // quarter
    half = len(spots) // 2
    full = [None] * (4 * per_run)
    full[:half] = spots[:half]
    full[2 * per_run : 2 * per_run + half] = spots[half:]
    return pl.pallas_call(
        functools.partial(place_kernel, which, full, len(shapes)),
        in_specs=[IN_SMEM] + [IN_VMEM] * 2 + [ANYWHERE] + [IN_HBM] * len(outs),
        out_specs=[IN_HBM] * len(shapes) + [IN_VMEM],
        out_shape=list(shapes) + [struct(8, 128, F32)],
        input_output_aliases={4 + k: k for k in range(len(outs))},
        scratch_shapes=[
            pltpu.VMEM((2 * per_run, quarter, width), F32),
            pltpu.SemaphoreType.DMA((2 * per_run,)),
        ],
        compiler_params=pltpu.CompilerParams(vmem_limit_bytes=24 * 1024 * 1024),
        cost_estimate=SMALL,
        name="place",
    )(runs, *pieces, after, *outs)


def step_kernel(items, group, rows_ref, after_ref, out_ref, o_low, o_res, o_out, o_levels, mark):
    mark[...] = jnp.zeros_like(mark)
    width = rows_ref.shape[1]
    half = width // 2
    rows = rows_ref[: rows_ref.shape[0] - EDGE, :].astype(F32).reshape(-1, group, width)
    lanes = (rows.shape[0], group, 128)
    index = 32.0 * rows[:, items : items + 1, :128] + rows[:, items + 1 : items + 2, :128]
    diagonal = lax.broadcasted_iota(jnp.int32, lanes, 1) == lax.broadcasted_iota(
        jnp.int32, lanes, 2
    )
    index = jnp.sum(jnp.where(diagonal, index, 0.0), axis=2, keepdims=True)
    index = index.reshape(-1, 1)
    lane = lax.broadcasted_iota(jnp.int32, (index.shape[0], half), 1).astype(F32)
    angle = index * jnp.exp(lane * F32(-math.log(10000.0) / half))
    emb = jnp.concatenate([jnp.sin(angle), jnp.cos(angle)], axis=1)
    used = lax.broadcasted_iota(jnp.int32, rows.shape, 1) < items
    sums = jnp.where(used, rows, 0.0).reshape(-1, width)
    out_ref[...] = tn(emb.astype(BF16), sums.astype(BF16))
    vec = rows_ref[rows_ref.shape[0] - EDGE :, :].astype(F32)
    for i, out in enumerate((o_low, o_res, o_out)):
        out[:, :width] = vec[2 * i : 2 * i + 1, :]
        out[:, width:] = vec[2 * i + 1 : 2 * i + 2, :]
    digit = lax.broadcasted_iota(jnp.int32, (1, width), 1)
    weight = jnp.where(digit < 8, 1 << (3 * jnp.minimum(digit, 8)), 0).astype(F32)
    frames = jnp.sum(vec[9:10, :] * weight, axis=1, keepdims=True) * width
    sizes = jnp.sum(vec[6:9, :], axis=1, keepdims=True)
    o_levels[...] = jnp.broadcast_to(jnp.sqrt(sizes / frames), o_levels.shape)


def padded(x, rows):
    return x if x.shape[0] == rows else jnp.pad(x, ((0, rows - x.shape[0]), (0, 0)))


def on_device(
    input_rows,
    conditioning,
    prompt,
    buckets,
    item_len,
    step_index,
    output_gradient,
    grad_skip,
    step_w,
    conv_w,
    cond_w,
    conv_b,
    res_w,
    res_b,
    query_w,
    key_w,
    value_w,
    out_w,
    out_b,
):
    section = lax.axis_index("section")
    sec = section.astype(jnp.int32).reshape(1)
    total, width = input_rows.shape
    micro, slots = item_len.shape
    nq = prompt.shape[2]
    frames = total // micro
    tile = frames // slots
    own = total // 2
    tiles = own // tile
    subs = 2
    size = subs * tile
    grid = tiles // subs
    mb_own = -(-own // frames)
    items = mb_own * slots
    half = width // 2
    taps = conv_w.shape[0]
    per = size // EDGE
    last = total // EDGE - 1
    wide = 2 * width
    conv_flat = conv_w.reshape(taps * width, wide)
    flat_prompt = prompt.reshape(-1, width)

    def whole(x):
        n = x.ndim
        return pl.BlockSpec(x.shape, lambda t, *_: (0,) * n, pipeline_mode=pl.Buffered(1))

    smem = pl.BlockSpec(memory_space=pltpu.SMEM)

    def chip_tile(cols):
        return pl.BlockSpec((size, cols), lambda t, s, *_: (s[0] * grid + t, 0))

    def own_tile(cols):
        return pl.BlockSpec((size, cols), lambda t, *_: (t, 0))

    def const(shape):
        return pl.BlockSpec(shape, lambda t, *_: (0,) * len(shape))

    prev_chip = pl.BlockSpec(
        (EDGE, width), lambda t, s, *_: (jnp.maximum((s[0] * grid + t) * per - 1, 0), 0)
    )
    next_chip = pl.BlockSpec(
        (EDGE, width), lambda t, s, *_: (jnp.minimum((s[0] * grid + t + 1) * per, last), 0)
    )
    vectors = [x.reshape(1, -1) for x in (conv_b, res_b, out_b)]
    weights = [
        step_w,
        conv_flat,
        cond_w,
        vectors[0],
        res_w,
        vectors[1],
        query_w,
        key_w,
        value_w,
        out_w,
        vectors[2],
    ]

    def shape(*dims, dtype=BF16):
        return jax.ShapeDtypeStruct(dims, dtype)

    def blocks_of(n):
        return const((n, half, width)), shape(n, half, width)

    film_spec, film_shape = blocks_of(5)
    side_spec, side_shape = blocks_of(4)
    (
        stack,
        d_pre,
        edge,
        d_sent,
        block_keep,
        block_give,
        skip_keep,
        skip_give,
        keep_a,
        give_a,
        keep_c,
        give_c,
        vec,
    ) = pl.pallas_call(
        functools.partial(forward_kernel, (tile, slots, nq, subs, tiles, mb_own, micro)),
        grid_spec=pltpu.PrefetchScalarGridSpec(
            num_scalar_prefetch=1,
            grid=(grid,),
            in_specs=[smem, smem, smem, prev_chip, chip_tile(width), next_chip]
            + [chip_tile(width)] * 3
            + [whole(flat_prompt)]
            + [whole(w) for w in weights],
            out_specs=[own_tile(taps * width), own_tile(wide), const((2 * EDGE, wide))]
            + [own_tile(width)]
            + [own_tile(half)] * 4
            + [film_spec, film_spec, side_spec, side_spec, const((16, width))],
            scratch_shapes=[
                pltpu.VMEM((items, width), F32),
                pltpu.VMEM((items * nq, width), BF16),
                pltpu.VMEM((items * nq, width), BF16),
                pltpu.VMEM((items * nq, width), F32),
                pltpu.VMEM((items * nq, width), F32),
                pltpu.VMEM((width, wide), F32),
                pltpu.VMEM((width, width), F32),
                pltpu.VMEM((3, 8, wide), F32),
                pltpu.VMEM((3, 8, width), F32),
                pltpu.SMEM((1,), jnp.int32),
                pltpu.VMEM((wide, width), BF16),
                pltpu.VMEM((width, width), BF16),
                pltpu.VMEM((wide, width), BF16),
                pltpu.VMEM((width, wide), F32),
                pltpu.VMEM((width, wide), F32),
                pltpu.VMEM((HEADS * nq, width), BF16),
            ],
        ),
        out_shape=[
            shape(own, taps * width),
            shape(own, wide),
            shape(2 * EDGE, wide),
            shape(own, width),
            shape(own, half),
            shape(own, half),
            shape(own, half),
            shape(own, half),
            film_shape,
            film_shape,
            side_shape,
            side_shape,
            shape(16, width, dtype=F32),
        ],
        compiler_params=pltpu.CompilerParams(vmem_limit_bytes=VMEM),
        cost_estimate=LARGE,
        name="forward",
    )(
        sec,
        buckets,
        item_len,
        step_index,
        input_rows,
        input_rows,
        input_rows,
        conditioning,
        output_gradient,
        grad_skip,
        flat_prompt,
        *weights,
    )

    bits = list(range(lax.axis_size("dp").bit_length() - 1))
    other = [bits[1], bits[0]] + bits[2:]
    if len(other) > 3:
        other[-2], other[-1] = other[-1], other[-2]
    sums = Sum((bits, other))
    far_first = Sum((bits[2:] + bits[:2], bits[:1:-1] + bits[1::-1]))
    unit = 16 * lax.axis_size("dp") // 2

    def batch(keep, give, sums):
        rows = keep.shape[0] * half
        rows = -(-rows // unit) * unit
        return Batch(
            sums, padded(keep.reshape(-1, width), rows), padded(give.reshape(-1, width), rows)
        )

    batch_a, batch_c = batch(keep_a, give_a, far_first), batch(keep_c, give_c, sums)
    block_got, skip_got, other_edge = swap(block_give), swap(skip_give), swap(edge)
    spec = pl.BlockSpec((2, half, width), lambda i, *_: (i, 0, 0))
    keep_b, give_b = pl.pallas_call(
        weight_kernel,
        grid_spec=pltpu.PrefetchScalarGridSpec(
            num_scalar_prefetch=1,
            grid=(taps,),
            in_specs=[pl.BlockSpec((own, width), lambda i, *_: (0, i)), whole(d_pre)],
            out_specs=[spec, spec],
            scratch_shapes=[pltpu.VMEM((width, wide), F32)],
        ),
        out_shape=[shape(2 * taps, half, width)] * 2,
        compiler_params=pltpu.CompilerParams(vmem_limit_bytes=KB_VMEM),
        cost_estimate=LARGE,
        name="weights",
    )(sec, stack, d_pre)
    batch_b = batch(keep_b, give_b, sums)
    (after,) = batch_a.turn(keep_b)
    (after,) = batch_c.turn(after)

    group = -(-(micro * slots + 2) // 16) * 16
    rows_last = own // EDGE - 1
    in_keep, in_give, rows_now = pl.pallas_call(
        functools.partial(back_kernel, (tile, slots, subs, tiles, micro)),
        grid_spec=pltpu.PrefetchScalarGridSpec(
            num_scalar_prefetch=1,
            grid=(grid,),
            in_specs=[
                smem,
                smem,
                pl.BlockSpec((EDGE, wide), lambda t, *_: (jnp.maximum(t * per - 1, 0), 0)),
                own_tile(wide),
                pl.BlockSpec(
                    (EDGE, wide), lambda t, *_: (jnp.minimum((t + 1) * per, rows_last), 0)
                ),
                whole(other_edge),
                own_tile(width),
                whole(conv_flat),
                smem,
                whole(vec),
                ANYWHERE,
            ],
            out_specs=[own_tile(half), own_tile(half), const((group + EDGE, width))],
            scratch_shapes=[pltpu.VMEM((group, width), F32)],
        ),
        out_shape=[shape(own, half), shape(own, half), shape(group + EDGE, width)],
        compiler_params=pltpu.CompilerParams(vmem_limit_bytes=KC_VMEM),
        cost_estimate=LARGE,
        name="back",
    )(
        sec,
        buckets,
        item_len,
        d_pre,
        d_pre,
        d_pre,
        other_edge,
        d_sent,
        conv_flat,
        step_index,
        vec,
        after,
    )
    in_got = swap(in_give)

    (after,) = batch_b.turn(rows_now)
    block_out, skip_out, after = join(
        sec, after, (block_keep, block_got), (skip_keep, skip_got)
    )
    rows_got, rows_bit, gathered = swap(rows_now), sec, 0
    batches = {"a": batch_a, "b": batch_b, "c": batch_c}
    order = "acb" + "cab" * 2 + "acb" * (batch_a.turns - 5) + "cab"
    for name in order:
        turner = batches[name]
        if name == "b" and gathered <= sums.levels:
            n = rows_now.shape[0]
            work = (add_body, rows_bit, rows_now, rows_got, [struct(n, width)])
            if gathered:
                work = (gather_body, rows_bit, rows_now, rows_got, [struct(2 * n - EDGE, width)])
            after, rows_now = turner.turn(after, [work])
            if gathered < sums.levels:
                at = sums.levels - 1 - gathered
                route = [(d, d ^ (1 << at)) for d in range(sums.chips)]
                rows_got = lax.ppermute(rows_now, "dp", route)
                rows_bit = ((sums.chip >> at) & 1).astype(jnp.int32).reshape(1)
            gathered += 1
        else:
            (after,) = turner.turn(after)

    line = struct(1, wide, F32)
    g_step, g_convb, g_resb, g_outb, levels, mark = pl.pallas_call(
        functools.partial(step_kernel, micro * slots, group),
        in_specs=[IN_VMEM, ANYWHERE],
        out_specs=[IN_VMEM] * 6,
        out_shape=[struct(width, width, F32), line, line, line]
        + [struct(3, 128, F32), struct(8, 128, F32)],
        compiler_params=pltpu.CompilerParams(vmem_limit_bytes=24 * 1024 * 1024),
        cost_estimate=LARGE,
        name="step_grad",
    )(rows_now, after)
    in_grad, mark = join(sec, mark, (in_keep, in_got))

    def pairs(k, count, base=0):
        return [(k, base + i * width, col) for i in range(count) for col in (0, width)]

    square, tall = struct(width, width, F32), struct(width, wide, F32)
    shapes_a = [tall, square, square, square]
    spots_a = spots_of(pairs(0, 1) + [(k, 0, 0) for k in (1, 2, 3)], width)
    shapes_b, spots_b = [struct(taps * width, wide, F32)], spots_of(pairs(0, taps), width)
    shapes_c, spots_c = [tall, tall], spots_of(pairs(0, 1) + pairs(1, 1), width)
    *outs_a, mark = batch_a.early(shapes_a, spots_a, mark)
    *outs_c, mark = batch_c.early(shapes_c, spots_c, mark)
    *outs_b, mark = batch_b.early(shapes_b, spots_b, mark)
    mark = batch_b.arrive(batch_c.arrive(batch_a.arrive(mark)))
    *outs_a, mark = batch_a.late(shapes_a, spots_a, mark, outs_a)
    *outs_c, mark = batch_c.late(shapes_c, spots_c, mark, outs_c)
    *outs_b, mark = batch_b.late(shapes_b, spots_b, mark, outs_b)
    g_out, g_query, g_key, g_value = outs_a
    g_conv = outs_b[0].reshape(conv_w.shape)
    g_res, g_cond = outs_c
    g_convb, g_resb, g_outb = (x.reshape(wide) for x in (g_convb, g_resb, g_outb))
    levels = levels[:, 0]
    return (
        block_out,
        skip_out,
        in_grad,
        g_step,
        g_conv,
        g_cond,
        g_convb,
        g_res,
        g_resb,
        g_query,
        g_key,
        g_value,
        g_out,
        g_outb,
        levels,
    )


def solution(mesh):
    rows = P("dp", None)
    split = P("dp", "section")
    return jax.shard_map(
        on_device,
        mesh=mesh,
        in_specs=(rows, rows, P("dp", None, None, None), P("dp"), rows, rows, rows, rows)
        + (P(),) * 11,
        out_specs=(split,) * 3 + (P(),) * 12,
        check_vma=False,
    )
```

```python
import functools
import math

import jax
import jax.numpy as jnp
from jax import lax
from jax.experimental import pallas as pl
from jax.experimental.pallas import tpu as pltpu
from jax.sharding import PartitionSpec as P

HEADS = 8
SHIFT = 2
EDGE = 16
ISQ2 = 0.7071067811865476
F32 = jnp.float32
BF16 = jnp.bfloat16
VMEM = 56 * 1024 * 1024
KB_VMEM = 56 * 1024 * 1024
KC_VMEM = 32 * 1024 * 1024


def nn(a, b):
    return lax.dot_general(a, b, (((1,), (0,)), ((), ())), preferred_element_type=F32)


def nt(a, b):
    return lax.dot_general(a, b, (((1,), (1,)), ((), ())), preferred_element_type=F32)


def tn(a, b):
    return lax.dot_general(a, b, (((0,), (0,)), ((), ())), preferred_element_type=F32)


def rows_iota(rows, cols):
    return lax.broadcasted_iota(jnp.int32, (rows, cols), 0)


def col_sums(x):
    rows, cols = x.shape
    return jnp.sum(x.reshape(rows // 8, 8, cols), axis=0)


def plan(g, tile, slots, buckets, item_len):
    mb = g // slots
    q = g - mb * slots
    span = slots >> buckets[mb]
    slot = q // span
    off = q - slot * span
    lim = item_len[mb, slot] - off * tile
    return mb, slot, lim, off > 0, off < span - 1


def forward_kernel(
    cfg,
    sec_ref,
    buckets,
    item_len,
    steps,
    prev_ref,
    rows_ref,
    next_ref,
    cond_ref,
    gout_ref,
    gskip_ref,
    prompt_ref,
    step_w,
    conv_w,
    cond_w,
    conv_b,
    res_w,
    res_b,
    query_w,
    key_w,
    value_w,
    out_w,
    out_b,
    o_stack,
    o_dpre,
    o_edge,
    o_dsent,
    o_block_keep,
    o_block_give,
    o_skip_keep,
    o_skip_give,
    o_keep,
    o_give,
    o_keep_c,
    o_give_c,
    o_vec,
    proj,
    keys,
    values,
    d_keys,
    d_values,
    g_out,
    g_query,
    sums,
    stats,
    count,
    out_t,
    query_t,
    res_t,
    g_res,
    g_cond,
    own_head,
):
    tile, slots, nq, subs, tiles, mb_own, micro = cfg
    t = pl.program_id(0)
    section = sec_ref[0]
    size = subs * tile
    width = rows_ref.shape[1]
    half = width // 2
    head = width // HEADS
    mb0 = section * (micro - mb_own)
    items = mb_own * slots
    keep_left = section == 0

    @pl.when(t == 0)
    def _():
        row = rows_iota(items, half)
        when = jnp.zeros((items, half), F32)
        for i in range(items):
            s = steps[mb0 + i // slots, i % slots].astype(F32)
            when = jnp.where(row == i, s, when)
        lane = lax.broadcasted_iota(jnp.int32, (items, half), 1).astype(F32)
        angle = when * jnp.exp(lane * F32(-math.log(10000.0) / half))
        emb = jnp.concatenate([jnp.sin(angle), jnp.cos(angle)], axis=1)
        proj[...] = nn(emb.astype(BF16), step_w[...])
        here = prompt_ref[pl.ds(pl.multiple_of(mb0 * slots * nq, 16), items * nq), :]
        factor = head ** (-0.5)
        keys[...] = (nn(here, key_w[...]).astype(BF16) * BF16(factor)).astype(BF16)
        values[...] = nn(here, value_w[...]).astype(BF16)
        d_keys[...] = jnp.zeros_like(d_keys)
        d_values[...] = jnp.zeros_like(d_values)
        g_out[...] = jnp.zeros_like(g_out)
        out_t[...] = out_w[...].T
        query_t[...] = query_w[...].T
        res_t[...] = res_w[...].T
        g_res[...] = jnp.zeros_like(g_res)
        g_cond[...] = jnp.zeros_like(g_cond)
        at_row = rows_iota(HEADS * nq, width) // nq
        at_lane = lax.broadcasted_iota(jnp.int32, (HEADS * nq, width), 1) // head
        own_head[...] = jnp.where(at_row == at_lane, 1.0, 0.0).astype(BF16)
        g_query[...] = jnp.zeros_like(g_query)
        sums[...] = jnp.zeros_like(sums)
        stats[...] = jnp.zeros_like(stats)
        count[0] = 0

    ext = jnp.concatenate([prev_ref[...], rows_ref[...], next_ref[...]], axis=0)
    spread = tile + 2 * EDGE
    place = rows_iota(spread, 128)

    def lanes(mask):
        return jnp.concatenate([mask] * (width // 128), axis=1)

    mixed, behind, ahead, at = [], [], [], []
    valid = []
    row = rows_iota(tile, 128)
    for k in range(subs):
        mb, slot, lim, prev_in, next_in = plan(
            section * tiles + t * subs + k, tile, slots, buckets, item_len
        )
        item = (mb - mb0) * slots + slot
        at.append(pl.multiple_of(item * nq, nq))
        lo = jnp.where(prev_in, 0, EDGE)
        hi = jnp.where(next_in, tile + 2 * EDGE, tile + EDGE)
        hi = jnp.minimum(hi, lim + EDGE)
        part = ext[k * tile : k * tile + spread].astype(F32) + proj[pl.ds(item, 1), :]
        part = part * lanes(jnp.where((place >= lo) & (place < hi), 1.0, 0.0))
        mixed.append(part[EDGE : EDGE + tile])
        behind.append(pltpu.roll(part, SHIFT, 0)[EDGE : EDGE + tile].astype(BF16))
        ahead.append(pltpu.roll(part, spread - SHIFT, 0)[EDGE : EDGE + tile].astype(BF16))
        valid.append(jnp.where(row < lim, 1.0, 0.0))
        count[0] += jnp.clip(lim, 0, tile)
    mixed = jnp.concatenate(mixed, axis=0)
    valid = lanes(jnp.concatenate(valid, axis=0))
    stacked = jnp.concatenate(
        [jnp.concatenate(behind, axis=0), mixed.astype(BF16), jnp.concatenate(ahead, axis=0)],
        axis=1,
    )
    o_stack[...] = stacked
    pre = nn(stacked, conv_w[...]) + nn(cond_ref[...], cond_w[...]) + conv_b[...]
    a = jnp.tanh(pre[:, :width])
    s = 0.5 * jnp.tanh(0.5 * pre[:, width:]) + 0.5
    both = a * s
    gate = both.astype(BF16)
    slope_a = s - both * a
    slope_s = both - both * s
    branch = nn(gate, res_w[...]) + res_b[...]
    res_part = branch[:, :width] * valid
    skip = (branch[:, width:] * valid).astype(BF16)
    o_skip_keep[...] = jnp.where(keep_left, skip[:, :half], skip[:, half:])
    o_skip_give[...] = jnp.where(keep_left, skip[:, half:], skip[:, :half])
    hidden = (mixed + res_part) * ISQ2
    sent = hidden.astype(BF16)
    sent_f = sent.astype(F32)
    stats[0] += col_sums(hidden * hidden)
    stats[1] += col_sums(res_part * res_part)

    query = nn(sent, query_w[...]).astype(BF16)
    mask = own_head[...]
    probs, probs_low, key_bd, value_bd, attended = [], [], [], [], []
    for k in range(subs):
        key_bd.append(jnp.concatenate([keys[pl.ds(at[k], nq), :]] * HEADS, axis=0) * mask)
        value_bd.append(jnp.concatenate([values[pl.ds(at[k], nq), :]] * HEADS, axis=0) * mask)
        scores = nt(key_bd[k], query[k * tile : (k + 1) * tile]).reshape(HEADS, nq, tile)
        expo = jnp.exp(scores - jnp.max(scores, axis=1, keepdims=True))
        probs.append(expo * (1.0 / jnp.sum(expo, axis=1, keepdims=True)))
        probs_low.append(probs[k].astype(BF16).reshape(HEADS * nq, tile))
        attended.append(tn(probs_low[k], value_bd[k]).astype(BF16))
    attended = jnp.concatenate(attended, axis=0)
    film = nn(attended, out_w[...]) + out_b[...]
    scale = film[:, :width]
    change = (sent_f * scale + film[:, width:]) * valid
    block = (sent_f + change).astype(BF16)
    o_block_keep[...] = jnp.where(keep_left, block[:, :half], block[:, half:])
    o_block_give[...] = jnp.where(keep_left, block[:, half:], block[:, :half])
    stats[2] += col_sums(change * change)

    gy = gout_ref[...].astype(F32) * valid
    d_film = jnp.concatenate([(gy * sent_f).astype(BF16), gy.astype(BF16)], axis=1)
    sums[2] += col_sums(d_film.astype(F32))
    g_out[...] += tn(attended, d_film)
    d_att = nn(d_film, out_t[...]).astype(BF16)
    low_lane = lax.broadcasted_iota(jnp.int32, (nq, 2 * head), 1) < head

    def own_heads(x):
        pieces = []
        for p in range(HEADS // 2):
            at_row, at_lane = 2 * p * nq, 2 * p * head
            first = x[at_row : at_row + nq, at_lane : at_lane + 2 * head]
            second = x[at_row + nq : at_row + 2 * nq, at_lane : at_lane + 2 * head]
            pieces.append(jnp.where(low_lane, first, second))
        return jnp.concatenate(pieces, axis=1)

    d_query = []
    for k in range(subs):
        here = slice(k * tile, (k + 1) * tile)
        d_probs = nt(value_bd[k], d_att[here]).reshape(HEADS, nq, tile)
        weighted = probs[k] * d_probs
        inner = jnp.sum(weighted, axis=1, keepdims=True)
        d_scores = (weighted - probs[k] * inner).astype(BF16).reshape(HEADS * nq, tile)
        d_values[pl.ds(at[k], nq), :] += own_heads(nn(probs_low[k], d_att[here]))
        d_keys[pl.ds(at[k], nq), :] += own_heads(nn(d_scores, query[here]))
        d_query.append(tn(d_scores, key_bd[k]).astype(BF16))
    d_query = jnp.concatenate(d_query, axis=0)
    g_query[...] += tn(sent, d_query)
    d_sent = (gy * (1.0 + scale) + nn(d_query, query_t[...])).astype(BF16)
    o_dsent[...] = d_sent

    d_res = (d_sent.astype(F32) * ISQ2).astype(BF16)
    gs = (gskip_ref[...].astype(F32) * valid).astype(BF16)
    d_branch = jnp.concatenate([d_res, gs], axis=1)
    sums[1] += col_sums(d_branch.astype(F32))
    g_res[...] += tn(gate, d_branch)
    d_gate = nn(d_branch, res_t[...])
    d_pre = jnp.concatenate(
        [(d_gate * slope_a).astype(BF16), (d_gate * slope_s).astype(BF16)], axis=1
    )
    sums[0] += col_sums(d_pre.astype(F32))
    o_dpre[...] = d_pre
    g_cond[...] += tn(cond_ref[...], d_pre)

    @pl.when(t == 0)
    def _():
        o_edge[:EDGE, :] = d_pre[:EDGE, :]

    @pl.when(t == tiles // subs - 1)
    def _():
        here = prompt_ref[pl.ds(pl.multiple_of(mb0 * slots * nq, 16), items * nq), :]
        factor = head ** (-0.5)
        mine = pl.multiple_of(section * half, half)
        theirs = pl.multiple_of(half - section * half, half)

        o_edge[EDGE:, :] = d_pre[size - EDGE :, :]

        def put(i, ref, left, keep=o_keep, give=o_give):
            keep[i] = ref[pl.ds(mine, half), pl.ds(left, width)].astype(BF16)
            give[i] = ref[pl.ds(theirs, half), pl.ds(left, width)].astype(BF16)

        put(0, g_out, 0)
        put(1, g_out, width)
        put(2, g_query, 0)
        g_query[...] = tn(here, (d_keys[...] * factor).astype(BF16))
        put(3, g_query, 0)
        g_query[...] = tn(here, d_values[...].astype(BF16))
        put(4, g_query, 0)
        put(0, g_res, 0, o_keep_c, o_give_c)
        put(1, g_res, width, o_keep_c, o_give_c)
        put(2, g_cond, 0, o_keep_c, o_give_c)
        put(3, g_cond, width, o_keep_c, o_give_c)
        for i in range(3):
            line = jnp.sum(sums[i], axis=0, keepdims=True)
            o_vec[2 * i : 2 * i + 1, :] = line[:, :width]
            o_vec[2 * i + 1 : 2 * i + 2, :] = line[:, width:]
        for i in range(3):
            o_vec[6 + i : 7 + i, :] = jnp.sum(stats[i], axis=0, keepdims=True)
        lane = lax.broadcasted_iota(jnp.int32, (16 - 9, width), 1)
        digits = (count[0] >> (3 * jnp.minimum(lane, 8))) & 7
        o_vec[9:16, :] = jnp.where(lane < 8, digits, 0).astype(F32)


def weight_kernel(sec_ref, left_ref, dpre_ref, *refs):
    o_keep, o_give, acc = refs[-3:]
    section = sec_ref[0]
    width = acc.shape[0]
    half = width // 2
    acc[...] = tn(left_ref[...], dpre_ref[...])
    mine = pl.multiple_of(section * half, half)
    theirs = pl.multiple_of(half - section * half, half)
    for side in range(2):
        o_keep[side] = acc[pl.ds(mine, half), pl.ds(side * width, width)].astype(BF16)
        o_give[side] = acc[pl.ds(theirs, half), pl.ds(side * width, width)].astype(BF16)


def back_kernel(
    cfg,
    sec_ref,
    buckets,
    item_len,
    prev_ref,
    dpre_ref,
    next_ref,
    other_ref,
    dsent_ref,
    conv_w,
    steps,
    vec_ref,
    after_ref,
    o_keep,
    o_give,
    o_rows,
    d_step,
):
    tile, slots, subs, tiles, micro = cfg
    t = pl.program_id(0)
    section = sec_ref[0]
    width = dsent_ref.shape[1]
    half = width // 2
    count = tiles // subs

    @pl.when(t == 0)
    def _():
        d_step[...] = jnp.zeros_like(d_step)

    before = jnp.where(t == 0, other_ref[EDGE:, :], prev_ref[...])
    after = jnp.where(t == count - 1, other_ref[:EDGE, :], next_ref[...])
    ext = jnp.concatenate([before, dpre_ref[...], after], axis=0)
    spread = tile + 2 * EDGE
    place = rows_iota(spread, 128)
    row = rows_iota(tile, 128)
    ahead, behind, valid, item = [], [], [], []
    for k in range(subs):
        mb, slot, lim, prev_in, next_in = plan(
            section * tiles + t * subs + k, tile, slots, buckets, item_len
        )
        item.append(mb * slots + slot)
        lo = jnp.where(prev_in, 0, EDGE)
        hi = jnp.where(next_in, spread, tile + EDGE)
        here = jnp.where((place >= lo) & (place < hi), 1.0, 0.0)
        part = ext[k * tile : k * tile + spread].astype(F32)
        part = part * jnp.concatenate([here] * (2 * width // 128), axis=1)
        ahead.append(pltpu.roll(part, spread - SHIFT, 0)[EDGE : EDGE + tile].astype(BF16))
        behind.append(pltpu.roll(part, SHIFT, 0)[EDGE : EDGE + tile].astype(BF16))
        valid.append(jnp.where(row < lim, 1.0, 0.0))
    valid = jnp.concatenate([jnp.concatenate(valid, axis=0)] * (width // 128), axis=1)
    d_in = nt(jnp.concatenate(ahead, axis=0), conv_w[:width, :])
    d_in += nt(dpre_ref[...], conv_w[width : 2 * width, :])
    d_in += nt(jnp.concatenate(behind, axis=0), conv_w[2 * width :, :])
    d_mixed = (dsent_ref[...].astype(F32) * ISQ2 + d_in) * valid
    for k in range(subs):
        line = jnp.sum(col_sums(d_mixed[k * tile : (k + 1) * tile]), axis=0, keepdims=True)
        d_step[pl.ds(item[k], 1), :] += line
    low = d_mixed.astype(BF16)
    o_keep[...] = jnp.where(section == 0, low[:, :half], low[:, half:])
    o_give[...] = jnp.where(section == 0, low[:, half:], low[:, :half])

    @pl.when(t == count - 1)
    def _():
        items = micro * slots
        group = d_step.shape[0]
        lane = lax.broadcasted_iota(jnp.int32, (1, width), 1)
        index = jnp.zeros((1, width), jnp.int32)
        for i in range(items):
            index = jnp.where(lane == i, steps[i // slots, i % slots], index)
        index = jnp.where(section == 0, index, 0)
        d_step[items : items + 1, :] = (index >> 5).astype(F32)
        d_step[items + 1 : items + 2, :] = (index & 31).astype(F32)
        o_rows[:group, :] = d_step[...].astype(BF16)
        o_rows[group:, :] = vec_ref[...].astype(BF16)


SMALL = pl.CostEstimate(flops=1024, bytes_accessed=1024, transcendentals=0)
LARGE = pl.CostEstimate(flops=1 << 36, bytes_accessed=1024, transcendentals=0)
ANYWHERE = pl.BlockSpec(memory_space=pl.ANY)
PARAMS = pltpu.CompilerParams(vmem_limit_bytes=VMEM)


IN_VMEM = pl.BlockSpec(memory_space=pltpu.VMEM)
IN_SMEM = pl.BlockSpec(memory_space=pltpu.SMEM)
IN_HBM = pl.BlockSpec(memory_space=pltpu.HBM)


def struct(rows, width, dtype=BF16):
    return jax.ShapeDtypeStruct((rows, width), dtype)


def total(a, b):
    return (a.astype(F32) + b.astype(F32)).astype(BF16)


def at_bit(bit, rows):
    return pl.ds(pl.multiple_of(bit * rows, 16), rows)


def split_body(bit, held, got, keep, give):
    rows = keep.shape[0]
    keep[...] = total(held[at_bit(bit, rows), :], got[at_bit(bit, rows), :])
    give[...] = total(held[at_bit(1 - bit, rows), :], got[at_bit(1 - bit, rows), :])


def add_body(bit, held, got, out):
    out[...] = total(held[...], got[...])


def merge_body(bit, cur, got, out):
    rows = cur.shape[0]
    out[at_bit(bit, rows), :] = cur[...]
    out[at_bit(1 - bit, rows), :] = got[...]


def gather_body(bit, cur, got, out):
    rows = cur.shape[0] - EDGE
    out[at_bit(bit, rows), :] = cur[:rows, :]
    out[at_bit(1 - bit, rows), :] = got[:rows, :]
    out[2 * rows :, :] = total(cur[rows:, :], got[rows:, :])


def pair_kernel(bodies, outs, *refs):
    n = len(bodies)
    bits, arrays, results = refs[:n], refs[n : 3 * n], refs[3 * n + 1 :]
    for i, body in enumerate(bodies):
        count = outs[i]
        body(bits[i][0], arrays[2 * i], arrays[2 * i + 1], *results[:count])
        results = results[count:]


def pair_call(works, after, cost):
    outs = [len(w[4]) for w in works]
    shapes = [x for w in works for x in w[4]]
    return pl.pallas_call(
        functools.partial(pair_kernel, [w[0] for w in works], outs),
        in_specs=[IN_SMEM] * len(works) + [IN_VMEM] * (2 * len(works)) + [ANYWHERE],
        out_specs=[IN_VMEM] * len(shapes),
        out_shape=shapes,
        compiler_params=pltpu.CompilerParams(vmem_limit_bytes=24 * 1024 * 1024),
        cost_estimate=cost,
        name=works[0][0].__name__,
    )(*[w[1] for w in works], *[x for w in works for x in w[2:4]], after)


def first_kernel(bit_ref, held, got, after_ref, keep, give, bufs, sems):
    rows = keep.shape[0]
    bit = bit_ref[0]
    copies = []
    for i, half in enumerate((1 - bit, bit)):
        for j, array in enumerate((held, got)):
            copies.append(
                pltpu.make_async_copy(
                    array.at[at_bit(half, rows), :], bufs.at[2 * i + j], sems.at[2 * i + j]
                )
            )
    for copy in copies:
        copy.start()
    for i, out in enumerate((give, keep)):
        copies[2 * i].wait()
        copies[2 * i + 1].wait()
        out[...] = total(bufs[2 * i], bufs[2 * i + 1])


def split_first(held, got, bit, after, cost):
    rows, width = held.shape[0] // 2, held.shape[1]
    return pl.pallas_call(
        first_kernel,
        in_specs=[IN_SMEM, ANYWHERE, ANYWHERE, ANYWHERE],
        out_specs=[IN_VMEM] * 2,
        out_shape=[struct(rows, width)] * 2,
        scratch_shapes=[pltpu.VMEM((4, rows, width), BF16), pltpu.SemaphoreType.DMA((4,))],
        compiler_params=pltpu.CompilerParams(vmem_limit_bytes=24 * 1024 * 1024),
        cost_estimate=cost,
        name="split_first",
    )(bit, held, got, after)


def then_kernel(x_ref, after_ref, out_ref):
    out_ref[...] = x_ref[...]


def then(x, after):
    return pl.pallas_call(
        then_kernel,
        in_specs=[IN_VMEM, ANYWHERE],
        out_specs=IN_VMEM,
        out_shape=jax.ShapeDtypeStruct(x.shape, x.dtype),
        compiler_params=pltpu.CompilerParams(vmem_limit_bytes=16 * 1024 * 1024),
        cost_estimate=SMALL,
        name="then",
    )(x, after)


def join_kernel(count, sec_ref, *refs):
    section = sec_ref[0]
    arrays, outs = refs[: 2 * count], refs[2 * count + 1 : 3 * count + 1]
    mark, sems = refs[-2:]
    mark[...] = jnp.zeros_like(mark)
    copies = []
    for i in range(count):
        rows = arrays[2 * i].shape[0]
        for j, place in enumerate((section, 1 - section)):
            copies.append(
                pltpu.make_async_copy(
                    arrays[2 * i + j], outs[i].at[at_bit(place, rows), :], sems.at[2 * i + j]
                )
            )
    for copy in copies:
        copy.start()
    for copy in copies:
        copy.wait()


def join(sec, after, *pairs):
    rows, width = pairs[0][0].shape
    count = len(pairs)
    return pl.pallas_call(
        functools.partial(join_kernel, count),
        in_specs=[IN_SMEM] + [IN_VMEM] * (2 * count) + [ANYWHERE],
        out_specs=[IN_HBM] * count + [IN_VMEM],
        out_shape=[struct(2 * rows, width)] * count + [struct(8, 128, F32)],
        scratch_shapes=[pltpu.SemaphoreType.DMA((2 * count,))],
        compiler_params=pltpu.CompilerParams(vmem_limit_bytes=16 * 1024 * 1024),
        cost_estimate=SMALL,
        name="join",
    )(sec, *[x for pair in pairs for x in pair], after)


def swap(x):
    return lax.ppermute(x, "section", [(0, 1), (1, 0)])


class Sum:
    def __init__(self, orders):
        self.chips = lax.axis_size("dp")
        self.section = lax.axis_index("section")
        self.chip = lax.axis_index("dp")
        self.orders = orders
        self.levels = len(orders[0])

    def bit_of(self, step, section):
        where = jnp.where(section == 0, self.orders[0][step], self.orders[1][step])
        return ((self.chip >> where) & 1).astype(jnp.int32)

    def bit(self, step):
        return self.bit_of(step, self.section).reshape(1)

    def send(self, x, step):
        chips = self.chips
        route = [
            (s * chips + d, s * chips + (d ^ (1 << self.orders[s][step])))
            for s in range(2)
            for d in range(chips)
        ]
        return lax.ppermute(x, ("section", "dp"), route)

    def runs(self):
        mine, theirs = self.section, 1 - self.section
        own, other = self.bit_of(0, mine), self.bit_of(0, theirs)
        return jnp.stack(
            [2 * mine + own, 2 * mine + 1 - own, 2 * theirs + other, 2 * theirs + 1 - other]
        ).astype(jnp.int32)


class Batch:
    def __init__(self, sums, keep, give):
        self.sums = sums
        self.held = keep
        self.got = swap(give)
        self.step = 0

    def turn(self, after, more=(), cost=LARGE):
        sums, last = self.sums, self.sums.levels - 1
        at = self.step
        self.step += 1
        rows, width = self.held.shape
        if at == 0:
            self.held, give = split_first(self.held, self.got, sums.bit(0), after, cost)
            self.got, rest = sums.send(give, 0), []
        elif at < last:
            work = (split_body, sums.bit(at), self.held, self.got, [struct(rows // 2, width)] * 2)
            self.held, give, *rest = pair_call([work, *more], after, cost)
            self.got = sums.send(give, at)
        elif at <= last + 1:
            work = (add_body, sums.bit(0), self.held, self.got, [struct(rows, width)])
            self.held, *rest = pair_call([work, *more], after, cost)
            self.got = sums.send(self.held, at if at == last else last - 1)
        else:
            back = 2 * last + 1 - at
            work = (merge_body, sums.bit(back), self.held, self.got, [struct(2 * rows, width)])
            self.held, *rest = pair_call([work, *more], after, cost)
            self.got = sums.send(self.held, back - 1)
        return (self.held, *rest)

    @property
    def turns(self):
        return 2 * self.sums.levels - 1

    def early(self, shapes, spots, after, outs=()):
        return place(self.sums.runs(), (0, 2), (self.held, swap(self.held)), shapes, spots, after, outs)

    def arrive(self, after):
        self.got = then(self.got, after)
        self.last = swap(self.got)
        return self.got

    def late(self, shapes, spots, after, outs):
        return place(self.sums.runs(), (1, 3), (self.got, self.last), shapes, spots, after, outs)


def place_kernel(which, spots, count, runs, p0, p1, after_ref, *refs):
    outs, (mark, buf, sems) = refs[-3 - count : -3], refs[-3:]
    mark[...] = jnp.zeros_like(mark)
    rows = buf.shape[1]
    per_run = p0.shape[0] // rows
    for wait in (False, True):
        for run in range(4):
            mine, theirs = runs[which[0]] == run, runs[which[1]] == run
            base = run * per_run

            @pl.when(mine | theirs)
            def _(run=run, mine=mine):
                slot = jnp.where(mine, 0, 1)
                for w in range(run * per_run, (run + 1) * per_run):
                    spot = spots[w]
                    if spot is None:
                        continue
                    j = w - base
                    k, row, col = spot
                    copy = pltpu.make_async_copy(
                        buf.at[slot * per_run + j],
                        outs[k].at[pl.ds(row, rows), pl.ds(col, buf.shape[2])],
                        sems.at[slot * per_run + j],
                    )
                    if wait:
                        copy.wait()
                    else:
                        part = slice(j * rows, (j + 1) * rows)
                        value = jnp.where(mine, p0[part, :], p1[part, :])
                        buf[slot * per_run + j] = value.astype(F32)
                        copy.start()


def spots_of(targets, width):
    quarter = width // 4
    spots = []
    for section in range(2):
        for k, row, col in targets:
            for u in range(2):
                spots.append((k, row + (2 * section + u) * quarter, col))
    return spots


def place(runs, which, pieces, shapes, spots, after, outs=()):
    length, width = pieces[0].shape
    quarter = width // 4
    per_run = length // quarter
    half = len(spots) // 2
    full = [None] * (4 * per_run)
    full[:half] = spots[:half]
    full[2 * per_run : 2 * per_run + half] = spots[half:]
    return pl.pallas_call(
        functools.partial(place_kernel, which, full, len(shapes)),
        in_specs=[IN_SMEM] + [IN_VMEM] * 2 + [ANYWHERE] + [IN_HBM] * len(outs),
        out_specs=[IN_HBM] * len(shapes) + [IN_VMEM],
        out_shape=list(shapes) + [struct(8, 128, F32)],
        input_output_aliases={4 + k: k for k in range(len(outs))},
        scratch_shapes=[
            pltpu.VMEM((2 * per_run, quarter, width), F32),
            pltpu.SemaphoreType.DMA((2 * per_run,)),
        ],
        compiler_params=pltpu.CompilerParams(vmem_limit_bytes=24 * 1024 * 1024),
        cost_estimate=SMALL,
        name="place",
    )(runs, *pieces, after, *outs)


def step_kernel(items, group, rows_ref, after_ref, out_ref, o_low, o_res, o_out, o_levels, mark):
    mark[...] = jnp.zeros_like(mark)
    width = rows_ref.shape[1]
    half = width // 2
    rows = rows_ref[: rows_ref.shape[0] - EDGE, :].astype(F32).reshape(-1, group, width)
    lanes = (rows.shape[0], group, 128)
    index = 32.0 * rows[:, items : items + 1, :128] + rows[:, items + 1 : items + 2, :128]
    diagonal = lax.broadcasted_iota(jnp.int32, lanes, 1) == lax.broadcasted_iota(
        jnp.int32, lanes, 2
    )
    index = jnp.sum(jnp.where(diagonal, index, 0.0), axis=2, keepdims=True)
    index = index.reshape(-1, 1)
    lane = lax.broadcasted_iota(jnp.int32, (index.shape[0], half), 1).astype(F32)
    angle = index * jnp.exp(lane * F32(-math.log(10000.0) / half))
    emb = jnp.concatenate([jnp.sin(angle), jnp.cos(angle)], axis=1)
    used = lax.broadcasted_iota(jnp.int32, rows.shape, 1) < items
    sums = jnp.where(used, rows, 0.0).reshape(-1, width)
    out_ref[...] = tn(emb.astype(BF16), sums.astype(BF16))
    vec = rows_ref[rows_ref.shape[0] - EDGE :, :].astype(F32)
    for i, out in enumerate((o_low, o_res, o_out)):
        out[:, :width] = vec[2 * i : 2 * i + 1, :]
        out[:, width:] = vec[2 * i + 1 : 2 * i + 2, :]
    digit = lax.broadcasted_iota(jnp.int32, (1, width), 1)
    weight = jnp.where(digit < 8, 1 << (3 * jnp.minimum(digit, 8)), 0).astype(F32)
    frames = jnp.sum(vec[9:10, :] * weight, axis=1, keepdims=True) * width
    sizes = jnp.sum(vec[6:9, :], axis=1, keepdims=True)
    o_levels[...] = jnp.broadcast_to(jnp.sqrt(sizes / frames), o_levels.shape)


def padded(x, rows):
    return x if x.shape[0] == rows else jnp.pad(x, ((0, rows - x.shape[0]), (0, 0)))


def on_device(
    input_rows,
    conditioning,
    prompt,
    buckets,
    item_len,
    step_index,
    output_gradient,
    grad_skip,
    step_w,
    conv_w,
    cond_w,
    conv_b,
    res_w,
    res_b,
    query_w,
    key_w,
    value_w,
    out_w,
    out_b,
):
    section = lax.axis_index("section")
    sec = section.astype(jnp.int32).reshape(1)
    total, width = input_rows.shape
    micro, slots = item_len.shape
    nq = prompt.shape[2]
    frames = total // micro
    tile = frames // slots
    own = total // 2
    tiles = own // tile
    subs = 2
    size = subs * tile
    grid = tiles // subs
    mb_own = -(-own // frames)
    items = mb_own * slots
    half = width // 2
    taps = conv_w.shape[0]
    per = size // EDGE
    last = total // EDGE - 1
    wide = 2 * width
    conv_flat = conv_w.reshape(taps * width, wide)
    flat_prompt = prompt.reshape(-1, width)

    def whole(x):
        n = x.ndim
        return pl.BlockSpec(x.shape, lambda t, *_: (0,) * n, pipeline_mode=pl.Buffered(1))

    smem = pl.BlockSpec(memory_space=pltpu.SMEM)

    def chip_tile(cols):
        return pl.BlockSpec((size, cols), lambda t, s, *_: (s[0] * grid + t, 0))

    def own_tile(cols):
        return pl.BlockSpec((size, cols), lambda t, *_: (t, 0))

    def const(shape):
        return pl.BlockSpec(shape, lambda t, *_: (0,) * len(shape))

    prev_chip = pl.BlockSpec(
        (EDGE, width), lambda t, s, *_: (jnp.maximum((s[0] * grid + t) * per - 1, 0), 0)
    )
    next_chip = pl.BlockSpec(
        (EDGE, width), lambda t, s, *_: (jnp.minimum((s[0] * grid + t + 1) * per, last), 0)
    )
    vectors = [x.reshape(1, -1) for x in (conv_b, res_b, out_b)]
    weights = [
        step_w,
        conv_flat,
        cond_w,
        vectors[0],
        res_w,
        vectors[1],
        query_w,
        key_w,
        value_w,
        out_w,
        vectors[2],
    ]

    def shape(*dims, dtype=BF16):
        return jax.ShapeDtypeStruct(dims, dtype)

    def blocks_of(n):
        return const((n, half, width)), shape(n, half, width)

    film_spec, film_shape = blocks_of(5)
    side_spec, side_shape = blocks_of(4)[0], shape(6, half, width)
    (
        stack,
        d_pre,
        edge,
        d_sent,
        block_keep,
        block_give,
        skip_keep,
        skip_give,
        keep_a,
        give_a,
        keep_c,
        give_c,
        vec,
    ) = pl.pallas_call(
        functools.partial(forward_kernel, (tile, slots, nq, subs, tiles, mb_own, micro)),
        grid_spec=pltpu.PrefetchScalarGridSpec(
            num_scalar_prefetch=1,
            grid=(grid,),
            in_specs=[smem, smem, smem, prev_chip, chip_tile(width), next_chip]
            + [chip_tile(width)] * 3
            + [whole(flat_prompt)]
            + [whole(w) for w in weights],
            out_specs=[own_tile(taps * width), own_tile(wide), const((2 * EDGE, wide))]
            + [own_tile(width)]
            + [own_tile(half)] * 4
            + [film_spec, film_spec, side_spec, side_spec, const((16, width))],
            scratch_shapes=[
                pltpu.VMEM((items, width), F32),
                pltpu.VMEM((items * nq, width), BF16),
                pltpu.VMEM((items * nq, width), BF16),
                pltpu.VMEM((items * nq, width), F32),
                pltpu.VMEM((items * nq, width), F32),
                pltpu.VMEM((width, wide), F32),
                pltpu.VMEM((width, width), F32),
                pltpu.VMEM((3, 8, wide), F32),
                pltpu.VMEM((3, 8, width), F32),
                pltpu.SMEM((1,), jnp.int32),
                pltpu.VMEM((wide, width), BF16),
                pltpu.VMEM((width, width), BF16),
                pltpu.VMEM((wide, width), BF16),
                pltpu.VMEM((width, wide), F32),
                pltpu.VMEM((width, wide), F32),
                pltpu.VMEM((HEADS * nq, width), BF16),
            ],
        ),
        out_shape=[
            shape(own, taps * width),
            shape(own, wide),
            shape(2 * EDGE, wide),
            shape(own, width),
            shape(own, half),
            shape(own, half),
            shape(own, half),
            shape(own, half),
            film_shape,
            film_shape,
            side_shape,
            side_shape,
            shape(16, width, dtype=F32),
        ],
        compiler_params=pltpu.CompilerParams(vmem_limit_bytes=VMEM),
        cost_estimate=LARGE,
        name="forward",
    )(
        sec,
        buckets,
        item_len,
        step_index,
        input_rows,
        input_rows,
        input_rows,
        conditioning,
        output_gradient,
        grad_skip,
        flat_prompt,
        *weights,
    )

    bits = list(range(lax.axis_size("dp").bit_length() - 1))
    other = [bits[1], bits[0]] + bits[2:]
    if len(other) > 3:
        other[-2], other[-1] = other[-1], other[-2]
    sums = Sum((bits, other))
    far_first = Sum((bits[2:] + bits[:2], bits[:1:-1] + bits[1::-1]))
    unit = 16 * lax.axis_size("dp") // 2

    def batch(keep, give, sums):
        rows = keep.shape[0] * half
        rows = -(-rows // unit) * unit
        return Batch(
            sums, padded(keep.reshape(-1, width), rows), padded(give.reshape(-1, width), rows)
        )

    def tap_grads(first, end, blocks, at, after, outs=()):
        spec = pl.BlockSpec((2, half, width), lambda i, *_: (at + i, 0, 0))
        return pl.pallas_call(
            weight_kernel,
            grid_spec=pltpu.PrefetchScalarGridSpec(
                num_scalar_prefetch=1,
                grid=(end - first,),
                in_specs=[pl.BlockSpec((own, width), lambda i, *_: (0, first + i)), whole(d_pre)]
                + [ANYWHERE] * (1 + len(outs)),
                out_specs=[spec, spec],
                scratch_shapes=[pltpu.VMEM((width, wide), F32)],
            ),
            out_shape=[shape(blocks, half, width)] * 2,
            input_output_aliases={4 + k: k for k in range(len(outs))},
            compiler_params=pltpu.CompilerParams(vmem_limit_bytes=KB_VMEM),
            cost_estimate=LARGE,
            name="weights",
        )(sec, stack, d_pre, after, *outs)

    batch_a = batch(keep_a, give_a, far_first)
    block_got, skip_got, other_edge = swap(block_give), swap(skip_give), swap(edge)
    keep_c, give_c = tap_grads(0, 1, 6, 2, vec, (keep_c, give_c))
    batch_c = batch(keep_c, give_c, sums)
    (after,) = batch_a.turn(keep_c)
    (after,) = batch_c.turn(after)
    keep_b, give_b = tap_grads(1, taps, 2 * (taps - 1), 0, after)
    batch_b = batch(keep_b, give_b, sums)

    group = -(-(micro * slots + 2) // 16) * 16
    rows_last = own // EDGE - 1
    in_keep, in_give, rows_now = pl.pallas_call(
        functools.partial(back_kernel, (tile, slots, subs, tiles, micro)),
        grid_spec=pltpu.PrefetchScalarGridSpec(
            num_scalar_prefetch=1,
            grid=(grid,),
            in_specs=[
                smem,
                smem,
                pl.BlockSpec((EDGE, wide), lambda t, *_: (jnp.maximum(t * per - 1, 0), 0)),
                own_tile(wide),
                pl.BlockSpec(
                    (EDGE, wide), lambda t, *_: (jnp.minimum((t + 1) * per, rows_last), 0)
                ),
                whole(other_edge),
                own_tile(width),
                whole(conv_flat),
                smem,
                whole(vec),
                ANYWHERE,
            ],
            out_specs=[own_tile(half), own_tile(half), const((group + EDGE, width))],
            scratch_shapes=[pltpu.VMEM((group, width), F32)],
        ),
        out_shape=[shape(own, half), shape(own, half), shape(group + EDGE, width)],
        compiler_params=pltpu.CompilerParams(vmem_limit_bytes=KC_VMEM),
        cost_estimate=SMALL,
        name="back",
    )(
        sec,
        buckets,
        item_len,
        d_pre,
        d_pre,
        d_pre,
        other_edge,
        d_sent,
        conv_flat,
        step_index,
        vec,
        keep_b,
    )
    in_got = swap(in_give)

    block_out, skip_out, after = join(
        sec, rows_now, (block_keep, block_got), (skip_keep, skip_got)
    )
    rows_got, rows_bit, gathered = swap(rows_now), sec, 0
    batches = {"a": batch_a, "b": batch_b, "c": batch_c}
    order = "cab" * (batch_a.turns - 1) + "b"
    for name in order:
        turner = batches[name]
        if name == "b" and turner.step and gathered <= sums.levels:
            n = rows_now.shape[0]
            work = (add_body, rows_bit, rows_now, rows_got, [struct(n, width)])
            if gathered:
                work = (gather_body, rows_bit, rows_now, rows_got, [struct(2 * n - EDGE, width)])
            after, rows_now = turner.turn(after, [work])
            if gathered < sums.levels:
                at = sums.levels - 1 - gathered
                route = [(d, d ^ (1 << at)) for d in range(sums.chips)]
                rows_got = lax.ppermute(rows_now, "dp", route)
                rows_bit = ((sums.chip >> at) & 1).astype(jnp.int32).reshape(1)
            gathered += 1
        else:
            (after,) = turner.turn(after)

    line = struct(1, wide, F32)
    g_step, g_convb, g_resb, g_outb, levels, mark = pl.pallas_call(
        functools.partial(step_kernel, micro * slots, group),
        in_specs=[IN_VMEM, ANYWHERE],
        out_specs=[IN_VMEM] * 6,
        out_shape=[struct(width, width, F32), line, line, line]
        + [struct(3, 128, F32), struct(8, 128, F32)],
        compiler_params=pltpu.CompilerParams(vmem_limit_bytes=24 * 1024 * 1024),
        cost_estimate=LARGE,
        name="step_grad",
    )(rows_now, after)
    in_grad, mark = join(sec, mark, (in_keep, in_got))

    def pairs(k, count, base=0):
        return [(k, base + i * width, col) for i in range(count) for col in (0, width)]

    square, tall = struct(width, width, F32), struct(width, wide, F32)
    shapes_a = [tall, square, square, square]
    spots_a = spots_of(pairs(0, 1) + [(k, 0, 0) for k in (1, 2, 3)], width)
    conv = struct(taps * width, wide, F32)
    shapes_c, spots_c = [tall, tall, conv], spots_of(pairs(0, 1) + pairs(1, 1) + pairs(2, 1), width)
    shapes_b, spots_b = [conv], spots_of(pairs(0, taps - 1, width), width)
    *outs_a, mark = batch_a.early(shapes_a, spots_a, mark)
    *outs_c, mark = batch_c.early(shapes_c, spots_c, mark)
    outs_c[2], mark = batch_b.early(shapes_b, spots_b, mark, outs_c[2:])
    mark = batch_a.arrive(mark)
    mark = batch_c.arrive(mark)
    mark = batch_b.arrive(mark)
    *outs_a, mark = batch_a.late(shapes_a, spots_a, mark, outs_a)
    *outs_c, mark = batch_c.late(shapes_c, spots_c, mark, outs_c)
    outs_c[2], mark = batch_b.late(shapes_b, spots_b, mark, outs_c[2:])
    g_out, g_query, g_key, g_value = outs_a
    g_res, g_cond, g_conv = outs_c
    g_conv = g_conv.reshape(conv_w.shape)
    g_convb, g_resb, g_outb = (x.reshape(wide) for x in (g_convb, g_resb, g_outb))
    levels = levels[:, 0]
    return (
        block_out,
        skip_out,
        in_grad,
        g_step,
        g_conv,
        g_cond,
        g_convb,
        g_res,
        g_resb,
        g_query,
        g_key,
        g_value,
        g_out,
        g_outb,
        levels,
    )


def solution(mesh):
    rows = P("dp", None)
    split = P("dp", "section")
    return jax.shard_map(
        on_device,
        mesh=mesh,
        in_specs=(rows, rows, P("dp", None, None, None), P("dp"), rows, rows, rows, rows)
        + (P(),) * 11,
        out_specs=(split,) * 3 + (P(),) * 12,
        check_vma=False,
    )
```

```python
import functools
import math

import jax
import jax.numpy as jnp
from jax import lax
from jax.experimental import pallas as pl
from jax.experimental.pallas import tpu as pltpu
from jax.sharding import PartitionSpec as P

HEADS = 8
SHIFT = 2
EDGE = 16
ISQ2 = 0.7071067811865476
F32 = jnp.float32
BF16 = jnp.bfloat16
VMEM = 56 * 1024 * 1024
KB_VMEM = 56 * 1024 * 1024
KC_VMEM = 32 * 1024 * 1024


def nn(a, b):
    return lax.dot_general(a, b, (((1,), (0,)), ((), ())), preferred_element_type=F32)


def nt(a, b):
    return lax.dot_general(a, b, (((1,), (1,)), ((), ())), preferred_element_type=F32)


def tn(a, b):
    return lax.dot_general(a, b, (((0,), (0,)), ((), ())), preferred_element_type=F32)


def rows_iota(rows, cols):
    return lax.broadcasted_iota(jnp.int32, (rows, cols), 0)


def col_sums(x):
    rows, cols = x.shape
    return jnp.sum(x.reshape(rows // 8, 8, cols), axis=0)


def plan(g, tile, slots, buckets, item_len):
    mb = g // slots
    q = g - mb * slots
    span = slots >> buckets[mb]
    slot = q // span
    off = q - slot * span
    lim = item_len[mb, slot] - off * tile
    return mb, slot, lim, off > 0, off < span - 1


def forward_kernel(
    cfg,
    sec_ref,
    buckets,
    item_len,
    steps,
    prev_ref,
    rows_ref,
    next_ref,
    cond_ref,
    gout_ref,
    gskip_ref,
    prompt_ref,
    step_w,
    conv_w,
    cond_w,
    conv_b,
    res_w,
    res_b,
    query_w,
    key_w,
    value_w,
    out_w,
    out_b,
    o_stack,
    o_dpre,
    o_edge,
    o_dsent,
    o_block_keep,
    o_block_give,
    o_skip_keep,
    o_skip_give,
    o_keep,
    o_give,
    o_keep_c,
    o_give_c,
    o_vec,
    proj,
    keys,
    values,
    d_keys,
    d_values,
    g_out,
    g_query,
    sums,
    stats,
    count,
    out_t,
    query_t,
    res_t,
    g_res,
    g_cond,
    own_head,
):
    tile, slots, nq, subs, tiles, mb_own, micro = cfg
    t = pl.program_id(0)
    section = sec_ref[0]
    size = subs * tile
    width = rows_ref.shape[1]
    half = width // 2
    head = width // HEADS
    mb0 = section * (micro - mb_own)
    items = mb_own * slots
    keep_left = section == 0

    @pl.when(t == 0)
    def _():
        row = rows_iota(items, half)
        when = jnp.zeros((items, half), F32)
        for i in range(items):
            s = steps[mb0 + i // slots, i % slots].astype(F32)
            when = jnp.where(row == i, s, when)
        lane = lax.broadcasted_iota(jnp.int32, (items, half), 1).astype(F32)
        angle = when * jnp.exp(lane * F32(-math.log(10000.0) / half))
        emb = jnp.concatenate([jnp.sin(angle), jnp.cos(angle)], axis=1)
        proj[...] = nn(emb.astype(BF16), step_w[...])
        here = prompt_ref[pl.ds(pl.multiple_of(mb0 * slots * nq, 16), items * nq), :]
        factor = head ** (-0.5)
        keys[...] = (nn(here, key_w[...]).astype(BF16) * BF16(factor)).astype(BF16)
        values[...] = nn(here, value_w[...]).astype(BF16)
        d_keys[...] = jnp.zeros_like(d_keys)
        d_values[...] = jnp.zeros_like(d_values)
        g_out[...] = jnp.zeros_like(g_out)
        out_t[...] = out_w[...].T
        query_t[...] = query_w[...].T
        res_t[...] = res_w[...].T
        g_res[...] = jnp.zeros_like(g_res)
        g_cond[...] = jnp.zeros_like(g_cond)
        at_row = rows_iota(HEADS * nq, width) // nq
        at_lane = lax.broadcasted_iota(jnp.int32, (HEADS * nq, width), 1) // head
        own_head[...] = jnp.where(at_row == at_lane, 1.0, 0.0).astype(BF16)
        g_query[...] = jnp.zeros_like(g_query)
        sums[...] = jnp.zeros_like(sums)
        stats[...] = jnp.zeros_like(stats)
        count[0] = 0

    ext = jnp.concatenate([prev_ref[...], rows_ref[...], next_ref[...]], axis=0)
    spread = tile + 2 * EDGE
    place = rows_iota(spread, 128)

    def lanes(mask):
        return jnp.concatenate([mask] * (width // 128), axis=1)

    mixed, behind, ahead, at = [], [], [], []
    valid = []
    row = rows_iota(tile, 128)
    for k in range(subs):
        mb, slot, lim, prev_in, next_in = plan(
            section * tiles + t * subs + k, tile, slots, buckets, item_len
        )
        item = (mb - mb0) * slots + slot
        at.append(pl.multiple_of(item * nq, nq))
        lo = jnp.where(prev_in, 0, EDGE)
        hi = jnp.where(next_in, tile + 2 * EDGE, tile + EDGE)
        hi = jnp.minimum(hi, lim + EDGE)
        part = ext[k * tile : k * tile + spread].astype(F32) + proj[pl.ds(item, 1), :]
        part = part * lanes(jnp.where((place >= lo) & (place < hi), 1.0, 0.0))
        mixed.append(part[EDGE : EDGE + tile])
        behind.append(pltpu.roll(part, SHIFT, 0)[EDGE : EDGE + tile].astype(BF16))
        ahead.append(pltpu.roll(part, spread - SHIFT, 0)[EDGE : EDGE + tile].astype(BF16))
        valid.append(jnp.where(row < lim, 1.0, 0.0))
        count[0] += jnp.clip(lim, 0, tile)
    mixed = jnp.concatenate(mixed, axis=0)
    valid = lanes(jnp.concatenate(valid, axis=0))
    stacked = jnp.concatenate(
        [jnp.concatenate(behind, axis=0), mixed.astype(BF16), jnp.concatenate(ahead, axis=0)],
        axis=1,
    )
    o_stack[...] = stacked
    pre = nn(stacked, conv_w[...]) + nn(cond_ref[...], cond_w[...]) + conv_b[...]
    a = jnp.tanh(pre[:, :width])
    s = 0.5 * jnp.tanh(0.5 * pre[:, width:]) + 0.5
    both = a * s
    gate = both.astype(BF16)
    slope_a = s - both * a
    slope_s = both - both * s
    branch = nn(gate, res_w[...]) + res_b[...]
    res_part = branch[:, :width] * valid
    skip = (branch[:, width:] * valid).astype(BF16)
    o_skip_keep[...] = jnp.where(keep_left, skip[:, :half], skip[:, half:])
    o_skip_give[...] = jnp.where(keep_left, skip[:, half:], skip[:, :half])
    hidden = (mixed + res_part) * ISQ2
    sent = hidden.astype(BF16)
    sent_f = sent.astype(F32)
    stats[0] += col_sums(hidden * hidden)
    stats[1] += col_sums(res_part * res_part)

    query = nn(sent, query_w[...]).astype(BF16)
    mask = own_head[...]
    probs, probs_low, key_bd, value_bd, attended = [], [], [], [], []
    for k in range(subs):
        key_bd.append(jnp.concatenate([keys[pl.ds(at[k], nq), :]] * HEADS, axis=0) * mask)
        value_bd.append(jnp.concatenate([values[pl.ds(at[k], nq), :]] * HEADS, axis=0) * mask)
        scores = nt(key_bd[k], query[k * tile : (k + 1) * tile]).reshape(HEADS, nq, tile)
        expo = jnp.exp(scores - jnp.max(scores, axis=1, keepdims=True))
        probs.append(expo * (1.0 / jnp.sum(expo, axis=1, keepdims=True)))
        probs_low.append(probs[k].astype(BF16).reshape(HEADS * nq, tile))
        attended.append(tn(probs_low[k], value_bd[k]).astype(BF16))
    attended = jnp.concatenate(attended, axis=0)
    film = nn(attended, out_w[...]) + out_b[...]
    scale = film[:, :width]
    change = (sent_f * scale + film[:, width:]) * valid
    block = (sent_f + change).astype(BF16)
    o_block_keep[...] = jnp.where(keep_left, block[:, :half], block[:, half:])
    o_block_give[...] = jnp.where(keep_left, block[:, half:], block[:, :half])
    stats[2] += col_sums(change * change)

    gy = gout_ref[...].astype(F32) * valid
    d_film = jnp.concatenate([(gy * sent_f).astype(BF16), gy.astype(BF16)], axis=1)
    sums[2] += col_sums(d_film.astype(F32))
    g_out[...] += tn(attended, d_film)
    d_att = nn(d_film, out_t[...]).astype(BF16)
    low_lane = lax.broadcasted_iota(jnp.int32, (nq, 2 * head), 1) < head

    def own_heads(x):
        pieces = []
        for p in range(HEADS // 2):
            at_row, at_lane = 2 * p * nq, 2 * p * head
            first = x[at_row : at_row + nq, at_lane : at_lane + 2 * head]
            second = x[at_row + nq : at_row + 2 * nq, at_lane : at_lane + 2 * head]
            pieces.append(jnp.where(low_lane, first, second))
        return jnp.concatenate(pieces, axis=1)

    d_query = []
    for k in range(subs):
        here = slice(k * tile, (k + 1) * tile)
        d_probs = nt(value_bd[k], d_att[here]).reshape(HEADS, nq, tile)
        weighted = probs[k] * d_probs
        inner = jnp.sum(weighted, axis=1, keepdims=True)
        d_scores = (weighted - probs[k] * inner).astype(BF16).reshape(HEADS * nq, tile)
        d_values[pl.ds(at[k], nq), :] += own_heads(nn(probs_low[k], d_att[here]))
        d_keys[pl.ds(at[k], nq), :] += own_heads(nn(d_scores, query[here]))
        d_query.append(tn(d_scores, key_bd[k]).astype(BF16))
    d_query = jnp.concatenate(d_query, axis=0)
    g_query[...] += tn(sent, d_query)
    d_sent = (gy * (1.0 + scale) + nn(d_query, query_t[...])).astype(BF16)
    o_dsent[...] = d_sent

    d_res = (d_sent.astype(F32) * ISQ2).astype(BF16)
    gs = (gskip_ref[...].astype(F32) * valid).astype(BF16)
    d_branch = jnp.concatenate([d_res, gs], axis=1)
    sums[1] += col_sums(d_branch.astype(F32))
    g_res[...] += tn(gate, d_branch)
    d_gate = nn(d_branch, res_t[...])
    d_pre = jnp.concatenate(
        [(d_gate * slope_a).astype(BF16), (d_gate * slope_s).astype(BF16)], axis=1
    )
    sums[0] += col_sums(d_pre.astype(F32))
    o_dpre[...] = d_pre
    g_cond[...] += tn(cond_ref[...], d_pre)

    @pl.when(t == 0)
    def _():
        o_edge[:EDGE, :] = d_pre[:EDGE, :]

    @pl.when(t == tiles // subs - 1)
    def _():
        here = prompt_ref[pl.ds(pl.multiple_of(mb0 * slots * nq, 16), items * nq), :]
        factor = head ** (-0.5)
        mine = pl.multiple_of(section * half, half)
        theirs = pl.multiple_of(half - section * half, half)

        o_edge[EDGE:, :] = d_pre[size - EDGE :, :]

        def put(i, ref, left, keep=o_keep, give=o_give):
            keep[i] = ref[pl.ds(mine, half), pl.ds(left, width)].astype(BF16)
            give[i] = ref[pl.ds(theirs, half), pl.ds(left, width)].astype(BF16)

        put(0, g_out, 0)
        put(1, g_out, width)
        put(2, g_query, 0)
        g_query[...] = tn(here, (d_keys[...] * factor).astype(BF16))
        put(3, g_query, 0)
        g_query[...] = tn(here, d_values[...].astype(BF16))
        put(4, g_query, 0)
        put(0, g_res, 0, o_keep_c, o_give_c)
        put(1, g_res, width, o_keep_c, o_give_c)
        put(2, g_cond, 0, o_keep_c, o_give_c)
        put(3, g_cond, width, o_keep_c, o_give_c)
        for i in range(3):
            line = jnp.sum(sums[i], axis=0, keepdims=True)
            o_vec[2 * i : 2 * i + 1, :] = line[:, :width]
            o_vec[2 * i + 1 : 2 * i + 2, :] = line[:, width:]
        for i in range(3):
            o_vec[6 + i : 7 + i, :] = jnp.sum(stats[i], axis=0, keepdims=True)
        lane = lax.broadcasted_iota(jnp.int32, (16 - 9, width), 1)
        digits = (count[0] >> (3 * jnp.minimum(lane, 8))) & 7
        o_vec[9:16, :] = jnp.where(lane < 8, digits, 0).astype(F32)


def weight_kernel(sec_ref, left_ref, dpre_ref, o_keep, o_give, mark, acc):
    mark[...] = jnp.zeros_like(mark)
    section = sec_ref[0]
    width = acc.shape[0]
    half = width // 2
    acc[...] = tn(left_ref[...], dpre_ref[...])
    mine = pl.multiple_of(section * half, half)
    theirs = pl.multiple_of(half - section * half, half)
    for side in range(2):
        o_keep[side] = acc[pl.ds(mine, half), pl.ds(side * width, width)].astype(BF16)
        o_give[side] = acc[pl.ds(theirs, half), pl.ds(side * width, width)].astype(BF16)


def back_kernel(
    cfg,
    sec_ref,
    buckets,
    item_len,
    prev_ref,
    dpre_ref,
    next_ref,
    other_ref,
    dsent_ref,
    conv_w,
    steps,
    vec_ref,
    after_ref,
    o_keep,
    o_give,
    o_rows,
    d_step,
):
    tile, slots, subs, tiles, micro = cfg
    t = pl.program_id(0)
    section = sec_ref[0]
    width = dsent_ref.shape[1]
    half = width // 2
    count = tiles // subs

    @pl.when(t == 0)
    def _():
        d_step[...] = jnp.zeros_like(d_step)

    before = jnp.where(t == 0, other_ref[EDGE:, :], prev_ref[...])
    after = jnp.where(t == count - 1, other_ref[:EDGE, :], next_ref[...])
    ext = jnp.concatenate([before, dpre_ref[...], after], axis=0)
    spread = tile + 2 * EDGE
    place = rows_iota(spread, 128)
    row = rows_iota(tile, 128)
    ahead, behind, valid, item = [], [], [], []
    for k in range(subs):
        mb, slot, lim, prev_in, next_in = plan(
            section * tiles + t * subs + k, tile, slots, buckets, item_len
        )
        item.append(mb * slots + slot)
        lo = jnp.where(prev_in, 0, EDGE)
        hi = jnp.where(next_in, spread, tile + EDGE)
        here = jnp.where((place >= lo) & (place < hi), 1.0, 0.0)
        part = ext[k * tile : k * tile + spread].astype(F32)
        part = part * jnp.concatenate([here] * (2 * width // 128), axis=1)
        ahead.append(pltpu.roll(part, spread - SHIFT, 0)[EDGE : EDGE + tile].astype(BF16))
        behind.append(pltpu.roll(part, SHIFT, 0)[EDGE : EDGE + tile].astype(BF16))
        valid.append(jnp.where(row < lim, 1.0, 0.0))
    valid = jnp.concatenate([jnp.concatenate(valid, axis=0)] * (width // 128), axis=1)
    d_in = nt(jnp.concatenate(ahead, axis=0), conv_w[:width, :])
    d_in += nt(dpre_ref[...], conv_w[width : 2 * width, :])
    d_in += nt(jnp.concatenate(behind, axis=0), conv_w[2 * width :, :])
    d_mixed = (dsent_ref[...].astype(F32) * ISQ2 + d_in) * valid
    for k in range(subs):
        line = jnp.sum(col_sums(d_mixed[k * tile : (k + 1) * tile]), axis=0, keepdims=True)
        d_step[pl.ds(item[k], 1), :] += line
    low = d_mixed.astype(BF16)
    o_keep[...] = jnp.where(section == 0, low[:, :half], low[:, half:])
    o_give[...] = jnp.where(section == 0, low[:, half:], low[:, :half])

    @pl.when(t == count - 1)
    def _():
        items = micro * slots
        group = d_step.shape[0]
        lane = lax.broadcasted_iota(jnp.int32, (1, width), 1)
        index = jnp.zeros((1, width), jnp.int32)
        for i in range(items):
            index = jnp.where(lane == i, steps[i // slots, i % slots], index)
        index = jnp.where(section == 0, index, 0)
        d_step[items : items + 1, :] = (index >> 5).astype(F32)
        d_step[items + 1 : items + 2, :] = (index & 31).astype(F32)
        o_rows[:group, :] = d_step[...].astype(BF16)
        o_rows[group:, :] = vec_ref[...].astype(BF16)


SMALL = pl.CostEstimate(flops=1024, bytes_accessed=1024, transcendentals=0)
LARGE = pl.CostEstimate(flops=1 << 36, bytes_accessed=1024, transcendentals=0)
ANYWHERE = pl.BlockSpec(memory_space=pl.ANY)
PARAMS = pltpu.CompilerParams(vmem_limit_bytes=VMEM)


IN_VMEM = pl.BlockSpec(memory_space=pltpu.VMEM)
IN_SMEM = pl.BlockSpec(memory_space=pltpu.SMEM)
IN_HBM = pl.BlockSpec(memory_space=pltpu.HBM)


def struct(rows, width, dtype=BF16):
    return jax.ShapeDtypeStruct((rows, width), dtype)


def total(a, b):
    return (a.astype(F32) + b.astype(F32)).astype(BF16)


def at_bit(bit, rows):
    return pl.ds(pl.multiple_of(bit * rows, 16), rows)


def split_body(bit, held, got, keep, give):
    rows = keep.shape[0]
    keep[...] = total(held[at_bit(bit, rows), :], got[at_bit(bit, rows), :])
    give[...] = total(held[at_bit(1 - bit, rows), :], got[at_bit(1 - bit, rows), :])


def add_body(bit, held, got, out):
    out[...] = total(held[...], got[...])


def merge_body(bit, cur, got, out):
    rows = cur.shape[0]
    out[at_bit(bit, rows), :] = cur[...]
    out[at_bit(1 - bit, rows), :] = got[...]


def gather_body(bit, cur, got, out):
    rows = cur.shape[0] - EDGE
    out[at_bit(bit, rows), :] = cur[:rows, :]
    out[at_bit(1 - bit, rows), :] = got[:rows, :]
    out[2 * rows :, :] = total(cur[rows:, :], got[rows:, :])


def pair_kernel(bodies, outs, *refs):
    n = len(bodies)
    bits, arrays, results = refs[:n], refs[n : 3 * n], refs[3 * n + 1 :]
    for i, body in enumerate(bodies):
        count = outs[i]
        body(bits[i][0], arrays[2 * i], arrays[2 * i + 1], *results[:count])
        results = results[count:]


def pair_call(works, after, cost):
    outs = [len(w[4]) for w in works]
    shapes = [x for w in works for x in w[4]]
    return pl.pallas_call(
        functools.partial(pair_kernel, [w[0] for w in works], outs),
        in_specs=[IN_SMEM] * len(works) + [IN_VMEM] * (2 * len(works)) + [ANYWHERE],
        out_specs=[IN_VMEM] * len(shapes),
        out_shape=shapes,
        compiler_params=pltpu.CompilerParams(vmem_limit_bytes=24 * 1024 * 1024),
        cost_estimate=cost,
        name=works[0][0].__name__,
    )(*[w[1] for w in works], *[x for w in works for x in w[2:4]], after)


def first_kernel(bit_ref, held, got, after_ref, keep, give, mark, same, bufs, sems):
    mark[...] = jnp.zeros_like(mark)
    rows = keep.shape[0]
    bit = bit_ref[0]
    copies = []
    for i, half in enumerate((1 - bit, bit)):
        for j, array in enumerate((held, got)):
            copies.append(
                pltpu.make_async_copy(
                    array.at[at_bit(half, rows), :], bufs.at[2 * i + j], sems.at[2 * i + j]
                )
            )
    for copy in copies:
        copy.start()
    for i, out in enumerate((give, keep)):
        copies[2 * i].wait()
        copies[2 * i + 1].wait()
        out[...] = total(bufs[2 * i], bufs[2 * i + 1])


def split_first(held, got, bit, after, cost):
    rows, width = held.shape[0] // 2, held.shape[1]
    return pl.pallas_call(
        first_kernel,
        in_specs=[IN_SMEM, ANYWHERE, ANYWHERE, ANYWHERE],
        out_specs=[IN_VMEM] * 3 + [ANYWHERE],
        out_shape=[struct(rows, width)] * 2 + [struct(8, 128, F32), struct(2 * rows, width)],
        input_output_aliases={1: 3},
        scratch_shapes=[pltpu.VMEM((4, rows, width), BF16), pltpu.SemaphoreType.DMA((4,))],
        compiler_params=pltpu.CompilerParams(vmem_limit_bytes=24 * 1024 * 1024),
        cost_estimate=cost,
        name="split_first",
    )(bit, held, got, after)[:3]


def then_kernel(x_ref, after_ref, out_ref):
    out_ref[...] = x_ref[...]


def then(x, after):
    return pl.pallas_call(
        then_kernel,
        in_specs=[IN_VMEM, ANYWHERE],
        out_specs=IN_VMEM,
        out_shape=jax.ShapeDtypeStruct(x.shape, x.dtype),
        compiler_params=pltpu.CompilerParams(vmem_limit_bytes=16 * 1024 * 1024),
        cost_estimate=SMALL,
        name="then",
    )(x, after)


def join_kernel(count, sec_ref, *refs):
    section = sec_ref[0]
    arrays, outs = refs[: 2 * count], refs[2 * count + 1 : 3 * count + 1]
    mark, sems = refs[-2:]
    mark[...] = jnp.zeros_like(mark)
    copies = []
    for i in range(count):
        rows = arrays[2 * i].shape[0]
        for j, place in enumerate((section, 1 - section)):
            copies.append(
                pltpu.make_async_copy(
                    arrays[2 * i + j], outs[i].at[at_bit(place, rows), :], sems.at[2 * i + j]
                )
            )
    for copy in copies:
        copy.start()
    for copy in copies:
        copy.wait()


def join(sec, after, *pairs):
    rows, width = pairs[0][0].shape
    count = len(pairs)
    return pl.pallas_call(
        functools.partial(join_kernel, count),
        in_specs=[IN_SMEM] + [IN_VMEM] * (2 * count) + [ANYWHERE],
        out_specs=[IN_HBM] * count + [IN_VMEM],
        out_shape=[struct(2 * rows, width)] * count + [struct(8, 128, F32)],
        scratch_shapes=[pltpu.SemaphoreType.DMA((2 * count,))],
        compiler_params=pltpu.CompilerParams(vmem_limit_bytes=16 * 1024 * 1024),
        cost_estimate=SMALL,
        name="join",
    )(sec, *[x for pair in pairs for x in pair], after)


def swap(x):
    return lax.ppermute(x, "section", [(0, 1), (1, 0)])


class Sum:
    def __init__(self, orders):
        self.chips = lax.axis_size("dp")
        self.section = lax.axis_index("section")
        self.chip = lax.axis_index("dp")
        self.orders = orders
        self.levels = len(orders[0])

    def bit_of(self, step, section):
        where = jnp.where(section == 0, self.orders[0][step], self.orders[1][step])
        return ((self.chip >> where) & 1).astype(jnp.int32)

    def bit(self, step):
        return self.bit_of(step, self.section).reshape(1)

    def send(self, x, step):
        chips = self.chips
        route = [
            (s * chips + d, s * chips + (d ^ (1 << self.orders[s][step])))
            for s in range(2)
            for d in range(chips)
        ]
        return lax.ppermute(x, ("section", "dp"), route)

    def runs(self):
        mine, theirs = self.section, 1 - self.section
        own, other = self.bit_of(0, mine), self.bit_of(0, theirs)
        return jnp.stack(
            [2 * mine + own, 2 * mine + 1 - own, 2 * theirs + other, 2 * theirs + 1 - other]
        ).astype(jnp.int32)


class Batch:
    def __init__(self, sums, keep, give):
        self.sums = sums
        self.held = keep
        self.got = swap(give)
        self.step = 0

    def turn(self, after, more=(), cost=LARGE):
        sums, last = self.sums, self.sums.levels - 1
        at = self.step
        self.step += 1
        rows, width = self.held.shape
        if at == 0:
            self.held, give, mark = split_first(self.held, self.got, sums.bit(0), after, cost)
            self.got = sums.send(give, 0)
            return (mark,)
        elif at < last:
            work = (split_body, sums.bit(at), self.held, self.got, [struct(rows // 2, width)] * 2)
            self.held, give, *rest = pair_call([work, *more], after, cost)
            self.got = sums.send(give, at)
        elif at <= last + 1:
            work = (add_body, sums.bit(0), self.held, self.got, [struct(rows, width)])
            self.held, *rest = pair_call([work, *more], after, cost)
            self.got = sums.send(self.held, at if at == last else last - 1)
        else:
            back = 2 * last + 1 - at
            work = (merge_body, sums.bit(back), self.held, self.got, [struct(2 * rows, width)])
            self.held, *rest = pair_call([work, *more], after, cost)
            self.got = sums.send(self.held, back - 1)
        return (self.held, *rest)

    @property
    def turns(self):
        return 2 * self.sums.levels - 1

    def early(self, shapes, spots, after, outs=()):
        return place(self.sums.runs(), (0, 2), (self.held, swap(self.held)), shapes, spots, after, outs)

    def arrive(self, after):
        self.got = then(self.got, after)
        self.last = swap(self.got)
        return self.got

    def late(self, shapes, spots, after, outs):
        return place(self.sums.runs(), (1, 3), (self.got, self.last), shapes, spots, after, outs)


def place_kernel(which, spots, count, runs, p0, p1, after_ref, *refs):
    outs, (mark, buf, sems) = refs[-3 - count : -3], refs[-3:]
    mark[...] = jnp.zeros_like(mark)
    rows = buf.shape[1]
    per_run = p0.shape[0] // rows
    for wait in (False, True):
        for run in range(4):
            mine, theirs = runs[which[0]] == run, runs[which[1]] == run
            base = run * per_run

            @pl.when(mine | theirs)
            def _(run=run, mine=mine):
                slot = jnp.where(mine, 0, 1)
                for w in range(run * per_run, (run + 1) * per_run):
                    spot = spots[w]
                    if spot is None:
                        continue
                    j = w - base
                    k, row, col = spot
                    copy = pltpu.make_async_copy(
                        buf.at[slot * per_run + j],
                        outs[k].at[pl.ds(row, rows), pl.ds(col, buf.shape[2])],
                        sems.at[slot * per_run + j],
                    )
                    if wait:
                        copy.wait()
                    else:
                        part = slice(j * rows, (j + 1) * rows)
                        value = jnp.where(mine, p0[part, :], p1[part, :])
                        buf[slot * per_run + j] = value.astype(F32)
                        copy.start()


def spots_of(targets, width):
    quarter = width // 4
    spots = []
    for section in range(2):
        for k, row, col in targets:
            for u in range(2):
                spots.append((k, row + (2 * section + u) * quarter, col))
    return spots


def place(runs, which, pieces, shapes, spots, after, outs=()):
    length, width = pieces[0].shape
    quarter = width // 4
    per_run = length // quarter
    half = len(spots) // 2
    full = [None] * (4 * per_run)
    full[:half] = spots[:half]
    full[2 * per_run : 2 * per_run + half] = spots[half:]
    return pl.pallas_call(
        functools.partial(place_kernel, which, full, len(shapes)),
        in_specs=[IN_SMEM] + [IN_VMEM] * 2 + [ANYWHERE] + [IN_HBM] * len(outs),
        out_specs=[IN_HBM] * len(shapes) + [IN_VMEM],
        out_shape=list(shapes) + [struct(8, 128, F32)],
        input_output_aliases={4 + k: k for k in range(len(outs))},
        scratch_shapes=[
            pltpu.VMEM((2 * per_run, quarter, width), F32),
            pltpu.SemaphoreType.DMA((2 * per_run,)),
        ],
        compiler_params=pltpu.CompilerParams(vmem_limit_bytes=24 * 1024 * 1024),
        cost_estimate=SMALL,
        name="place",
    )(runs, *pieces, after, *outs)


def step_kernel(items, group, rows_ref, after_ref, out_ref, o_low, o_res, o_out, o_levels, mark):
    mark[...] = jnp.zeros_like(mark)
    width = rows_ref.shape[1]
    half = width // 2
    rows = rows_ref[: rows_ref.shape[0] - EDGE, :].astype(F32).reshape(-1, group, width)
    lanes = (rows.shape[0], group, 128)
    index = 32.0 * rows[:, items : items + 1, :128] + rows[:, items + 1 : items + 2, :128]
    diagonal = lax.broadcasted_iota(jnp.int32, lanes, 1) == lax.broadcasted_iota(
        jnp.int32, lanes, 2
    )
    index = jnp.sum(jnp.where(diagonal, index, 0.0), axis=2, keepdims=True)
    index = index.reshape(-1, 1)
    lane = lax.broadcasted_iota(jnp.int32, (index.shape[0], half), 1).astype(F32)
    angle = index * jnp.exp(lane * F32(-math.log(10000.0) / half))
    emb = jnp.concatenate([jnp.sin(angle), jnp.cos(angle)], axis=1)
    used = lax.broadcasted_iota(jnp.int32, rows.shape, 1) < items
    sums = jnp.where(used, rows, 0.0).reshape(-1, width)
    out_ref[...] = tn(emb.astype(BF16), sums.astype(BF16))
    vec = rows_ref[rows_ref.shape[0] - EDGE :, :].astype(F32)
    for i, out in enumerate((o_low, o_res, o_out)):
        out[:, :width] = vec[2 * i : 2 * i + 1, :]
        out[:, width:] = vec[2 * i + 1 : 2 * i + 2, :]
    digit = lax.broadcasted_iota(jnp.int32, (1, width), 1)
    weight = jnp.where(digit < 8, 1 << (3 * jnp.minimum(digit, 8)), 0).astype(F32)
    frames = jnp.sum(vec[9:10, :] * weight, axis=1, keepdims=True) * width
    sizes = jnp.sum(vec[6:9, :], axis=1, keepdims=True)
    o_levels[...] = jnp.broadcast_to(jnp.sqrt(sizes / frames), o_levels.shape)


def padded(x, rows):
    return x if x.shape[0] == rows else jnp.pad(x, ((0, rows - x.shape[0]), (0, 0)))


def on_device(
    input_rows,
    conditioning,
    prompt,
    buckets,
    item_len,
    step_index,
    output_gradient,
    grad_skip,
    step_w,
    conv_w,
    cond_w,
    conv_b,
    res_w,
    res_b,
    query_w,
    key_w,
    value_w,
    out_w,
    out_b,
):
    section = lax.axis_index("section")
    sec = section.astype(jnp.int32).reshape(1)
    total, width = input_rows.shape
    micro, slots = item_len.shape
    nq = prompt.shape[2]
    frames = total // micro
    tile = frames // slots
    own = total // 2
    tiles = own // tile
    subs = 2
    size = subs * tile
    grid = tiles // subs
    mb_own = -(-own // frames)
    items = mb_own * slots
    half = width // 2
    taps = conv_w.shape[0]
    per = size // EDGE
    last = total // EDGE - 1
    wide = 2 * width
    conv_flat = conv_w.reshape(taps * width, wide)
    flat_prompt = prompt.reshape(-1, width)

    def whole(x):
        n = x.ndim
        return pl.BlockSpec(x.shape, lambda t, *_: (0,) * n, pipeline_mode=pl.Buffered(1))

    smem = pl.BlockSpec(memory_space=pltpu.SMEM)

    def chip_tile(cols):
        return pl.BlockSpec((size, cols), lambda t, s, *_: (s[0] * grid + t, 0))

    def own_tile(cols):
        return pl.BlockSpec((size, cols), lambda t, *_: (t, 0))

    def const(shape):
        return pl.BlockSpec(shape, lambda t, *_: (0,) * len(shape))

    prev_chip = pl.BlockSpec(
        (EDGE, width), lambda t, s, *_: (jnp.maximum((s[0] * grid + t) * per - 1, 0), 0)
    )
    next_chip = pl.BlockSpec(
        (EDGE, width), lambda t, s, *_: (jnp.minimum((s[0] * grid + t + 1) * per, last), 0)
    )
    vectors = [x.reshape(1, -1) for x in (conv_b, res_b, out_b)]
    weights = [
        step_w,
        conv_flat,
        cond_w,
        vectors[0],
        res_w,
        vectors[1],
        query_w,
        key_w,
        value_w,
        out_w,
        vectors[2],
    ]

    def shape(*dims, dtype=BF16):
        return jax.ShapeDtypeStruct(dims, dtype)

    def blocks_of(n):
        return const((n, half, width)), shape(n, half, width)

    film_spec, film_shape = blocks_of(5)
    side_spec, side_shape = blocks_of(4)
    (
        stack,
        d_pre,
        edge,
        d_sent,
        block_keep,
        block_give,
        skip_keep,
        skip_give,
        keep_a,
        give_a,
        keep_c,
        give_c,
        vec,
    ) = pl.pallas_call(
        functools.partial(forward_kernel, (tile, slots, nq, subs, tiles, mb_own, micro)),
        grid_spec=pltpu.PrefetchScalarGridSpec(
            num_scalar_prefetch=1,
            grid=(grid,),
            in_specs=[smem, smem, smem, prev_chip, chip_tile(width), next_chip]
            + [chip_tile(width)] * 3
            + [whole(flat_prompt)]
            + [whole(w) for w in weights],
            out_specs=[own_tile(taps * width), own_tile(wide), const((2 * EDGE, wide))]
            + [own_tile(width)]
            + [own_tile(half)] * 4
            + [film_spec, film_spec, side_spec, side_spec, const((16, width))],
            scratch_shapes=[
                pltpu.VMEM((items, width), F32),
                pltpu.VMEM((items * nq, width), BF16),
                pltpu.VMEM((items * nq, width), BF16),
                pltpu.VMEM((items * nq, width), F32),
                pltpu.VMEM((items * nq, width), F32),
                pltpu.VMEM((width, wide), F32),
                pltpu.VMEM((width, width), F32),
                pltpu.VMEM((3, 8, wide), F32),
                pltpu.VMEM((3, 8, width), F32),
                pltpu.SMEM((1,), jnp.int32),
                pltpu.VMEM((wide, width), BF16),
                pltpu.VMEM((width, width), BF16),
                pltpu.VMEM((wide, width), BF16),
                pltpu.VMEM((width, wide), F32),
                pltpu.VMEM((width, wide), F32),
                pltpu.VMEM((HEADS * nq, width), BF16),
            ],
        ),
        out_shape=[
            shape(own, taps * width),
            shape(own, wide),
            shape(2 * EDGE, wide),
            shape(own, width),
            shape(own, half),
            shape(own, half),
            shape(own, half),
            shape(own, half),
            film_shape,
            film_shape,
            side_shape,
            side_shape,
            shape(16, width, dtype=F32),
        ],
        compiler_params=pltpu.CompilerParams(vmem_limit_bytes=VMEM),
        cost_estimate=LARGE,
        name="forward",
    )(
        sec,
        buckets,
        item_len,
        step_index,
        input_rows,
        input_rows,
        input_rows,
        conditioning,
        output_gradient,
        grad_skip,
        flat_prompt,
        *weights,
    )

    bits = list(range(lax.axis_size("dp").bit_length() - 1))
    other = [bits[1], bits[0]] + bits[2:]
    if len(other) > 3:
        other[-2], other[-1] = other[-1], other[-2]
    sums = Sum((bits, other))
    far_first = Sum((bits[2:] + bits[:2], bits[:1:-1] + bits[1::-1]))
    unit = 16 * lax.axis_size("dp") // 2

    def batch(keep, give, sums):
        rows = keep.shape[0] * half
        rows = -(-rows // unit) * unit
        return Batch(
            sums, padded(keep.reshape(-1, width), rows), padded(give.reshape(-1, width), rows)
        )

    batch_a, batch_c = batch(keep_a, give_a, far_first), batch(keep_c, give_c, sums)
    block_got, skip_got, other_edge = swap(block_give), swap(skip_give), swap(edge)
    spec = pl.BlockSpec((2, half, width), lambda i, *_: (i, 0, 0))
    keep_b, give_b, after = pl.pallas_call(
        weight_kernel,
        grid_spec=pltpu.PrefetchScalarGridSpec(
            num_scalar_prefetch=1,
            grid=(taps,),
            in_specs=[pl.BlockSpec((own, width), lambda i, *_: (0, i)), whole(d_pre)],
            out_specs=[spec, spec, const((8, 128))],
            scratch_shapes=[pltpu.VMEM((width, wide), F32)],
        ),
        out_shape=[shape(2 * taps, half, width)] * 2 + [shape(8, 128, dtype=F32)],
        compiler_params=pltpu.CompilerParams(vmem_limit_bytes=KB_VMEM),
        cost_estimate=LARGE,
        name="weights",
    )(sec, stack, d_pre)
    batch_b = batch(keep_b, give_b, sums)
    (after,) = batch_a.turn(after)
    (after,) = batch_c.turn(after)

    group = -(-(micro * slots + 2) // 16) * 16
    rows_last = own // EDGE - 1
    in_keep, in_give, rows_now = pl.pallas_call(
        functools.partial(back_kernel, (tile, slots, subs, tiles, micro)),
        grid_spec=pltpu.PrefetchScalarGridSpec(
            num_scalar_prefetch=1,
            grid=(grid,),
            in_specs=[
                smem,
                smem,
                pl.BlockSpec((EDGE, wide), lambda t, *_: (jnp.maximum(t * per - 1, 0), 0)),
                own_tile(wide),
                pl.BlockSpec(
                    (EDGE, wide), lambda t, *_: (jnp.minimum((t + 1) * per, rows_last), 0)
                ),
                whole(other_edge),
                own_tile(width),
                whole(conv_flat),
                smem,
                whole(vec),
                ANYWHERE,
            ],
            out_specs=[own_tile(half), own_tile(half), const((group + EDGE, width))],
            scratch_shapes=[pltpu.VMEM((group, width), F32)],
        ),
        out_shape=[shape(own, half), shape(own, half), shape(group + EDGE, width)],
        compiler_params=pltpu.CompilerParams(vmem_limit_bytes=KC_VMEM),
        cost_estimate=LARGE,
        name="back",
    )(
        sec,
        buckets,
        item_len,
        d_pre,
        d_pre,
        d_pre,
        other_edge,
        d_sent,
        conv_flat,
        step_index,
        vec,
        after,
    )
    in_got = swap(in_give)

    (after,) = batch_b.turn(rows_now)
    block_out, skip_out, after = join(
        sec, after, (block_keep, block_got), (skip_keep, skip_got)
    )
    rows_got, rows_bit, gathered = swap(rows_now), sec, 0
    batches = {"a": batch_a, "b": batch_b, "c": batch_c}
    order = "acb" * (batch_a.turns - 1)
    for name in order:
        turner = batches[name]
        if name == "b" and gathered <= sums.levels:
            n = rows_now.shape[0]
            work = (add_body, rows_bit, rows_now, rows_got, [struct(n, width)])
            if gathered:
                work = (gather_body, rows_bit, rows_now, rows_got, [struct(2 * n - EDGE, width)])
            after, rows_now = turner.turn(after, [work])
            if gathered < sums.levels:
                at = sums.levels - 1 - gathered
                route = [(d, d ^ (1 << at)) for d in range(sums.chips)]
                rows_got = lax.ppermute(rows_now, "dp", route)
                rows_bit = ((sums.chip >> at) & 1).astype(jnp.int32).reshape(1)
            gathered += 1
        else:
            (after,) = turner.turn(after)

    line = struct(1, wide, F32)
    g_step, g_convb, g_resb, g_outb, levels, mark = pl.pallas_call(
        functools.partial(step_kernel, micro * slots, group),
        in_specs=[IN_VMEM, ANYWHERE],
        out_specs=[IN_VMEM] * 6,
        out_shape=[struct(width, width, F32), line, line, line]
        + [struct(3, 128, F32), struct(8, 128, F32)],
        compiler_params=pltpu.CompilerParams(vmem_limit_bytes=24 * 1024 * 1024),
        cost_estimate=LARGE,
        name="step_grad",
    )(rows_now, after)
    in_grad, mark = join(sec, mark, (in_keep, in_got))

    def pairs(k, count, base=0):
        return [(k, base + i * width, col) for i in range(count) for col in (0, width)]

    square, tall = struct(width, width, F32), struct(width, wide, F32)
    shapes_a = [tall, square, square, square]
    spots_a = spots_of(pairs(0, 1) + [(k, 0, 0) for k in (1, 2, 3)], width)
    shapes_b, spots_b = [struct(taps * width, wide, F32)], spots_of(pairs(0, taps), width)
    shapes_c, spots_c = [tall, tall], spots_of(pairs(0, 1) + pairs(1, 1), width)
    *outs_a, mark = batch_a.early(shapes_a, spots_a, mark)
    *outs_c, mark = batch_c.early(shapes_c, spots_c, mark)
    *outs_b, mark = batch_b.early(shapes_b, spots_b, mark)
    mark = batch_a.arrive(mark)
    mark = batch_c.arrive(mark)
    *outs_a, mark = batch_a.late(shapes_a, spots_a, mark, outs_a)
    *outs_c, mark = batch_c.late(shapes_c, spots_c, mark, outs_c)
    mark = batch_b.arrive(mark)
    *outs_b, mark = batch_b.late(shapes_b, spots_b, mark, outs_b)
    g_out, g_query, g_key, g_value = outs_a
    g_conv = outs_b[0].reshape(conv_w.shape)
    g_res, g_cond = outs_c
    g_convb, g_resb, g_outb = (x.reshape(wide) for x in (g_convb, g_resb, g_outb))
    levels = levels[:, 0]
    return (
        block_out,
        skip_out,
        in_grad,
        g_step,
        g_conv,
        g_cond,
        g_convb,
        g_res,
        g_resb,
        g_query,
        g_key,
        g_value,
        g_out,
        g_outb,
        levels,
    )


def solution(mesh):
    rows = P("dp", None)
    split = P("dp", "section")
    return jax.shard_map(
        on_device,
        mesh=mesh,
        in_specs=(rows, rows, P("dp", None, None, None), P("dp"), rows, rows, rows, rows)
        + (P(),) * 11,
        out_specs=(split,) * 3 + (P(),) * 12,
        check_vma=False,
    )
```

```python
import functools
import math

import jax
import jax.numpy as jnp
from jax import lax
from jax.experimental import pallas as pl
from jax.experimental.pallas import tpu as pltpu
from jax.sharding import PartitionSpec as P

HEADS = 8
SHIFT = 2
EDGE = 16
ISQ2 = 0.7071067811865476
F32 = jnp.float32
BF16 = jnp.bfloat16
VMEM = 56 * 1024 * 1024
KB_VMEM = 52 * 1024 * 1024
KC_VMEM = 32 * 1024 * 1024


def nn(a, b):
    return lax.dot_general(a, b, (((1,), (0,)), ((), ())), preferred_element_type=F32)


def nt(a, b):
    return lax.dot_general(a, b, (((1,), (1,)), ((), ())), preferred_element_type=F32)


def tn(a, b):
    return lax.dot_general(a, b, (((0,), (0,)), ((), ())), preferred_element_type=F32)


def rows_iota(rows, cols):
    return lax.broadcasted_iota(jnp.int32, (rows, cols), 0)


def col_sums(x):
    rows, cols = x.shape
    return jnp.sum(x.reshape(rows // 8, 8, cols), axis=0)


def plan(g, tile, slots, buckets, item_len):
    mb = g // slots
    q = g - mb * slots
    span = slots >> buckets[mb]
    slot = q // span
    off = q - slot * span
    lim = item_len[mb, slot] - off * tile
    return mb, slot, lim, off > 0, off < span - 1


def forward_kernel(
    cfg,
    sec_ref,
    buckets,
    item_len,
    steps,
    prev_ref,
    rows_ref,
    next_ref,
    cond_ref,
    gout_ref,
    gskip_ref,
    prompt_ref,
    step_w,
    conv_w,
    cond_w,
    conv_b,
    res_w,
    res_b,
    query_w,
    key_w,
    value_w,
    out_w,
    out_b,
    o_stack,
    o_dpre,
    o_edge,
    o_dsent,
    o_block_keep,
    o_block_give,
    o_skip_keep,
    o_skip_give,
    o_keep,
    o_give,
    o_keep_c,
    o_give_c,
    o_vec,
    proj,
    keys,
    values,
    d_keys,
    d_values,
    g_out,
    g_query,
    sums,
    stats,
    count,
    out_t,
    query_t,
    res_t,
    g_res,
    g_cond,
    own_head,
):
    tile, slots, nq, subs, tiles, mb_own, micro = cfg
    t = pl.program_id(0)
    section = sec_ref[0]
    size = subs * tile
    width = rows_ref.shape[1]
    half = width // 2
    head = width // HEADS
    mb0 = section * (micro - mb_own)
    items = mb_own * slots
    keep_left = section == 0

    @pl.when(t == 0)
    def _():
        row = rows_iota(items, half)
        when = jnp.zeros((items, half), F32)
        for i in range(items):
            s = steps[mb0 + i // slots, i % slots].astype(F32)
            when = jnp.where(row == i, s, when)
        lane = lax.broadcasted_iota(jnp.int32, (items, half), 1).astype(F32)
        angle = when * jnp.exp(lane * F32(-math.log(10000.0) / half))
        emb = jnp.concatenate([jnp.sin(angle), jnp.cos(angle)], axis=1)
        proj[...] = nn(emb.astype(BF16), step_w[...])
        here = prompt_ref[pl.ds(pl.multiple_of(mb0 * slots * nq, 16), items * nq), :]
        factor = head ** (-0.5)
        keys[...] = (nn(here, key_w[...]).astype(BF16) * BF16(factor)).astype(BF16)
        values[...] = nn(here, value_w[...]).astype(BF16)
        d_keys[...] = jnp.zeros_like(d_keys)
        d_values[...] = jnp.zeros_like(d_values)
        g_out[...] = jnp.zeros_like(g_out)
        out_t[...] = out_w[...].T
        query_t[...] = query_w[...].T
        res_t[...] = res_w[...].T
        g_res[...] = jnp.zeros_like(g_res)
        g_cond[...] = jnp.zeros_like(g_cond)
        at_row = rows_iota(HEADS * nq, width) // nq
        at_lane = lax.broadcasted_iota(jnp.int32, (HEADS * nq, width), 1) // head
        own_head[...] = jnp.where(at_row == at_lane, 1.0, 0.0).astype(BF16)
        g_query[...] = jnp.zeros_like(g_query)
        sums[...] = jnp.zeros_like(sums)
        stats[...] = jnp.zeros_like(stats)
        count[0] = 0

    ext = jnp.concatenate([prev_ref[...], rows_ref[...], next_ref[...]], axis=0)
    spread = tile + 2 * EDGE
    place = rows_iota(spread, 128)

    def lanes(mask):
        return jnp.concatenate([mask] * (width // 128), axis=1)

    mixed, behind, ahead, at = [], [], [], []
    valid = []
    row = rows_iota(tile, 128)
    for k in range(subs):
        mb, slot, lim, prev_in, next_in = plan(
            section * tiles + t * subs + k, tile, slots, buckets, item_len
        )
        item = (mb - mb0) * slots + slot
        at.append(pl.multiple_of(item * nq, nq))
        lo = jnp.where(prev_in, 0, EDGE)
        hi = jnp.where(next_in, tile + 2 * EDGE, tile + EDGE)
        hi = jnp.minimum(hi, lim + EDGE)
        part = ext[k * tile : k * tile + spread].astype(F32) + proj[pl.ds(item, 1), :]
        part = part * lanes(jnp.where((place >= lo) & (place < hi), 1.0, 0.0))
        mixed.append(part[EDGE : EDGE + tile])
        behind.append(pltpu.roll(part, SHIFT, 0)[EDGE : EDGE + tile].astype(BF16))
        ahead.append(pltpu.roll(part, spread - SHIFT, 0)[EDGE : EDGE + tile].astype(BF16))
        valid.append(jnp.where(row < lim, 1.0, 0.0))
        count[0] += jnp.clip(lim, 0, tile)
    mixed = jnp.concatenate(mixed, axis=0)
    valid = lanes(jnp.concatenate(valid, axis=0))
    stacked = jnp.concatenate(
        [jnp.concatenate(behind, axis=0), mixed.astype(BF16), jnp.concatenate(ahead, axis=0)],
        axis=1,
    )
    o_stack[...] = stacked
    pre = nn(stacked, conv_w[...]) + nn(cond_ref[...], cond_w[...]) + conv_b[...]
    a = jnp.tanh(pre[:, :width])
    s = 0.5 * jnp.tanh(0.5 * pre[:, width:]) + 0.5
    both = a * s
    gate = both.astype(BF16)
    slope_a = s - both * a
    slope_s = both - both * s
    branch = nn(gate, res_w[...]) + res_b[...]
    res_part = branch[:, :width] * valid
    skip = (branch[:, width:] * valid).astype(BF16)
    o_skip_keep[...] = jnp.where(keep_left, skip[:, :half], skip[:, half:])
    o_skip_give[...] = jnp.where(keep_left, skip[:, half:], skip[:, :half])
    hidden = (mixed + res_part) * ISQ2
    sent = hidden.astype(BF16)
    sent_f = sent.astype(F32)
    stats[0] += col_sums(hidden * hidden)
    stats[1] += col_sums(res_part * res_part)

    query = nn(sent, query_w[...]).astype(BF16)
    mask = own_head[...]
    probs, probs_low, key_bd, value_bd, attended = [], [], [], [], []
    for k in range(subs):
        key_bd.append(jnp.concatenate([keys[pl.ds(at[k], nq), :]] * HEADS, axis=0) * mask)
        value_bd.append(jnp.concatenate([values[pl.ds(at[k], nq), :]] * HEADS, axis=0) * mask)
        scores = nt(key_bd[k], query[k * tile : (k + 1) * tile]).reshape(HEADS, nq, tile)
        expo = jnp.exp(scores - jnp.max(scores, axis=1, keepdims=True))
        probs.append(expo * (1.0 / jnp.sum(expo, axis=1, keepdims=True)))
        probs_low.append(probs[k].astype(BF16).reshape(HEADS * nq, tile))
        attended.append(tn(probs_low[k], value_bd[k]).astype(BF16))
    attended = jnp.concatenate(attended, axis=0)
    film = nn(attended, out_w[...]) + out_b[...]
    scale = film[:, :width]
    change = (sent_f * scale + film[:, width:]) * valid
    block = (sent_f + change).astype(BF16)
    o_block_keep[...] = jnp.where(keep_left, block[:, :half], block[:, half:])
    o_block_give[...] = jnp.where(keep_left, block[:, half:], block[:, :half])
    stats[2] += col_sums(change * change)

    gy = gout_ref[...].astype(F32) * valid
    d_film = jnp.concatenate([(gy * sent_f).astype(BF16), gy.astype(BF16)], axis=1)
    sums[2] += col_sums(d_film.astype(F32))
    g_out[...] += tn(attended, d_film)
    d_att = nn(d_film, out_t[...]).astype(BF16)
    low_lane = lax.broadcasted_iota(jnp.int32, (nq, 2 * head), 1) < head

    def own_heads(x):
        pieces = []
        for p in range(HEADS // 2):
            at_row, at_lane = 2 * p * nq, 2 * p * head
            first = x[at_row : at_row + nq, at_lane : at_lane + 2 * head]
            second = x[at_row + nq : at_row + 2 * nq, at_lane : at_lane + 2 * head]
            pieces.append(jnp.where(low_lane, first, second))
        return jnp.concatenate(pieces, axis=1)

    d_query = []
    for k in range(subs):
        here = slice(k * tile, (k + 1) * tile)
        d_probs = nt(value_bd[k], d_att[here]).reshape(HEADS, nq, tile)
        weighted = probs[k] * d_probs
        inner = jnp.sum(weighted, axis=1, keepdims=True)
        d_scores = (weighted - probs[k] * inner).astype(BF16).reshape(HEADS * nq, tile)
        d_values[pl.ds(at[k], nq), :] += own_heads(nn(probs_low[k], d_att[here]))
        d_keys[pl.ds(at[k], nq), :] += own_heads(nn(d_scores, query[here]))
        d_query.append(tn(d_scores, key_bd[k]).astype(BF16))
    d_query = jnp.concatenate(d_query, axis=0)
    g_query[...] += tn(sent, d_query)
    d_sent = (gy * (1.0 + scale) + nn(d_query, query_t[...])).astype(BF16)
    o_dsent[...] = d_sent

    d_res = (d_sent.astype(F32) * ISQ2).astype(BF16)
    gs = (gskip_ref[...].astype(F32) * valid).astype(BF16)
    d_branch = jnp.concatenate([d_res, gs], axis=1)
    sums[1] += col_sums(d_branch.astype(F32))
    g_res[...] += tn(gate, d_branch)
    d_gate = nn(d_branch, res_t[...])
    d_pre = jnp.concatenate(
        [(d_gate * slope_a).astype(BF16), (d_gate * slope_s).astype(BF16)], axis=1
    )
    sums[0] += col_sums(d_pre.astype(F32))
    o_dpre[...] = d_pre
    g_cond[...] += tn(cond_ref[...], d_pre)

    @pl.when(t == 0)
    def _():
        o_edge[:EDGE, :] = d_pre[:EDGE, :]

    @pl.when(t == tiles // subs - 1)
    def _():
        here = prompt_ref[pl.ds(pl.multiple_of(mb0 * slots * nq, 16), items * nq), :]
        factor = head ** (-0.5)
        mine = pl.multiple_of(section * half, half)
        theirs = pl.multiple_of(half - section * half, half)

        o_edge[EDGE:, :] = d_pre[size - EDGE :, :]

        def put(i, ref, left, keep=o_keep, give=o_give):
            keep[i] = ref[pl.ds(mine, half), pl.ds(left, width)].astype(BF16)
            give[i] = ref[pl.ds(theirs, half), pl.ds(left, width)].astype(BF16)

        put(0, g_query, 0)
        g_query[...] = tn(here, (d_keys[...] * factor).astype(BF16))
        put(1, g_query, 0)
        g_query[...] = tn(here, d_values[...].astype(BF16))
        put(2, g_query, 0)
        put(3, g_out, 0)
        put(4, g_out, width)
        for i, (ref, left) in enumerate(((g_res, 0), (g_res, width), (g_cond, 0), (g_cond, width))):
            put(i, ref, left, o_keep_c, o_give_c)
        for i in range(3):
            line = jnp.sum(sums[i], axis=0, keepdims=True)
            o_vec[2 * i : 2 * i + 1, :] = line[:, :width]
            o_vec[2 * i + 1 : 2 * i + 2, :] = line[:, width:]
        for i in range(3):
            o_vec[6 + i : 7 + i, :] = jnp.sum(stats[i], axis=0, keepdims=True)
        lane = lax.broadcasted_iota(jnp.int32, (16 - 9, width), 1)
        digits = (count[0] >> (3 * jnp.minimum(lane, 8))) & 7
        o_vec[9:16, :] = jnp.where(lane < 8, digits, 0).astype(F32)


def weight_kernel(sec_ref, left_ref, dpre_ref, o_keep, o_give, mark, acc):
    mark[...] = jnp.zeros_like(mark)
    section = sec_ref[0]
    width = acc.shape[0]
    half = width // 2
    acc[...] = tn(left_ref[...], dpre_ref[...])
    mine = pl.multiple_of(section * half, half)
    theirs = pl.multiple_of(half - section * half, half)
    for side in range(2):
        o_keep[side] = acc[pl.ds(mine, half), pl.ds(side * width, width)].astype(BF16)
        o_give[side] = acc[pl.ds(theirs, half), pl.ds(side * width, width)].astype(BF16)


def back_kernel(
    cfg,
    sec_ref,
    buckets,
    item_len,
    prev_ref,
    dpre_ref,
    next_ref,
    other_ref,
    dsent_ref,
    conv_w,
    steps,
    vec_ref,
    after_ref,
    o_keep,
    o_give,
    o_rows,
    d_step,
):
    tile, slots, subs, tiles, micro = cfg
    t = pl.program_id(0)
    section = sec_ref[0]
    width = dsent_ref.shape[1]
    half = width // 2
    count = tiles // subs

    @pl.when(t == 0)
    def _():
        d_step[...] = jnp.zeros_like(d_step)

    before = jnp.where(t == 0, other_ref[EDGE:, :], prev_ref[...])
    after = jnp.where(t == count - 1, other_ref[:EDGE, :], next_ref[...])
    ext = jnp.concatenate([before, dpre_ref[...], after], axis=0)
    spread = tile + 2 * EDGE
    place = rows_iota(spread, 128)
    row = rows_iota(tile, 128)
    ahead, behind, valid, item = [], [], [], []
    for k in range(subs):
        mb, slot, lim, prev_in, next_in = plan(
            section * tiles + t * subs + k, tile, slots, buckets, item_len
        )
        item.append(mb * slots + slot)
        lo = jnp.where(prev_in, 0, EDGE)
        hi = jnp.where(next_in, spread, tile + EDGE)
        here = jnp.where((place >= lo) & (place < hi), 1.0, 0.0)
        part = ext[k * tile : k * tile + spread].astype(F32)
        part = part * jnp.concatenate([here] * (2 * width // 128), axis=1)
        ahead.append(pltpu.roll(part, spread - SHIFT, 0)[EDGE : EDGE + tile].astype(BF16))
        behind.append(pltpu.roll(part, SHIFT, 0)[EDGE : EDGE + tile].astype(BF16))
        valid.append(jnp.where(row < lim, 1.0, 0.0))
    valid = jnp.concatenate([jnp.concatenate(valid, axis=0)] * (width // 128), axis=1)
    d_in = nt(jnp.concatenate(ahead, axis=0), conv_w[:width, :])
    d_in += nt(dpre_ref[...], conv_w[width : 2 * width, :])
    d_in += nt(jnp.concatenate(behind, axis=0), conv_w[2 * width :, :])
    d_mixed = (dsent_ref[...].astype(F32) * ISQ2 + d_in) * valid
    for k in range(subs):
        line = jnp.sum(col_sums(d_mixed[k * tile : (k + 1) * tile]), axis=0, keepdims=True)
        d_step[pl.ds(item[k], 1), :] += line
    low = d_mixed.astype(BF16)
    o_keep[...] = jnp.where(section == 0, low[:, :half], low[:, half:])
    o_give[...] = jnp.where(section == 0, low[:, half:], low[:, :half])

    @pl.when(t == count - 1)
    def _():
        items = micro * slots
        group = d_step.shape[0]
        lane = lax.broadcasted_iota(jnp.int32, (1, width), 1)
        index = jnp.zeros((1, width), jnp.int32)
        for i in range(items):
            index = jnp.where(lane == i, steps[i // slots, i % slots], index)
        d_step[items : items + 1, :] = (index >> 5).astype(F32)
        d_step[items + 1 : items + 2, :] = (index & 31).astype(F32)
        o_rows[:group, :] = d_step[...].astype(BF16)
        o_rows[group:, :] = vec_ref[...].astype(BF16)


SMALL = pl.CostEstimate(flops=1024, bytes_accessed=1024, transcendentals=0)
LARGE = pl.CostEstimate(flops=1 << 36, bytes_accessed=1024, transcendentals=0)
ANYWHERE = pl.BlockSpec(memory_space=pl.ANY)
PARAMS = pltpu.CompilerParams(vmem_limit_bytes=VMEM)


IN_VMEM = pl.BlockSpec(memory_space=pltpu.VMEM)
IN_SMEM = pl.BlockSpec(memory_space=pltpu.SMEM)
IN_HBM = pl.BlockSpec(memory_space=pltpu.HBM)


def struct(rows, width, dtype=BF16):
    return jax.ShapeDtypeStruct((rows, width), dtype)


def total(a, b):
    return (a.astype(F32) + b.astype(F32)).astype(BF16)


def at_bit(bit, rows):
    return pl.ds(pl.multiple_of(bit * rows, 16), rows)


def split_body(bit, held, got, keep, give):
    rows = keep.shape[0]
    keep[...] = total(held[at_bit(bit, rows), :], got[at_bit(bit, rows), :])
    give[...] = total(held[at_bit(1 - bit, rows), :], got[at_bit(1 - bit, rows), :])


def add_body(bit, held, got, out):
    out[...] = total(held[...], got[...])


def merge_body(bit, cur, got, out):
    rows = cur.shape[0]
    out[at_bit(bit, rows), :] = cur[...]
    out[at_bit(1 - bit, rows), :] = got[...]


def ride(bit, sent, got, out, before, place):
    rows = sent.shape[0] - before - EDGE
    end = before + rows
    out[pl.ds(pl.multiple_of(place + bit * rows, 16), rows), :] = sent[before:end, :]
    out[pl.ds(pl.multiple_of(place + rows - bit * rows, 16), rows), :] = got[before:end, :]
    out[place + 2 * rows :, :] = total(sent[end:, :], got[end:, :])


def split_ride_kernel(bit_ref, last_ref, held, got, sent, after_ref, keep, give):
    rows = keep.shape[0]
    bit = bit_ref[0]
    keep[...] = total(held[at_bit(bit, rows), :], got[at_bit(bit, rows), :])
    give[:rows, :] = total(held[at_bit(1 - bit, rows), :], got[at_bit(1 - bit, rows), :])
    ride(last_ref[0], sent, got, give, 2 * rows, rows)


def add_ride_kernel(last_ref, held, got, sent, after_ref, out):
    rows = held.shape[0]
    out[:rows, :] = total(held[...], got[:rows, :])
    ride(last_ref[0], sent, got, out, rows, rows)


def end_ride_kernel(last_ref, sent, got, after_ref, out, rows_out):
    rows = out.shape[0]
    out[...] = total(sent[:rows, :], got[:rows, :])
    ride(last_ref[0], sent, got, rows_out, rows, 0)


def ride_call(kernel, bits, arrays, after, shapes):
    return pl.pallas_call(
        kernel,
        in_specs=[IN_SMEM] * len(bits) + [IN_VMEM] * len(arrays) + [ANYWHERE],
        out_specs=[IN_VMEM] * len(shapes),
        out_shape=shapes,
        compiler_params=pltpu.CompilerParams(vmem_limit_bytes=24 * 1024 * 1024),
        cost_estimate=LARGE,
        name="ride",
    )(*bits, *arrays, after)


def pair_kernel(bodies, outs, *refs):
    n = len(bodies)
    bits, arrays, results = refs[:n], refs[n : 3 * n], refs[3 * n + 1 :]
    for i, body in enumerate(bodies):
        count = outs[i]
        body(bits[i][0], arrays[2 * i], arrays[2 * i + 1], *results[:count])
        results = results[count:]


def pair_call(works, after, cost):
    outs = [len(w[4]) for w in works]
    shapes = [x for w in works for x in w[4]]
    return pl.pallas_call(
        functools.partial(pair_kernel, [w[0] for w in works], outs),
        in_specs=[IN_SMEM] * len(works) + [IN_VMEM] * (2 * len(works)) + [ANYWHERE],
        out_specs=[IN_VMEM] * len(shapes),
        out_shape=shapes,
        compiler_params=pltpu.CompilerParams(vmem_limit_bytes=24 * 1024 * 1024),
        cost_estimate=cost,
        name=works[0][0].__name__,
    )(*[w[1] for w in works], *[x for w in works for x in w[2:4]], after)


def first_kernel(bit_ref, held, got, after_ref, *refs):
    behind, (keep, give, mark, same, bufs, sems) = refs[:-6], refs[-6:]
    mark[...] = jnp.zeros_like(mark)
    rows = keep.shape[0]
    bit = bit_ref[0]
    copies = []
    for i, half in enumerate((1 - bit, bit)):
        for j, array in enumerate((held, got)):
            copies.append(
                pltpu.make_async_copy(
                    array.at[at_bit(half, rows), :], bufs.at[2 * i + j], sems.at[2 * i + j]
                )
            )
    for copy in copies:
        copy.start()
    for i, out in enumerate((give, keep)):
        copies[2 * i].wait()
        copies[2 * i + 1].wait()
        out[:rows, :] = total(bufs[2 * i], bufs[2 * i + 1])
    if behind:
        give[rows:, :] = behind[0][...]


def split_first(held, got, bit, after, cost, behind=()):
    rows, width = held.shape[0] // 2, held.shape[1]
    more = sum(x.shape[0] for x in behind)
    return pl.pallas_call(
        first_kernel,
        in_specs=[IN_SMEM, ANYWHERE, ANYWHERE, ANYWHERE] + [IN_VMEM] * len(behind),
        out_specs=[IN_VMEM] * 3 + [ANYWHERE],
        out_shape=[struct(rows, width), struct(rows + more, width)]
        + [struct(8, 128, F32), struct(2 * rows, width)],
        input_output_aliases={1: 3},
        scratch_shapes=[pltpu.VMEM((4, rows, width), BF16), pltpu.SemaphoreType.DMA((4,))],
        compiler_params=pltpu.CompilerParams(vmem_limit_bytes=24 * 1024 * 1024),
        cost_estimate=cost,
        name="split_first",
    )(bit, held, got, after, *behind)[:3]


def then_kernel(x_ref, after_ref, out_ref):
    out_ref[...] = x_ref[...]


def then(x, after):
    return pl.pallas_call(
        then_kernel,
        in_specs=[IN_VMEM, ANYWHERE],
        out_specs=IN_VMEM,
        out_shape=jax.ShapeDtypeStruct(x.shape, x.dtype),
        compiler_params=pltpu.CompilerParams(vmem_limit_bytes=16 * 1024 * 1024),
        cost_estimate=SMALL,
        name="then",
    )(x, after)


def join_kernel(count, sec_ref, *refs):
    section = sec_ref[0]
    arrays, outs = refs[: 2 * count], refs[2 * count + 1 : 3 * count + 1]
    mark, sems = refs[-2:]
    mark[...] = jnp.zeros_like(mark)
    copies = []
    for i in range(count):
        rows = arrays[2 * i].shape[0]
        for j, place in enumerate((section, 1 - section)):
            copies.append(
                pltpu.make_async_copy(
                    arrays[2 * i + j], outs[i].at[at_bit(place, rows), :], sems.at[2 * i + j]
                )
            )
    for copy in copies:
        copy.start()
    for copy in copies:
        copy.wait()


def join(sec, after, *pairs):
    rows, width = pairs[0][0].shape
    count = len(pairs)
    return pl.pallas_call(
        functools.partial(join_kernel, count),
        in_specs=[IN_SMEM] + [IN_VMEM] * (2 * count) + [ANYWHERE],
        out_specs=[IN_HBM] * count + [IN_VMEM],
        out_shape=[struct(2 * rows, width)] * count + [struct(8, 128, F32)],
        scratch_shapes=[pltpu.SemaphoreType.DMA((2 * count,))],
        compiler_params=pltpu.CompilerParams(vmem_limit_bytes=16 * 1024 * 1024),
        cost_estimate=SMALL,
        name="join",
    )(sec, *[x for pair in pairs for x in pair], after)


def swap(x):
    return lax.ppermute(x, "section", [(0, 1), (1, 0)])


class Sum:
    def __init__(self, orders):
        self.chips = lax.axis_size("dp")
        self.section = lax.axis_index("section")
        self.chip = lax.axis_index("dp")
        self.orders = orders
        self.levels = len(orders[0])

    def bit_of(self, step, section):
        where = jnp.where(section == 0, self.orders[0][step], self.orders[1][step])
        return ((self.chip >> where) & 1).astype(jnp.int32)

    def bit(self, step):
        return self.bit_of(step, self.section).reshape(1)

    def send(self, x, step):
        chips = self.chips
        route = [
            (s * chips + d, s * chips + (d ^ (1 << self.orders[s][step])))
            for s in range(2)
            for d in range(chips)
        ]
        return lax.ppermute(x, ("section", "dp"), route)

    def runs(self):
        mine, theirs = self.section, 1 - self.section
        own, other = self.bit_of(0, mine), self.bit_of(0, theirs)
        return jnp.stack(
            [2 * mine + own, 2 * mine + 1 - own, 2 * theirs + other, 2 * theirs + 1 - other]
        ).astype(jnp.int32)


class Batch:
    def __init__(self, sums, keep, give):
        self.sums = sums
        self.held = keep
        self.got = swap(give)
        self.step = 0

    def turn(self, after, cost=LARGE, behind=None):
        sums, last = self.sums, self.sums.levels - 1
        at = self.step
        self.step += 1
        rows, width = self.held.shape
        if at == 0:
            more = () if behind is None else (behind,)
            self.held, give, mark = split_first(
                self.held, self.got, sums.bit(0), after, cost, more
            )
            self.riders = 0 if behind is None else behind.shape[0]
            self.sent = give
            self.got = sums.send(give, 0)
            return mark
        if self.riders and at <= last + 1:
            return self.ride(at, after)
        if at < last:
            work = (split_body, sums.bit(at), self.held, self.got, [struct(rows // 2, width)] * 2)
            self.held, give = pair_call([work], after, cost)
            self.got = sums.send(give, at)
        elif at <= last + 1:
            work = (add_body, sums.bit(0), self.held, self.got, [struct(rows, width)])
            (self.held,) = pair_call([work], after, cost)
            self.got = sums.send(self.held, at if at == last else last - 1)
        else:
            back = 2 * last + 1 - at
            work = (merge_body, sums.bit(back), self.held, self.got, [struct(2 * rows, width)])
            (self.held,) = pair_call([work], after, cost)
            self.got = sums.send(self.held, back - 1)
        return self.held

    def ride(self, at, after):
        sums, last = self.sums, self.sums.levels - 1
        rows, width = self.held.shape
        before = sums.bit(at - 1)
        more = 2 * self.riders - EDGE
        self.riders = more
        if at < last:
            shapes = [struct(rows // 2, width), struct(rows // 2 + more, width)]
            arrays = (self.held, self.got, self.sent)
            bits = (sums.bit(at), before)
            self.held, self.sent = ride_call(split_ride_kernel, bits, arrays, after, shapes)
            self.got = sums.send(self.sent, at)
            return self.held
        if at == last:
            shapes = [struct(rows + more, width)]
            arrays = (self.held, self.got, self.sent)
            (self.sent,) = ride_call(add_ride_kernel, (before,), arrays, after, shapes)
            self.got = sums.send(self.sent, at)
            return self.sent
        shapes = [struct(rows, width), struct(more, width)]
        arrays = (self.sent, self.got)
        self.held, self.rows = ride_call(end_ride_kernel, (before,), arrays, after, shapes)
        self.got = sums.send(self.held, last - 1)
        return self.held

    @property
    def turns(self):
        return 2 * self.sums.levels - 1

    def early(self):
        return self.sums.runs(), (0, 2), (self.held, swap(self.held)), self.spots

    def arrive(self, after):
        self.got = then(self.got, after)
        self.last = swap(self.got)
        return self.got

    def late(self):
        return self.sums.runs(), (1, 3), (self.got, self.last), self.spots


def place_kernel(groups, count, *refs):
    n = len(groups)
    runs, pieces = refs[:n], refs[n : 3 * n]
    outs, mark = refs[-count - 1 - 2 * n : -1 - 2 * n], refs[-1 - 2 * n]
    bufs, sems = refs[-2 * n : -n], refs[-n:]
    mark[...] = jnp.zeros_like(mark)
    for wait in (False, True):
        for g, (which, spots) in enumerate(groups):
            rows, width = bufs[g].shape[1:]
            per_run = pieces[2 * g].shape[0] // rows
            for run in range(4):
                mine = runs[g][which[0]] == run
                theirs = runs[g][which[1]] == run

                @pl.when(mine | theirs)
                def _(g=g, run=run, mine=mine, spots=spots, rows=rows, per_run=per_run):
                    slot = jnp.where(mine, 0, 1) * per_run
                    for j in range(per_run):
                        spot = spots[run * per_run + j]
                        if spot is None:
                            continue
                        k, row, col = spot
                        copy = pltpu.make_async_copy(
                            bufs[g].at[slot + j],
                            outs[k].at[pl.ds(row, rows), pl.ds(col, width)],
                            sems[g].at[slot + j],
                        )
                        if wait:
                            copy.wait()
                        else:
                            part = slice(j * rows, (j + 1) * rows)
                            value = jnp.where(
                                mine, pieces[2 * g][part, :], pieces[2 * g + 1][part, :]
                            )
                            bufs[g][slot + j] = value.astype(F32)
                            copy.start()


def spots_of(targets, width):
    quarter = width // 4
    spots = []
    for section in range(2):
        for k, row, col in targets:
            for u in range(2):
                spots.append((k, row + (2 * section + u) * quarter, col))
    return spots


def place(parts, shapes, after, outs=()):
    groups, scratch, sems = [], [], []
    for _, which, pieces, spots in parts:
        length, width = pieces[0].shape
        quarter = width // 4
        per_run = length // quarter
        half = len(spots) // 2
        full = [None] * (4 * per_run)
        full[:half] = spots[:half]
        full[2 * per_run : 2 * per_run + half] = spots[half:]
        groups.append((which, full))
        scratch.append(pltpu.VMEM((2 * per_run, quarter, width), F32))
        sems.append(pltpu.SemaphoreType.DMA((2 * per_run,)))
    n = len(parts)
    return pl.pallas_call(
        functools.partial(place_kernel, groups, len(shapes)),
        in_specs=[IN_SMEM] * n + [IN_VMEM] * (2 * n) + [ANYWHERE] + [IN_HBM] * len(outs),
        out_specs=[IN_HBM] * len(shapes) + [IN_VMEM],
        out_shape=list(shapes) + [struct(8, 128, F32)],
        input_output_aliases={3 * n + 1 + k: k for k in range(len(outs))},
        scratch_shapes=scratch + sems,
        compiler_params=pltpu.CompilerParams(vmem_limit_bytes=40 * 1024 * 1024),
        cost_estimate=SMALL,
        name="place",
    )(*[p[0] for p in parts], *[x for p in parts for x in p[2]], after, *outs)


def step_kernel(
    items, group, own_ref, other_ref, after_ref, out_ref, o_low, o_res, o_out, o_levels, mark
):
    mark[...] = jnp.zeros_like(mark)
    width = own_ref.shape[1]
    half = width // 2
    count = own_ref.shape[0] - EDGE

    def product(rows_ref):
        rows = rows_ref[:count, :].astype(F32).reshape(-1, group, width)
        lanes = (rows.shape[0], group, 128)
        index = 32.0 * rows[:, items : items + 1, :128] + rows[:, items + 1 : items + 2, :128]
        diagonal = lax.broadcasted_iota(jnp.int32, lanes, 1) == lax.broadcasted_iota(
            jnp.int32, lanes, 2
        )
        index = jnp.sum(jnp.where(diagonal, index, 0.0), axis=2, keepdims=True)
        index = index.reshape(-1, 1)
        lane = lax.broadcasted_iota(jnp.int32, (index.shape[0], half), 1).astype(F32)
        angle = index * jnp.exp(lane * F32(-math.log(10000.0) / half))
        emb = jnp.concatenate([jnp.sin(angle), jnp.cos(angle)], axis=1)
        used = lax.broadcasted_iota(jnp.int32, rows.shape, 1) < items
        sums = jnp.where(used, rows, 0.0).reshape(-1, width)
        return tn(emb.astype(BF16), sums.astype(BF16))

    out_ref[...] = product(own_ref) + product(other_ref)
    vec = own_ref[count:, :].astype(F32) + other_ref[count:, :].astype(F32)
    for i, out in enumerate((o_low, o_res, o_out)):
        out[:, :width] = vec[2 * i : 2 * i + 1, :]
        out[:, width:] = vec[2 * i + 1 : 2 * i + 2, :]
    digit = lax.broadcasted_iota(jnp.int32, (1, width), 1)
    weight = jnp.where(digit < 8, 1 << (3 * jnp.minimum(digit, 8)), 0).astype(F32)
    frames = jnp.sum(vec[9:10, :] * weight, axis=1, keepdims=True) * width
    sizes = jnp.sum(vec[6:9, :], axis=1, keepdims=True)
    o_levels[...] = jnp.broadcast_to(jnp.sqrt(sizes / frames), o_levels.shape)


def padded(x, rows):
    return x if x.shape[0] == rows else jnp.pad(x, ((0, rows - x.shape[0]), (0, 0)))


def on_device(
    input_rows,
    conditioning,
    prompt,
    buckets,
    item_len,
    step_index,
    output_gradient,
    grad_skip,
    step_w,
    conv_w,
    cond_w,
    conv_b,
    res_w,
    res_b,
    query_w,
    key_w,
    value_w,
    out_w,
    out_b,
):
    section = lax.axis_index("section")
    sec = section.astype(jnp.int32).reshape(1)
    total, width = input_rows.shape
    micro, slots = item_len.shape
    nq = prompt.shape[2]
    frames = total // micro
    tile = frames // slots
    own = total // 2
    tiles = own // tile
    subs = 2
    size = subs * tile
    grid = tiles // subs
    mb_own = -(-own // frames)
    items = mb_own * slots
    half = width // 2
    taps = conv_w.shape[0]
    per = size // EDGE
    last = total // EDGE - 1
    wide = 2 * width
    conv_flat = conv_w.reshape(taps * width, wide)
    flat_prompt = prompt.reshape(-1, width)

    def whole(x):
        n = x.ndim
        return pl.BlockSpec(x.shape, lambda t, *_: (0,) * n, pipeline_mode=pl.Buffered(1))

    smem = pl.BlockSpec(memory_space=pltpu.SMEM)

    def chip_tile(cols):
        return pl.BlockSpec((size, cols), lambda t, s, *_: (s[0] * grid + t, 0))

    def own_tile(cols):
        return pl.BlockSpec((size, cols), lambda t, *_: (t, 0))

    def const(shape):
        return pl.BlockSpec(shape, lambda t, *_: (0,) * len(shape))

    prev_chip = pl.BlockSpec(
        (EDGE, width), lambda t, s, *_: (jnp.maximum((s[0] * grid + t) * per - 1, 0), 0)
    )
    next_chip = pl.BlockSpec(
        (EDGE, width), lambda t, s, *_: (jnp.minimum((s[0] * grid + t + 1) * per, last), 0)
    )
    vectors = [x.reshape(1, -1) for x in (conv_b, res_b, out_b)]
    weights = [
        step_w,
        conv_flat,
        cond_w,
        vectors[0],
        res_w,
        vectors[1],
        query_w,
        key_w,
        value_w,
        out_w,
        vectors[2],
    ]

    def shape(*dims, dtype=BF16):
        return jax.ShapeDtypeStruct(dims, dtype)

    def blocks_of(n):
        return const((n, half, width)), shape(n, half, width)

    film_spec, film_shape = blocks_of(5)
    side_spec, side_shape = blocks_of(4)
    (
        stack,
        d_pre,
        edge,
        d_sent,
        block_keep,
        block_give,
        skip_keep,
        skip_give,
        keep_a,
        give_a,
        keep_c,
        give_c,
        vec,
    ) = pl.pallas_call(
        functools.partial(forward_kernel, (tile, slots, nq, subs, tiles, mb_own, micro)),
        grid_spec=pltpu.PrefetchScalarGridSpec(
            num_scalar_prefetch=1,
            grid=(grid,),
            in_specs=[smem, smem, smem, prev_chip, chip_tile(width), next_chip]
            + [chip_tile(width)] * 3
            + [whole(flat_prompt)]
            + [whole(w) for w in weights],
            out_specs=[own_tile(taps * width), own_tile(wide), const((2 * EDGE, wide))]
            + [own_tile(width)]
            + [own_tile(half)] * 4
            + [film_spec, film_spec, side_spec, side_spec, const((16, width))],
            scratch_shapes=[
                pltpu.VMEM((items, width), F32),
                pltpu.VMEM((items * nq, width), BF16),
                pltpu.VMEM((items * nq, width), BF16),
                pltpu.VMEM((items * nq, width), F32),
                pltpu.VMEM((items * nq, width), F32),
                pltpu.VMEM((width, wide), F32),
                pltpu.VMEM((width, width), F32),
                pltpu.VMEM((3, 8, wide), F32),
                pltpu.VMEM((3, 8, width), F32),
                pltpu.SMEM((1,), jnp.int32),
                pltpu.VMEM((wide, width), BF16),
                pltpu.VMEM((width, width), BF16),
                pltpu.VMEM((wide, width), BF16),
                pltpu.VMEM((width, wide), F32),
                pltpu.VMEM((width, wide), F32),
                pltpu.VMEM((HEADS * nq, width), BF16),
            ],
        ),
        out_shape=[
            shape(own, taps * width),
            shape(own, wide),
            shape(2 * EDGE, wide),
            shape(own, width),
            shape(own, half),
            shape(own, half),
            shape(own, half),
            shape(own, half),
            film_shape,
            film_shape,
            side_shape,
            side_shape,
            shape(16, width, dtype=F32),
        ],
        compiler_params=pltpu.CompilerParams(vmem_limit_bytes=VMEM),
        cost_estimate=LARGE,
        name="forward",
    )(
        sec,
        buckets,
        item_len,
        step_index,
        input_rows,
        input_rows,
        input_rows,
        conditioning,
        output_gradient,
        grad_skip,
        flat_prompt,
        *weights,
    )

    bits = list(range(lax.axis_size("dp").bit_length() - 1))
    other = [bits[1], bits[0]] + bits[2:]
    if len(other) > 3:
        other[-2], other[-1] = other[-1], other[-2]
    sums = Sum((bits, other))
    far_first = Sum((bits[2:] + bits[:2], bits[:1:-1] + bits[1::-1]))
    unit = 16 * lax.axis_size("dp") // 2

    def batch(keep, give, sums):
        rows = keep.shape[0] * half
        rows = -(-rows // unit) * unit
        return Batch(
            sums, padded(keep.reshape(-1, width), rows), padded(give.reshape(-1, width), rows)
        )

    batch_a, batch_c = batch(keep_a, give_a, far_first), batch(keep_c, give_c, sums)
    block_got, skip_got, other_edge = swap(block_give), swap(skip_give), swap(edge)
    spec = pl.BlockSpec((2, half, width), lambda i, *_: (i, 0, 0))
    keep_b, give_b, after = pl.pallas_call(
        weight_kernel,
        grid_spec=pltpu.PrefetchScalarGridSpec(
            num_scalar_prefetch=1,
            grid=(taps,),
            in_specs=[pl.BlockSpec((own, width), lambda i, *_: (0, i)), whole(d_pre)],
            out_specs=[spec, spec, const((8, 128))],
            scratch_shapes=[pltpu.VMEM((width, wide), F32)],
        ),
        out_shape=[shape(2 * taps, half, width)] * 2 + [shape(8, 128, dtype=F32)],
        compiler_params=pltpu.CompilerParams(vmem_limit_bytes=KB_VMEM),
        cost_estimate=LARGE,
        name="weights",
    )(sec, stack, d_pre)
    batch_b = batch(keep_b, give_b, sums)
    after = batch_c.turn(batch_a.turn(after))

    group = -(-(micro * slots + 2) // 16) * 16
    rows_last = own // EDGE - 1
    in_keep, in_give, rows_now = pl.pallas_call(
        functools.partial(back_kernel, (tile, slots, subs, tiles, micro)),
        grid_spec=pltpu.PrefetchScalarGridSpec(
            num_scalar_prefetch=1,
            grid=(grid,),
            in_specs=[
                smem,
                smem,
                pl.BlockSpec((EDGE, wide), lambda t, *_: (jnp.maximum(t * per - 1, 0), 0)),
                own_tile(wide),
                pl.BlockSpec(
                    (EDGE, wide), lambda t, *_: (jnp.minimum((t + 1) * per, rows_last), 0)
                ),
                whole(other_edge),
                own_tile(width),
                whole(conv_flat),
                smem,
                whole(vec),
                ANYWHERE,
            ],
            out_specs=[own_tile(half), own_tile(half), const((group + EDGE, width))],
            scratch_shapes=[pltpu.VMEM((group, width), F32)],
        ),
        out_shape=[shape(own, half), shape(own, half), shape(group + EDGE, width)],
        compiler_params=pltpu.CompilerParams(vmem_limit_bytes=KC_VMEM),
        cost_estimate=LARGE,
        name="back",
    )(
        sec,
        buckets,
        item_len,
        d_pre,
        d_pre,
        d_pre,
        other_edge,
        d_sent,
        conv_flat,
        step_index,
        vec,
        after,
    )
    in_got = swap(in_give)

    after = batch_b.turn(rows_now, behind=rows_now)
    batches = {"a": batch_a, "b": batch_b, "c": batch_c}
    order = "acb" * 2 + "J" + "acb" * (batch_a.turns - 3)
    for name in order:
        if name == "J":
            block_out, skip_out, after = join(
                sec, after, (block_keep, block_got), (skip_keep, skip_got)
            )
            continue
        turner = batches[name]
        after = turner.turn(after)

    line = struct(1, wide, F32)
    g_step, g_convb, g_resb, g_outb, levels, mark = pl.pallas_call(
        functools.partial(step_kernel, micro * slots, group),
        in_specs=[IN_VMEM, IN_VMEM, ANYWHERE],
        out_specs=[IN_VMEM] * 6,
        out_shape=[struct(width, width, F32), line, line, line]
        + [struct(3, 128, F32), struct(8, 128, F32)],
        compiler_params=pltpu.CompilerParams(vmem_limit_bytes=24 * 1024 * 1024),
        cost_estimate=LARGE,
        name="step_grad",
    )(batch_b.rows, swap(batch_b.rows), after)
    in_grad, mark = join(sec, mark, (in_keep, in_got))

    def pairs(k, count, base=0):
        return [(k, base + i * width, col) for i in range(count) for col in (0, width)]

    square, tall = struct(width, width, F32), struct(width, wide, F32)
    shapes = [tall, square, square, square, tall, tall, struct(taps * width, wide, F32)]
    batch_a.spots = spots_of([(1, 0, 0), (2, 0, 0), (3, 0, 0)] + pairs(0, 1), width)
    batch_c.spots = spots_of(pairs(4, 1) + pairs(5, 1), width)
    batch_b.spots = spots_of(pairs(6, taps), width)
    both = (batch_a, batch_c, batch_b)
    *outs, mark = place([batch_a.early()], shapes, mark)
    *outs, mark = place([batch_c.early()], shapes, mark, outs)
    *outs, mark = place([batch_b.early()], shapes, mark, outs)
    mark = batch_a.arrive(mark)
    mark = batch_c.arrive(mark)
    *outs, mark = place([batch_a.late(), batch_c.late()], shapes, mark, outs)
    mark = batch_b.arrive(mark)
    *outs, mark = place([batch_b.late()], shapes, mark, outs)
    g_out, g_query, g_key, g_value, g_res, g_cond, g_conv = outs
    g_conv = g_conv.reshape(conv_w.shape)
    g_convb, g_resb, g_outb = (x.reshape(wide) for x in (g_convb, g_resb, g_outb))
    levels = levels[:, 0]
    return (
        block_out,
        skip_out,
        in_grad,
        g_step,
        g_conv,
        g_cond,
        g_convb,
        g_res,
        g_resb,
        g_query,
        g_key,
        g_value,
        g_out,
        g_outb,
        levels,
    )


def solution(mesh):
    rows = P("dp", None)
    split = P("dp", "section")
    return jax.shard_map(
        on_device,
        mesh=mesh,
        in_specs=(rows, rows, P("dp", None, None, None), P("dp"), rows, rows, rows, rows)
        + (P(),) * 11,
        out_specs=(split,) * 3 + (P(),) * 12,
        check_vma=False,
    )
```

```python
import functools
import math

import jax
import jax.numpy as jnp
from jax import lax
from jax.experimental import pallas as pl
from jax.experimental.pallas import tpu as pltpu
from jax.sharding import PartitionSpec as P

HEADS = 8
SHIFT = 2
EDGE = 16
ISQ2 = 0.7071067811865476
F32 = jnp.float32
BF16 = jnp.bfloat16
VMEM = 56 * 1024 * 1024
KB_VMEM = 56 * 1024 * 1024
KC_VMEM = 32 * 1024 * 1024


def nn(a, b):
    return lax.dot_general(a, b, (((1,), (0,)), ((), ())), preferred_element_type=F32)


def nt(a, b):
    return lax.dot_general(a, b, (((1,), (1,)), ((), ())), preferred_element_type=F32)


def tn(a, b):
    return lax.dot_general(a, b, (((0,), (0,)), ((), ())), preferred_element_type=F32)


def rows_iota(rows, cols):
    return lax.broadcasted_iota(jnp.int32, (rows, cols), 0)


def col_sums(x):
    rows, cols = x.shape
    return jnp.sum(x.reshape(rows // 8, 8, cols), axis=0)


def plan(g, tile, slots, buckets, item_len):
    mb = g // slots
    q = g - mb * slots
    span = slots >> buckets[mb]
    slot = q // span
    off = q - slot * span
    lim = item_len[mb, slot] - off * tile
    return mb, slot, lim, off > 0, off < span - 1


def forward_kernel(
    cfg,
    sec_ref,
    buckets,
    item_len,
    steps,
    prev_ref,
    rows_ref,
    next_ref,
    cond_ref,
    gout_ref,
    gskip_ref,
    prompt_ref,
    step_w,
    conv_w,
    cond_w,
    conv_b,
    res_w,
    res_b,
    query_w,
    key_w,
    value_w,
    out_w,
    out_b,
    o_stack,
    o_dpre,
    o_edge,
    o_dsent,
    o_block_keep,
    o_block_give,
    o_skip_keep,
    o_skip_give,
    o_keep,
    o_give,
    o_keep_c,
    o_give_c,
    o_vec,
    proj,
    keys,
    values,
    d_keys,
    d_values,
    g_out,
    g_query,
    sums,
    stats,
    count,
    out_t,
    query_t,
    res_t,
    g_res,
    g_cond,
    own_head,
):
    tile, slots, nq, subs, tiles, mb_own, micro = cfg
    t = pl.program_id(0)
    section = sec_ref[0]
    size = subs * tile
    width = rows_ref.shape[1]
    half = width // 2
    head = width // HEADS
    mb0 = section * (micro - mb_own)
    items = mb_own * slots
    keep_left = section == 0

    @pl.when(t == 0)
    def _():
        row = rows_iota(items, half)
        when = jnp.zeros((items, half), F32)
        for i in range(items):
            s = steps[mb0 + i // slots, i % slots].astype(F32)
            when = jnp.where(row == i, s, when)
        lane = lax.broadcasted_iota(jnp.int32, (items, half), 1).astype(F32)
        angle = when * jnp.exp(lane * F32(-math.log(10000.0) / half))
        emb = jnp.concatenate([jnp.sin(angle), jnp.cos(angle)], axis=1)
        proj[...] = nn(emb.astype(BF16), step_w[...])
        here = prompt_ref[pl.ds(pl.multiple_of(mb0 * slots * nq, 16), items * nq), :]
        factor = head ** (-0.5)
        keys[...] = (nn(here, key_w[...]).astype(BF16) * BF16(factor)).astype(BF16)
        values[...] = nn(here, value_w[...]).astype(BF16)
        d_keys[...] = jnp.zeros_like(d_keys)
        d_values[...] = jnp.zeros_like(d_values)
        g_out[...] = jnp.zeros_like(g_out)
        out_t[...] = out_w[...].T
        query_t[...] = query_w[...].T
        res_t[...] = res_w[...].T
        g_res[...] = jnp.zeros_like(g_res)
        g_cond[...] = jnp.zeros_like(g_cond)
        at_row = rows_iota(HEADS * nq, width) // nq
        at_lane = lax.broadcasted_iota(jnp.int32, (HEADS * nq, width), 1) // head
        own_head[...] = jnp.where(at_row == at_lane, 1.0, 0.0).astype(BF16)
        g_query[...] = jnp.zeros_like(g_query)
        sums[...] = jnp.zeros_like(sums)
        stats[...] = jnp.zeros_like(stats)
        count[0] = 0

    ext = jnp.concatenate([prev_ref[...], rows_ref[...], next_ref[...]], axis=0)
    spread = tile + 2 * EDGE
    place = rows_iota(spread, 128)

    def lanes(mask):
        return jnp.concatenate([mask] * (width // 128), axis=1)

    mixed, behind, ahead, at = [], [], [], []
    valid = []
    row = rows_iota(tile, 128)
    for k in range(subs):
        mb, slot, lim, prev_in, next_in = plan(
            section * tiles + t * subs + k, tile, slots, buckets, item_len
        )
        item = (mb - mb0) * slots + slot
        at.append(pl.multiple_of(item * nq, nq))
        lo = jnp.where(prev_in, 0, EDGE)
        hi = jnp.where(next_in, tile + 2 * EDGE, tile + EDGE)
        hi = jnp.minimum(hi, lim + EDGE)
        part = ext[k * tile : k * tile + spread].astype(F32) + proj[pl.ds(item, 1), :]
        part = part * lanes(jnp.where((place >= lo) & (place < hi), 1.0, 0.0))
        mixed.append(part[EDGE : EDGE + tile])
        behind.append(pltpu.roll(part, SHIFT, 0)[EDGE : EDGE + tile].astype(BF16))
        ahead.append(pltpu.roll(part, spread - SHIFT, 0)[EDGE : EDGE + tile].astype(BF16))
        valid.append(jnp.where(row < lim, 1.0, 0.0))
        count[0] += jnp.clip(lim, 0, tile)
    mixed = jnp.concatenate(mixed, axis=0)
    valid = lanes(jnp.concatenate(valid, axis=0))
    stacked = jnp.concatenate(
        [jnp.concatenate(behind, axis=0), mixed.astype(BF16), jnp.concatenate(ahead, axis=0)],
        axis=1,
    )
    o_stack[...] = stacked
    pre = nn(stacked, conv_w[...]) + nn(cond_ref[...], cond_w[...]) + conv_b[...]
    a = jnp.tanh(pre[:, :width])
    s = 0.5 * jnp.tanh(0.5 * pre[:, width:]) + 0.5
    both = a * s
    gate = both.astype(BF16)
    slope_a = s - both * a
    slope_s = both - both * s
    branch = nn(gate, res_w[...]) + res_b[...]
    res_part = branch[:, :width] * valid
    skip = (branch[:, width:] * valid).astype(BF16)
    o_skip_keep[...] = jnp.where(keep_left, skip[:, :half], skip[:, half:])
    o_skip_give[...] = jnp.where(keep_left, skip[:, half:], skip[:, :half])
    hidden = (mixed + res_part) * ISQ2
    sent = hidden.astype(BF16)
    sent_f = sent.astype(F32)
    stats[0] += col_sums(hidden * hidden)
    stats[1] += col_sums(res_part * res_part)

    query = nn(sent, query_w[...]).astype(BF16)
    mask = own_head[...]
    probs, probs_low, key_bd, value_bd, attended = [], [], [], [], []
    for k in range(subs):
        key_bd.append(jnp.concatenate([keys[pl.ds(at[k], nq), :]] * HEADS, axis=0) * mask)
        value_bd.append(jnp.concatenate([values[pl.ds(at[k], nq), :]] * HEADS, axis=0) * mask)
        scores = nt(key_bd[k], query[k * tile : (k + 1) * tile]).reshape(HEADS, nq, tile)
        expo = jnp.exp(scores - jnp.max(scores, axis=1, keepdims=True))
        probs.append(expo * (1.0 / jnp.sum(expo, axis=1, keepdims=True)))
        probs_low.append(probs[k].astype(BF16).reshape(HEADS * nq, tile))
        attended.append(tn(probs_low[k], value_bd[k]).astype(BF16))
    attended = jnp.concatenate(attended, axis=0)
    film = nn(attended, out_w[...]) + out_b[...]
    scale = film[:, :width]
    change = (sent_f * scale + film[:, width:]) * valid
    block = (sent_f + change).astype(BF16)
    o_block_keep[...] = jnp.where(keep_left, block[:, :half], block[:, half:])
    o_block_give[...] = jnp.where(keep_left, block[:, half:], block[:, :half])
    stats[2] += col_sums(change * change)

    gy = gout_ref[...].astype(F32) * valid
    d_film = jnp.concatenate([(gy * sent_f).astype(BF16), gy.astype(BF16)], axis=1)
    sums[2] += col_sums(d_film.astype(F32))
    g_out[...] += tn(attended, d_film)
    d_att = nn(d_film, out_t[...]).astype(BF16)
    low_lane = lax.broadcasted_iota(jnp.int32, (nq, 2 * head), 1) < head

    def own_heads(x):
        pieces = []
        for p in range(HEADS // 2):
            at_row, at_lane = 2 * p * nq, 2 * p * head
            first = x[at_row : at_row + nq, at_lane : at_lane + 2 * head]
            second = x[at_row + nq : at_row + 2 * nq, at_lane : at_lane + 2 * head]
            pieces.append(jnp.where(low_lane, first, second))
        return jnp.concatenate(pieces, axis=1)

    d_query = []
    for k in range(subs):
        here = slice(k * tile, (k + 1) * tile)
        d_probs = nt(value_bd[k], d_att[here]).reshape(HEADS, nq, tile)
        weighted = probs[k] * d_probs
        inner = jnp.sum(weighted, axis=1, keepdims=True)
        d_scores = (weighted - probs[k] * inner).astype(BF16).reshape(HEADS * nq, tile)
        d_values[pl.ds(at[k], nq), :] += own_heads(nn(probs_low[k], d_att[here]))
        d_keys[pl.ds(at[k], nq), :] += own_heads(nn(d_scores, query[here]))
        d_query.append(tn(d_scores, key_bd[k]).astype(BF16))
    d_query = jnp.concatenate(d_query, axis=0)
    g_query[...] += tn(sent, d_query)
    d_sent = (gy * (1.0 + scale) + nn(d_query, query_t[...])).astype(BF16)
    o_dsent[...] = d_sent

    d_res = (d_sent.astype(F32) * ISQ2).astype(BF16)
    gs = (gskip_ref[...].astype(F32) * valid).astype(BF16)
    d_branch = jnp.concatenate([d_res, gs], axis=1)
    sums[1] += col_sums(d_branch.astype(F32))
    g_res[...] += tn(gate, d_branch)
    d_gate = nn(d_branch, res_t[...])
    d_pre = jnp.concatenate(
        [(d_gate * slope_a).astype(BF16), (d_gate * slope_s).astype(BF16)], axis=1
    )
    sums[0] += col_sums(d_pre.astype(F32))
    o_dpre[...] = d_pre
    g_cond[...] += tn(cond_ref[...], d_pre)

    @pl.when(t == 0)
    def _():
        o_edge[:EDGE, :] = d_pre[:EDGE, :]

    @pl.when(t == tiles // subs - 1)
    def _():
        here = prompt_ref[pl.ds(pl.multiple_of(mb0 * slots * nq, 16), items * nq), :]
        factor = head ** (-0.5)
        mine = pl.multiple_of(section * half, half)
        theirs = pl.multiple_of(half - section * half, half)

        o_edge[EDGE:, :] = d_pre[size - EDGE :, :]

        def put(i, ref, left, keep=o_keep, give=o_give):
            keep[i] = ref[pl.ds(mine, half), pl.ds(left, width)].astype(BF16)
            give[i] = ref[pl.ds(theirs, half), pl.ds(left, width)].astype(BF16)

        put(0, g_query, 0)
        g_query[...] = tn(here, (d_keys[...] * factor).astype(BF16))
        put(1, g_query, 0)
        g_query[...] = tn(here, d_values[...].astype(BF16))
        put(2, g_query, 0)
        put(3, g_res, width)
        for i, (ref, left) in enumerate(
            ((g_out, 0), (g_out, width), (g_cond, 0), (g_cond, width), (g_res, 0))
        ):
            put(i, ref, left, o_keep_c, o_give_c)
        for i in range(3):
            line = jnp.sum(sums[i], axis=0, keepdims=True)
            o_vec[2 * i : 2 * i + 1, :] = line[:, :width]
            o_vec[2 * i + 1 : 2 * i + 2, :] = line[:, width:]
        for i in range(3):
            o_vec[6 + i : 7 + i, :] = jnp.sum(stats[i], axis=0, keepdims=True)
        lane = lax.broadcasted_iota(jnp.int32, (16 - 9, width), 1)
        digits = (count[0] >> (3 * jnp.minimum(lane, 8))) & 7
        o_vec[9:16, :] = jnp.where(lane < 8, digits, 0).astype(F32)


def weight_kernel(sec_ref, left_ref, dpre_ref, o_keep, o_give, mark, acc):
    mark[...] = jnp.zeros_like(mark)
    section = sec_ref[0]
    width = acc.shape[0]
    half = width // 2
    acc[...] = tn(left_ref[...], dpre_ref[...])
    mine = pl.multiple_of(section * half, half)
    theirs = pl.multiple_of(half - section * half, half)
    for side in range(2):
        o_keep[side] = acc[pl.ds(mine, half), pl.ds(side * width, width)].astype(BF16)
        o_give[side] = acc[pl.ds(theirs, half), pl.ds(side * width, width)].astype(BF16)


def back_kernel(
    cfg,
    sec_ref,
    buckets,
    item_len,
    prev_ref,
    dpre_ref,
    next_ref,
    other_ref,
    dsent_ref,
    conv_w,
    steps,
    vec_ref,
    after_ref,
    o_keep,
    o_give,
    o_rows,
    d_step,
):
    tile, slots, subs, tiles, micro = cfg
    t = pl.program_id(0)
    section = sec_ref[0]
    width = dsent_ref.shape[1]
    half = width // 2
    count = tiles // subs

    @pl.when(t == 0)
    def _():
        d_step[...] = jnp.zeros_like(d_step)

    before = jnp.where(t == 0, other_ref[EDGE:, :], prev_ref[...])
    after = jnp.where(t == count - 1, other_ref[:EDGE, :], next_ref[...])
    ext = jnp.concatenate([before, dpre_ref[...], after], axis=0)
    spread = tile + 2 * EDGE
    place = rows_iota(spread, 128)
    row = rows_iota(tile, 128)
    ahead, behind, valid, item = [], [], [], []
    for k in range(subs):
        mb, slot, lim, prev_in, next_in = plan(
            section * tiles + t * subs + k, tile, slots, buckets, item_len
        )
        item.append(mb * slots + slot)
        lo = jnp.where(prev_in, 0, EDGE)
        hi = jnp.where(next_in, spread, tile + EDGE)
        here = jnp.where((place >= lo) & (place < hi), 1.0, 0.0)
        part = ext[k * tile : k * tile + spread].astype(F32)
        part = part * jnp.concatenate([here] * (2 * width // 128), axis=1)
        ahead.append(pltpu.roll(part, spread - SHIFT, 0)[EDGE : EDGE + tile].astype(BF16))
        behind.append(pltpu.roll(part, SHIFT, 0)[EDGE : EDGE + tile].astype(BF16))
        valid.append(jnp.where(row < lim, 1.0, 0.0))
    valid = jnp.concatenate([jnp.concatenate(valid, axis=0)] * (width // 128), axis=1)
    d_in = nt(jnp.concatenate(ahead, axis=0), conv_w[:width, :])
    d_in += nt(dpre_ref[...], conv_w[width : 2 * width, :])
    d_in += nt(jnp.concatenate(behind, axis=0), conv_w[2 * width :, :])
    d_mixed = (dsent_ref[...].astype(F32) * ISQ2 + d_in) * valid
    for k in range(subs):
        line = jnp.sum(col_sums(d_mixed[k * tile : (k + 1) * tile]), axis=0, keepdims=True)
        d_step[pl.ds(item[k], 1), :] += line
    low = d_mixed.astype(BF16)
    o_keep[...] = jnp.where(section == 0, low[:, :half], low[:, half:])
    o_give[...] = jnp.where(section == 0, low[:, half:], low[:, :half])

    @pl.when(t == count - 1)
    def _():
        items = micro * slots
        group = d_step.shape[0]
        lane = lax.broadcasted_iota(jnp.int32, (1, width), 1)
        index = jnp.zeros((1, width), jnp.int32)
        for i in range(items):
            index = jnp.where(lane == i, steps[i // slots, i % slots], index)
        index = jnp.where(section == 0, index, 0)
        d_step[items : items + 1, :] = (index >> 5).astype(F32)
        d_step[items + 1 : items + 2, :] = (index & 31).astype(F32)
        o_rows[:group, :] = d_step[...].astype(BF16)
        o_rows[group:, :] = vec_ref[...].astype(BF16)


SMALL = pl.CostEstimate(flops=1024, bytes_accessed=1024, transcendentals=0)
LARGE = pl.CostEstimate(flops=1 << 36, bytes_accessed=1024, transcendentals=0)
ANYWHERE = pl.BlockSpec(memory_space=pl.ANY)
PARAMS = pltpu.CompilerParams(vmem_limit_bytes=VMEM)


IN_VMEM = pl.BlockSpec(memory_space=pltpu.VMEM)
IN_SMEM = pl.BlockSpec(memory_space=pltpu.SMEM)
IN_HBM = pl.BlockSpec(memory_space=pltpu.HBM)


def struct(rows, width, dtype=BF16):
    return jax.ShapeDtypeStruct((rows, width), dtype)


def total(a, b):
    return (a.astype(F32) + b.astype(F32)).astype(BF16)


def at_bit(bit, rows):
    return pl.ds(pl.multiple_of(bit * rows, 16), rows)


def split_body(bit, held, got, keep, give):
    rows = keep.shape[0]
    keep[...] = total(held[at_bit(bit, rows), :], got[at_bit(bit, rows), :])
    give[...] = total(held[at_bit(1 - bit, rows), :], got[at_bit(1 - bit, rows), :])


def add_body(bit, held, got, out):
    out[...] = total(held[...], got[...])


def merge_body(bit, cur, got, out):
    rows = cur.shape[0]
    out[at_bit(bit, rows), :] = cur[...]
    out[at_bit(1 - bit, rows), :] = got[...]


def gather_body(bit, cur, got, out):
    rows = cur.shape[0] - EDGE
    out[at_bit(bit, rows), :] = cur[:rows, :]
    out[at_bit(1 - bit, rows), :] = got[:rows, :]
    out[2 * rows :, :] = total(cur[rows:, :], got[rows:, :])


def pair_kernel(bodies, outs, *refs):
    n = len(bodies)
    bits, arrays, results = refs[:n], refs[n : 3 * n], refs[3 * n + 1 :]
    for i, body in enumerate(bodies):
        count = outs[i]
        body(bits[i][0], arrays[2 * i], arrays[2 * i + 1], *results[:count])
        results = results[count:]


def pair_call(works, after, cost):
    outs = [len(w[4]) for w in works]
    shapes = [x for w in works for x in w[4]]
    return pl.pallas_call(
        functools.partial(pair_kernel, [w[0] for w in works], outs),
        in_specs=[IN_SMEM] * len(works) + [IN_VMEM] * (2 * len(works)) + [ANYWHERE],
        out_specs=[IN_VMEM] * len(shapes),
        out_shape=shapes,
        compiler_params=pltpu.CompilerParams(vmem_limit_bytes=24 * 1024 * 1024),
        cost_estimate=cost,
        name=works[0][0].__name__,
    )(*[w[1] for w in works], *[x for w in works for x in w[2:4]], after)


def first_kernel(bit_ref, held, got, after_ref, keep, give, mark, same, bufs, sems):
    mark[...] = jnp.zeros_like(mark)
    rows = keep.shape[0]
    bit = bit_ref[0]
    copies = []
    for i, half in enumerate((1 - bit, bit)):
        for j, array in enumerate((held, got)):
            copies.append(
                pltpu.make_async_copy(
                    array.at[at_bit(half, rows), :], bufs.at[2 * i + j], sems.at[2 * i + j]
                )
            )
    for copy in copies:
        copy.start()
    for i, out in enumerate((give, keep)):
        copies[2 * i].wait()
        copies[2 * i + 1].wait()
        out[...] = total(bufs[2 * i], bufs[2 * i + 1])


def split_first(held, got, bit, after, cost):
    rows, width = held.shape[0] // 2, held.shape[1]
    return pl.pallas_call(
        first_kernel,
        in_specs=[IN_SMEM, ANYWHERE, ANYWHERE, ANYWHERE],
        out_specs=[IN_VMEM] * 3 + [ANYWHERE],
        out_shape=[struct(rows, width)] * 2 + [struct(8, 128, F32), struct(2 * rows, width)],
        input_output_aliases={1: 3},
        scratch_shapes=[pltpu.VMEM((4, rows, width), BF16), pltpu.SemaphoreType.DMA((4,))],
        compiler_params=pltpu.CompilerParams(vmem_limit_bytes=24 * 1024 * 1024),
        cost_estimate=cost,
        name="split_first",
    )(bit, held, got, after)[:3]


def then_kernel(x_ref, after_ref, out_ref):
    out_ref[...] = x_ref[...]


def then(x, after):
    return pl.pallas_call(
        then_kernel,
        in_specs=[IN_VMEM, ANYWHERE],
        out_specs=IN_VMEM,
        out_shape=jax.ShapeDtypeStruct(x.shape, x.dtype),
        compiler_params=pltpu.CompilerParams(vmem_limit_bytes=16 * 1024 * 1024),
        cost_estimate=SMALL,
        name="then",
    )(x, after)


def join_kernel(count, sec_ref, *refs):
    section = sec_ref[0]
    arrays, outs = refs[: 2 * count], refs[2 * count + 1 : 3 * count + 1]
    mark, sems = refs[-2:]
    mark[...] = jnp.zeros_like(mark)
    copies = []
    for i in range(count):
        rows = arrays[2 * i].shape[0]
        for j, place in enumerate((section, 1 - section)):
            copies.append(
                pltpu.make_async_copy(
                    arrays[2 * i + j], outs[i].at[at_bit(place, rows), :], sems.at[2 * i + j]
                )
            )
    for copy in copies:
        copy.start()
    for copy in copies:
        copy.wait()


def join(sec, after, *pairs):
    rows, width = pairs[0][0].shape
    count = len(pairs)
    return pl.pallas_call(
        functools.partial(join_kernel, count),
        in_specs=[IN_SMEM] + [IN_VMEM] * (2 * count) + [ANYWHERE],
        out_specs=[IN_HBM] * count + [IN_VMEM],
        out_shape=[struct(2 * rows, width)] * count + [struct(8, 128, F32)],
        scratch_shapes=[pltpu.SemaphoreType.DMA((2 * count,))],
        compiler_params=pltpu.CompilerParams(vmem_limit_bytes=16 * 1024 * 1024),
        cost_estimate=SMALL,
        name="join",
    )(sec, *[x for pair in pairs for x in pair], after)


def swap(x):
    return lax.ppermute(x, "section", [(0, 1), (1, 0)])


class Sum:
    def __init__(self, orders):
        self.chips = lax.axis_size("dp")
        self.section = lax.axis_index("section")
        self.chip = lax.axis_index("dp")
        self.orders = orders
        self.levels = len(orders[0])

    def bit_of(self, step, section):
        where = jnp.where(section == 0, self.orders[0][step], self.orders[1][step])
        return ((self.chip >> where) & 1).astype(jnp.int32)

    def bit(self, step):
        return self.bit_of(step, self.section).reshape(1)

    def send(self, x, step):
        chips = self.chips
        route = [
            (s * chips + d, s * chips + (d ^ (1 << self.orders[s][step])))
            for s in range(2)
            for d in range(chips)
        ]
        return lax.ppermute(x, ("section", "dp"), route)

    def runs(self):
        mine, theirs = self.section, 1 - self.section
        own, other = self.bit_of(0, mine), self.bit_of(0, theirs)
        return jnp.stack(
            [2 * mine + own, 2 * mine + 1 - own, 2 * theirs + other, 2 * theirs + 1 - other]
        ).astype(jnp.int32)


class Batch:
    def __init__(self, sums, keep, give):
        self.sums = sums
        self.held = keep
        self.got = swap(give)
        self.step = 0

    def turn(self, after, more=(), cost=LARGE):
        sums, last = self.sums, self.sums.levels - 1
        at = self.step
        self.step += 1
        rows, width = self.held.shape
        if at == 0:
            self.held, give, mark = split_first(self.held, self.got, sums.bit(0), after, cost)
            self.got = sums.send(give, 0)
            return (mark,)
        elif at < last:
            work = (split_body, sums.bit(at), self.held, self.got, [struct(rows // 2, width)] * 2)
            self.held, give, *rest = pair_call([work, *more], after, cost)
            self.got = sums.send(give, at)
        elif at <= last + 1:
            work = (add_body, sums.bit(0), self.held, self.got, [struct(rows, width)])
            self.held, *rest = pair_call([work, *more], after, cost)
            self.got = sums.send(self.held, at if at == last else last - 1)
        else:
            back = 2 * last + 1 - at
            work = (merge_body, sums.bit(back), self.held, self.got, [struct(2 * rows, width)])
            self.held, *rest = pair_call([work, *more], after, cost)
            self.got = sums.send(self.held, back - 1)
        return (self.held, *rest)

    @property
    def turns(self):
        return 2 * self.sums.levels - 1

    def early(self, shapes, spots, after, outs=()):
        return place(self.sums.runs(), (0, 2), (self.held, swap(self.held)), shapes, spots, after, outs)

    def arrive(self, after):
        self.got = then(self.got, after)
        self.last = swap(self.got)
        return self.got

    def late(self, shapes, spots, after, outs):
        return place(self.sums.runs(), (1, 3), (self.got, self.last), shapes, spots, after, outs)


def place_kernel(which, spots, count, runs, p0, p1, after_ref, *refs):
    outs, (mark, buf, sems) = refs[-3 - count : -3], refs[-3:]
    mark[...] = jnp.zeros_like(mark)
    rows = buf.shape[1]
    per_run = p0.shape[0] // rows
    for wait in (False, True):
        for run in range(4):
            mine, theirs = runs[which[0]] == run, runs[which[1]] == run
            base = run * per_run

            @pl.when(mine | theirs)
            def _(run=run, mine=mine):
                slot = jnp.where(mine, 0, 1)
                for w in range(run * per_run, (run + 1) * per_run):
                    spot = spots[w]
                    if spot is None:
                        continue
                    j = w - base
                    k, row, col = spot
                    copy = pltpu.make_async_copy(
                        buf.at[slot * per_run + j],
                        outs[k].at[pl.ds(row, rows), pl.ds(col, buf.shape[2])],
                        sems.at[slot * per_run + j],
                    )
                    if wait:
                        copy.wait()
                    else:
                        part = slice(j * rows, (j + 1) * rows)
                        value = jnp.where(mine, p0[part, :], p1[part, :])
                        buf[slot * per_run + j] = value.astype(F32)
                        copy.start()


def spots_of(targets, width):
    quarter = width // 4
    spots = []
    for section in range(2):
        for k, row, col in targets:
            for u in range(2):
                spots.append((k, row + (2 * section + u) * quarter, col))
    return spots


def place(runs, which, pieces, shapes, spots, after, outs=()):
    length, width = pieces[0].shape
    quarter = width // 4
    per_run = length // quarter
    half = len(spots) // 2
    full = [None] * (4 * per_run)
    full[:half] = spots[:half]
    full[2 * per_run : 2 * per_run + half] = spots[half:]
    return pl.pallas_call(
        functools.partial(place_kernel, which, full, len(shapes)),
        in_specs=[IN_SMEM] + [IN_VMEM] * 2 + [ANYWHERE] + [IN_HBM] * len(outs),
        out_specs=[IN_HBM] * len(shapes) + [IN_VMEM],
        out_shape=list(shapes) + [struct(8, 128, F32)],
        input_output_aliases={4 + k: k for k in range(len(outs))},
        scratch_shapes=[
            pltpu.VMEM((2 * per_run, quarter, width), F32),
            pltpu.SemaphoreType.DMA((2 * per_run,)),
        ],
        compiler_params=pltpu.CompilerParams(vmem_limit_bytes=24 * 1024 * 1024),
        cost_estimate=SMALL,
        name="place",
    )(runs, *pieces, after, *outs)


def step_kernel(items, group, rows_ref, after_ref, out_ref, o_low, o_res, o_out, o_levels, mark):
    mark[...] = jnp.zeros_like(mark)
    width = rows_ref.shape[1]
    half = width // 2
    rows = rows_ref[: rows_ref.shape[0] - EDGE, :].astype(F32).reshape(-1, group, width)
    lanes = (rows.shape[0], group, 128)
    index = 32.0 * rows[:, items : items + 1, :128] + rows[:, items + 1 : items + 2, :128]
    diagonal = lax.broadcasted_iota(jnp.int32, lanes, 1) == lax.broadcasted_iota(
        jnp.int32, lanes, 2
    )
    index = jnp.sum(jnp.where(diagonal, index, 0.0), axis=2, keepdims=True)
    index = index.reshape(-1, 1)
    lane = lax.broadcasted_iota(jnp.int32, (index.shape[0], half), 1).astype(F32)
    angle = index * jnp.exp(lane * F32(-math.log(10000.0) / half))
    emb = jnp.concatenate([jnp.sin(angle), jnp.cos(angle)], axis=1)
    used = lax.broadcasted_iota(jnp.int32, rows.shape, 1) < items
    sums = jnp.where(used, rows, 0.0).reshape(-1, width)
    out_ref[...] = tn(emb.astype(BF16), sums.astype(BF16))
    vec = rows_ref[rows_ref.shape[0] - EDGE :, :].astype(F32)
    for i, out in enumerate((o_low, o_res, o_out)):
        out[:, :width] = vec[2 * i : 2 * i + 1, :]
        out[:, width:] = vec[2 * i + 1 : 2 * i + 2, :]
    digit = lax.broadcasted_iota(jnp.int32, (1, width), 1)
    weight = jnp.where(digit < 8, 1 << (3 * jnp.minimum(digit, 8)), 0).astype(F32)
    frames = jnp.sum(vec[9:10, :] * weight, axis=1, keepdims=True) * width
    sizes = jnp.sum(vec[6:9, :], axis=1, keepdims=True)
    o_levels[...] = jnp.broadcast_to(jnp.sqrt(sizes / frames), o_levels.shape)


def padded(x, rows):
    return x if x.shape[0] == rows else jnp.pad(x, ((0, rows - x.shape[0]), (0, 0)))


def on_device(
    input_rows,
    conditioning,
    prompt,
    buckets,
    item_len,
    step_index,
    output_gradient,
    grad_skip,
    step_w,
    conv_w,
    cond_w,
    conv_b,
    res_w,
    res_b,
    query_w,
    key_w,
    value_w,
    out_w,
    out_b,
):
    section = lax.axis_index("section")
    sec = section.astype(jnp.int32).reshape(1)
    total, width = input_rows.shape
    micro, slots = item_len.shape
    nq = prompt.shape[2]
    frames = total // micro
    tile = frames // slots
    own = total // 2
    tiles = own // tile
    subs = 2
    size = subs * tile
    grid = tiles // subs
    mb_own = -(-own // frames)
    items = mb_own * slots
    half = width // 2
    taps = conv_w.shape[0]
    per = size // EDGE
    last = total // EDGE - 1
    wide = 2 * width
    conv_flat = conv_w.reshape(taps * width, wide)
    flat_prompt = prompt.reshape(-1, width)

    def whole(x):
        n = x.ndim
        return pl.BlockSpec(x.shape, lambda t, *_: (0,) * n, pipeline_mode=pl.Buffered(1))

    smem = pl.BlockSpec(memory_space=pltpu.SMEM)

    def chip_tile(cols):
        return pl.BlockSpec((size, cols), lambda t, s, *_: (s[0] * grid + t, 0))

    def own_tile(cols):
        return pl.BlockSpec((size, cols), lambda t, *_: (t, 0))

    def const(shape):
        return pl.BlockSpec(shape, lambda t, *_: (0,) * len(shape))

    prev_chip = pl.BlockSpec(
        (EDGE, width), lambda t, s, *_: (jnp.maximum((s[0] * grid + t) * per - 1, 0), 0)
    )
    next_chip = pl.BlockSpec(
        (EDGE, width), lambda t, s, *_: (jnp.minimum((s[0] * grid + t + 1) * per, last), 0)
    )
    vectors = [x.reshape(1, -1) for x in (conv_b, res_b, out_b)]
    weights = [
        step_w,
        conv_flat,
        cond_w,
        vectors[0],
        res_w,
        vectors[1],
        query_w,
        key_w,
        value_w,
        out_w,
        vectors[2],
    ]

    def shape(*dims, dtype=BF16):
        return jax.ShapeDtypeStruct(dims, dtype)

    def blocks_of(n):
        return const((n, half, width)), shape(n, half, width)

    film_spec, film_shape = blocks_of(4)
    side_spec, side_shape = blocks_of(5)
    (
        stack,
        d_pre,
        edge,
        d_sent,
        block_keep,
        block_give,
        skip_keep,
        skip_give,
        keep_a,
        give_a,
        keep_c,
        give_c,
        vec,
    ) = pl.pallas_call(
        functools.partial(forward_kernel, (tile, slots, nq, subs, tiles, mb_own, micro)),
        grid_spec=pltpu.PrefetchScalarGridSpec(
            num_scalar_prefetch=1,
            grid=(grid,),
            in_specs=[smem, smem, smem, prev_chip, chip_tile(width), next_chip]
            + [chip_tile(width)] * 3
            + [whole(flat_prompt)]
            + [whole(w) for w in weights],
            out_specs=[own_tile(taps * width), own_tile(wide), const((2 * EDGE, wide))]
            + [own_tile(width)]
            + [own_tile(half)] * 4
            + [film_spec, film_spec, side_spec, side_spec, const((16, width))],
            scratch_shapes=[
                pltpu.VMEM((items, width), F32),
                pltpu.VMEM((items * nq, width), BF16),
                pltpu.VMEM((items * nq, width), BF16),
                pltpu.VMEM((items * nq, width), F32),
                pltpu.VMEM((items * nq, width), F32),
                pltpu.VMEM((width, wide), F32),
                pltpu.VMEM((width, width), F32),
                pltpu.VMEM((3, 8, wide), F32),
                pltpu.VMEM((3, 8, width), F32),
                pltpu.SMEM((1,), jnp.int32),
                pltpu.VMEM((wide, width), BF16),
                pltpu.VMEM((width, width), BF16),
                pltpu.VMEM((wide, width), BF16),
                pltpu.VMEM((width, wide), F32),
                pltpu.VMEM((width, wide), F32),
                pltpu.VMEM((HEADS * nq, width), BF16),
            ],
        ),
        out_shape=[
            shape(own, taps * width),
            shape(own, wide),
            shape(2 * EDGE, wide),
            shape(own, width),
            shape(own, half),
            shape(own, half),
            shape(own, half),
            shape(own, half),
            film_shape,
            film_shape,
            side_shape,
            side_shape,
            shape(16, width, dtype=F32),
        ],
        compiler_params=pltpu.CompilerParams(vmem_limit_bytes=VMEM),
        cost_estimate=LARGE,
        name="forward",
    )(
        sec,
        buckets,
        item_len,
        step_index,
        input_rows,
        input_rows,
        input_rows,
        conditioning,
        output_gradient,
        grad_skip,
        flat_prompt,
        *weights,
    )

    bits = list(range(lax.axis_size("dp").bit_length() - 1))
    other = [bits[1], bits[0]] + bits[2:]
    if len(other) > 3:
        other[-2], other[-1] = other[-1], other[-2]
    sums = Sum((bits, other))
    far_first = Sum((bits[2:] + bits[:2], bits[:1:-1] + bits[1::-1]))
    unit = 16 * lax.axis_size("dp") // 2

    def batch(keep, give, sums):
        rows = keep.shape[0] * half
        rows = -(-rows // unit) * unit
        return Batch(
            sums, padded(keep.reshape(-1, width), rows), padded(give.reshape(-1, width), rows)
        )

    batch_a, batch_c = batch(keep_a, give_a, far_first), batch(keep_c, give_c, sums)
    block_got, skip_got, other_edge = swap(block_give), swap(skip_give), swap(edge)
    spec = pl.BlockSpec((2, half, width), lambda i, *_: (i, 0, 0))
    keep_b, give_b, after = pl.pallas_call(
        weight_kernel,
        grid_spec=pltpu.PrefetchScalarGridSpec(
            num_scalar_prefetch=1,
            grid=(taps,),
            in_specs=[pl.BlockSpec((own, width), lambda i, *_: (0, i)), whole(d_pre)],
            out_specs=[spec, spec, const((8, 128))],
            scratch_shapes=[pltpu.VMEM((width, wide), F32)],
        ),
        out_shape=[shape(2 * taps, half, width)] * 2 + [shape(8, 128, dtype=F32)],
        compiler_params=pltpu.CompilerParams(vmem_limit_bytes=KB_VMEM),
        cost_estimate=LARGE,
        name="weights",
    )(sec, stack, d_pre)
    batch_b = batch(keep_b, give_b, sums)
    (after,) = batch_a.turn(after)
    (after,) = batch_c.turn(after)

    group = -(-(micro * slots + 2) // 16) * 16
    rows_last = own // EDGE - 1
    in_keep, in_give, rows_now = pl.pallas_call(
        functools.partial(back_kernel, (tile, slots, subs, tiles, micro)),
        grid_spec=pltpu.PrefetchScalarGridSpec(
            num_scalar_prefetch=1,
            grid=(grid,),
            in_specs=[
                smem,
                smem,
                pl.BlockSpec((EDGE, wide), lambda t, *_: (jnp.maximum(t * per - 1, 0), 0)),
                own_tile(wide),
                pl.BlockSpec(
                    (EDGE, wide), lambda t, *_: (jnp.minimum((t + 1) * per, rows_last), 0)
                ),
                whole(other_edge),
                own_tile(width),
                whole(conv_flat),
                smem,
                whole(vec),
                ANYWHERE,
            ],
            out_specs=[own_tile(half), own_tile(half), const((group + EDGE, width))],
            scratch_shapes=[pltpu.VMEM((group, width), F32)],
        ),
        out_shape=[shape(own, half), shape(own, half), shape(group + EDGE, width)],
        compiler_params=pltpu.CompilerParams(vmem_limit_bytes=KC_VMEM),
        cost_estimate=LARGE,
        name="back",
    )(
        sec,
        buckets,
        item_len,
        d_pre,
        d_pre,
        d_pre,
        other_edge,
        d_sent,
        conv_flat,
        step_index,
        vec,
        after,
    )
    in_got = swap(in_give)

    (after,) = batch_b.turn(rows_now)
    block_out, skip_out, after = join(
        sec, after, (block_keep, block_got), (skip_keep, skip_got)
    )
    rows_got, rows_bit, gathered = swap(rows_now), sec, 0
    batches = {"a": batch_a, "b": batch_b, "c": batch_c}
    order = "acb" * (batch_a.turns - 1)
    for name in order:
        turner = batches[name]
        if name == "b" and gathered <= sums.levels:
            n = rows_now.shape[0]
            work = (add_body, rows_bit, rows_now, rows_got, [struct(n, width)])
            if gathered:
                work = (gather_body, rows_bit, rows_now, rows_got, [struct(2 * n - EDGE, width)])
            after, rows_now = turner.turn(after, [work])
            if gathered < sums.levels:
                at = sums.levels - 1 - gathered
                route = [(d, d ^ (1 << at)) for d in range(sums.chips)]
                rows_got = lax.ppermute(rows_now, "dp", route)
                rows_bit = ((sums.chip >> at) & 1).astype(jnp.int32).reshape(1)
            gathered += 1
        else:
            (after,) = turner.turn(after)

    line = struct(1, wide, F32)
    g_step, g_convb, g_resb, g_outb, levels, mark = pl.pallas_call(
        functools.partial(step_kernel, micro * slots, group),
        in_specs=[IN_VMEM, ANYWHERE],
        out_specs=[IN_VMEM] * 6,
        out_shape=[struct(width, width, F32), line, line, line]
        + [struct(3, 128, F32), struct(8, 128, F32)],
        compiler_params=pltpu.CompilerParams(vmem_limit_bytes=24 * 1024 * 1024),
        cost_estimate=LARGE,
        name="step_grad",
    )(rows_now, after)
    in_grad, mark = join(sec, mark, (in_keep, in_got))

    def pairs(k, count, base=0):
        return [(k, base + i * width, col) for i in range(count) for col in (0, width)]

    square, tall = struct(width, width, F32), struct(width, wide, F32)
    shapes_a = [tall, square, square, square]
    spots_a = spots_of([(k, 0, 0) for k in (1, 2, 3)] + [(0, 0, width)], width)
    shapes_b, spots_b = [struct(taps * width, wide, F32)], spots_of(pairs(0, taps), width)
    shapes_c = [tall, tall, tall]
    spots_c = spots_of(pairs(1, 1) + pairs(2, 1) + [(0, 0, 0)], width)
    g_res, *outs_a, mark = batch_a.early(shapes_a, spots_a, mark)
    g_res, *outs_c, mark = batch_c.early(shapes_c, spots_c, mark, [g_res])
    *outs_b, mark = batch_b.early(shapes_b, spots_b, mark)
    mark = batch_c.arrive(mark)
    mark = batch_a.arrive(mark)
    g_res, *outs_c, mark = batch_c.late(shapes_c, spots_c, mark, [g_res, *outs_c])
    g_res, *outs_a, mark = batch_a.late(shapes_a, spots_a, mark, [g_res, *outs_a])
    mark = batch_b.arrive(mark)
    *outs_b, mark = batch_b.late(shapes_b, spots_b, mark, outs_b)
    g_query, g_key, g_value = outs_a
    g_conv = outs_b[0].reshape(conv_w.shape)
    g_out, g_cond = outs_c
    g_convb, g_resb, g_outb = (x.reshape(wide) for x in (g_convb, g_resb, g_outb))
    levels = levels[:, 0]
    return (
        block_out,
        skip_out,
        in_grad,
        g_step,
        g_conv,
        g_cond,
        g_convb,
        g_res,
        g_resb,
        g_query,
        g_key,
        g_value,
        g_out,
        g_outb,
        levels,
    )


def solution(mesh):
    rows = P("dp", None)
    split = P("dp", "section")
    return jax.shard_map(
        on_device,
        mesh=mesh,
        in_specs=(rows, rows, P("dp", None, None, None), P("dp"), rows, rows, rows, rows)
        + (P(),) * 11,
        out_specs=(split,) * 3 + (P(),) * 12,
        check_vma=False,
    )
```

```python
import functools
import math

import jax
import jax.numpy as jnp
from jax import lax
from jax.experimental import pallas as pl
from jax.experimental.pallas import tpu as pltpu
from jax.sharding import PartitionSpec as P

HEADS = 8
SHIFT = 2
EDGE = 16
ISQ2 = 0.7071067811865476
F32 = jnp.float32
BF16 = jnp.bfloat16
VMEM = 56 * 1024 * 1024
KB_VMEM = 56 * 1024 * 1024
KC_VMEM = 32 * 1024 * 1024


def nn(a, b):
    return lax.dot_general(a, b, (((1,), (0,)), ((), ())), preferred_element_type=F32)


def nt(a, b):
    return lax.dot_general(a, b, (((1,), (1,)), ((), ())), preferred_element_type=F32)


def tn(a, b):
    return lax.dot_general(a, b, (((0,), (0,)), ((), ())), preferred_element_type=F32)


def rows_iota(rows, cols):
    return lax.broadcasted_iota(jnp.int32, (rows, cols), 0)


def col_sums(x):
    rows, cols = x.shape
    return jnp.sum(x.reshape(rows // 8, 8, cols), axis=0)


def plan(g, tile, slots, buckets, item_len):
    mb = g // slots
    q = g - mb * slots
    span = slots >> buckets[mb]
    slot = q // span
    off = q - slot * span
    lim = item_len[mb, slot] - off * tile
    return mb, slot, lim, off > 0, off < span - 1


def forward_kernel(
    cfg,
    sec_ref,
    buckets,
    item_len,
    steps,
    prev_ref,
    rows_ref,
    next_ref,
    cond_ref,
    gout_ref,
    gskip_ref,
    prompt_ref,
    step_w,
    conv_w,
    cond_w,
    conv_b,
    res_w,
    res_b,
    query_w,
    key_w,
    value_w,
    out_w,
    out_b,
    o_stack,
    o_dpre,
    o_edge,
    o_dsent,
    o_block_keep,
    o_block_give,
    o_skip_keep,
    o_skip_give,
    o_keep,
    o_give,
    o_keep_c,
    o_give_c,
    o_vec,
    proj,
    keys,
    values,
    d_keys,
    d_values,
    g_out,
    g_query,
    sums,
    stats,
    count,
    out_t,
    query_t,
    res_t,
    g_res,
    g_cond,
    own_head,
):
    tile, slots, nq, subs, tiles, mb_own, micro = cfg
    t = pl.program_id(0)
    section = sec_ref[0]
    size = subs * tile
    width = rows_ref.shape[1]
    half = width // 2
    head = width // HEADS
    mb0 = section * (micro - mb_own)
    items = mb_own * slots
    keep_left = section == 0

    @pl.when(t == 0)
    def _():
        row = rows_iota(items, half)
        when = jnp.zeros((items, half), F32)
        for i in range(items):
            s = steps[mb0 + i // slots, i % slots].astype(F32)
            when = jnp.where(row == i, s, when)
        lane = lax.broadcasted_iota(jnp.int32, (items, half), 1).astype(F32)
        angle = when * jnp.exp(lane * F32(-math.log(10000.0) / half))
        emb = jnp.concatenate([jnp.sin(angle), jnp.cos(angle)], axis=1)
        proj[...] = nn(emb.astype(BF16), step_w[...])
        here = prompt_ref[pl.ds(pl.multiple_of(mb0 * slots * nq, 16), items * nq), :]
        factor = head ** (-0.5)
        keys[...] = (nn(here, key_w[...]).astype(BF16) * BF16(factor)).astype(BF16)
        values[...] = nn(here, value_w[...]).astype(BF16)
        d_keys[...] = jnp.zeros_like(d_keys)
        d_values[...] = jnp.zeros_like(d_values)
        g_out[...] = jnp.zeros_like(g_out)
        out_t[...] = out_w[...].T
        query_t[...] = query_w[...].T
        res_t[...] = res_w[...].T
        g_res[...] = jnp.zeros_like(g_res)
        g_cond[...] = jnp.zeros_like(g_cond)
        at_row = rows_iota(HEADS * nq, width) // nq
        at_lane = lax.broadcasted_iota(jnp.int32, (HEADS * nq, width), 1) // head
        own_head[...] = jnp.where(at_row == at_lane, 1.0, 0.0).astype(BF16)
        g_query[...] = jnp.zeros_like(g_query)
        sums[...] = jnp.zeros_like(sums)
        stats[...] = jnp.zeros_like(stats)
        count[0] = 0

    ext = jnp.concatenate([prev_ref[...], rows_ref[...], next_ref[...]], axis=0)
    spread = tile + 2 * EDGE
    place = rows_iota(spread, 128)

    def lanes(mask):
        return jnp.concatenate([mask] * (width // 128), axis=1)

    mixed, behind, ahead, at = [], [], [], []
    valid = []
    row = rows_iota(tile, 128)
    for k in range(subs):
        mb, slot, lim, prev_in, next_in = plan(
            section * tiles + t * subs + k, tile, slots, buckets, item_len
        )
        item = (mb - mb0) * slots + slot
        at.append(pl.multiple_of(item * nq, nq))
        lo = jnp.where(prev_in, 0, EDGE)
        hi = jnp.where(next_in, tile + 2 * EDGE, tile + EDGE)
        hi = jnp.minimum(hi, lim + EDGE)
        part = ext[k * tile : k * tile + spread].astype(F32) + proj[pl.ds(item, 1), :]
        part = part * lanes(jnp.where((place >= lo) & (place < hi), 1.0, 0.0))
        mixed.append(part[EDGE : EDGE + tile])
        behind.append(pltpu.roll(part, SHIFT, 0)[EDGE : EDGE + tile].astype(BF16))
        ahead.append(pltpu.roll(part, spread - SHIFT, 0)[EDGE : EDGE + tile].astype(BF16))
        valid.append(jnp.where(row < lim, 1.0, 0.0))
        count[0] += jnp.clip(lim, 0, tile)
    mixed = jnp.concatenate(mixed, axis=0)
    valid = lanes(jnp.concatenate(valid, axis=0))
    stacked = jnp.concatenate(
        [jnp.concatenate(behind, axis=0), mixed.astype(BF16), jnp.concatenate(ahead, axis=0)],
        axis=1,
    )
    o_stack[...] = stacked
    pre = nn(stacked, conv_w[...]) + nn(cond_ref[...], cond_w[...]) + conv_b[...]
    a = jnp.tanh(pre[:, :width])
    s = 0.5 * jnp.tanh(0.5 * pre[:, width:]) + 0.5
    both = a * s
    gate = both.astype(BF16)
    slope_a = s - both * a
    slope_s = both - both * s
    branch = nn(gate, res_w[...]) + res_b[...]
    res_part = branch[:, :width] * valid
    skip = (branch[:, width:] * valid).astype(BF16)
    o_skip_keep[...] = jnp.where(keep_left, skip[:, :half], skip[:, half:])
    o_skip_give[...] = jnp.where(keep_left, skip[:, half:], skip[:, :half])
    hidden = (mixed + res_part) * ISQ2
    sent = hidden.astype(BF16)
    sent_f = sent.astype(F32)
    stats[0] += col_sums(hidden * hidden)
    stats[1] += col_sums(res_part * res_part)

    query = nn(sent, query_w[...]).astype(BF16)
    mask = own_head[...]
    probs, probs_low, key_bd, value_bd, attended = [], [], [], [], []
    for k in range(subs):
        key_bd.append(jnp.concatenate([keys[pl.ds(at[k], nq), :]] * HEADS, axis=0) * mask)
        value_bd.append(jnp.concatenate([values[pl.ds(at[k], nq), :]] * HEADS, axis=0) * mask)
        scores = nt(key_bd[k], query[k * tile : (k + 1) * tile]).reshape(HEADS, nq, tile)
        expo = jnp.exp(scores - jnp.max(scores, axis=1, keepdims=True))
        probs.append(expo * (1.0 / jnp.sum(expo, axis=1, keepdims=True)))
        probs_low.append(probs[k].astype(BF16).reshape(HEADS * nq, tile))
        attended.append(tn(probs_low[k], value_bd[k]).astype(BF16))
    attended = jnp.concatenate(attended, axis=0)
    film = nn(attended, out_w[...]) + out_b[...]
    scale = film[:, :width]
    change = (sent_f * scale + film[:, width:]) * valid
    block = (sent_f + change).astype(BF16)
    o_block_keep[...] = jnp.where(keep_left, block[:, :half], block[:, half:])
    o_block_give[...] = jnp.where(keep_left, block[:, half:], block[:, :half])
    stats[2] += col_sums(change * change)

    gy = gout_ref[...].astype(F32) * valid
    d_film = jnp.concatenate([(gy * sent_f).astype(BF16), gy.astype(BF16)], axis=1)
    sums[2] += col_sums(d_film.astype(F32))
    g_out[...] += tn(attended, d_film)
    d_att = nn(d_film, out_t[...]).astype(BF16)
    low_lane = lax.broadcasted_iota(jnp.int32, (nq, 2 * head), 1) < head

    def own_heads(x):
        pieces = []
        for p in range(HEADS // 2):
            at_row, at_lane = 2 * p * nq, 2 * p * head
            first = x[at_row : at_row + nq, at_lane : at_lane + 2 * head]
            second = x[at_row + nq : at_row + 2 * nq, at_lane : at_lane + 2 * head]
            pieces.append(jnp.where(low_lane, first, second))
        return jnp.concatenate(pieces, axis=1)

    d_query = []
    for k in range(subs):
        here = slice(k * tile, (k + 1) * tile)
        d_probs = nt(value_bd[k], d_att[here]).reshape(HEADS, nq, tile)
        weighted = probs[k] * d_probs
        inner = jnp.sum(weighted, axis=1, keepdims=True)
        d_scores = (weighted - probs[k] * inner).astype(BF16).reshape(HEADS * nq, tile)
        d_values[pl.ds(at[k], nq), :] += own_heads(nn(probs_low[k], d_att[here]))
        d_keys[pl.ds(at[k], nq), :] += own_heads(nn(d_scores, query[here]))
        d_query.append(tn(d_scores, key_bd[k]).astype(BF16))
    d_query = jnp.concatenate(d_query, axis=0)
    g_query[...] += tn(sent, d_query)
    d_sent = (gy * (1.0 + scale) + nn(d_query, query_t[...])).astype(BF16)
    o_dsent[...] = d_sent

    d_res = (d_sent.astype(F32) * ISQ2).astype(BF16)
    gs = (gskip_ref[...].astype(F32) * valid).astype(BF16)
    d_branch = jnp.concatenate([d_res, gs], axis=1)
    sums[1] += col_sums(d_branch.astype(F32))
    g_res[...] += tn(gate, d_branch)
    d_gate = nn(d_branch, res_t[...])
    d_pre = jnp.concatenate(
        [(d_gate * slope_a).astype(BF16), (d_gate * slope_s).astype(BF16)], axis=1
    )
    sums[0] += col_sums(d_pre.astype(F32))
    o_dpre[...] = d_pre
    g_cond[...] += tn(cond_ref[...], d_pre)

    @pl.when(t == 0)
    def _():
        o_edge[:EDGE, :] = d_pre[:EDGE, :]

    @pl.when(t == tiles // subs - 1)
    def _():
        here = prompt_ref[pl.ds(pl.multiple_of(mb0 * slots * nq, 16), items * nq), :]
        factor = head ** (-0.5)
        mine = pl.multiple_of(section * half, half)
        theirs = pl.multiple_of(half - section * half, half)

        o_edge[EDGE:, :] = d_pre[size - EDGE :, :]

        def put(i, ref, left, keep=o_keep, give=o_give):
            keep[i] = ref[pl.ds(mine, half), pl.ds(left, width)].astype(BF16)
            give[i] = ref[pl.ds(theirs, half), pl.ds(left, width)].astype(BF16)

        put(0, g_query, 0)
        g_query[...] = tn(here, (d_keys[...] * factor).astype(BF16))
        put(1, g_query, 0)
        g_query[...] = tn(here, d_values[...].astype(BF16))
        put(2, g_query, 0)
        put(3, g_res, width)
        for i, (ref, left) in enumerate(
            ((g_out, 0), (g_out, width), (g_cond, 0), (g_cond, width), (g_res, 0))
        ):
            put(i, ref, left, o_keep_c, o_give_c)
        for i in range(3):
            line = jnp.sum(sums[i], axis=0, keepdims=True)
            o_vec[2 * i : 2 * i + 1, :] = line[:, :width]
            o_vec[2 * i + 1 : 2 * i + 2, :] = line[:, width:]
        for i in range(3):
            o_vec[6 + i : 7 + i, :] = jnp.sum(stats[i], axis=0, keepdims=True)
        lane = lax.broadcasted_iota(jnp.int32, (16 - 9, width), 1)
        digits = (count[0] >> (3 * jnp.minimum(lane, 8))) & 7
        o_vec[9:16, :] = jnp.where(lane < 8, digits, 0).astype(F32)


def weight_kernel(sec_ref, left_ref, dpre_ref, o_keep, o_give, mark, acc):
    mark[...] = jnp.zeros_like(mark)
    section = sec_ref[0]
    width = acc.shape[0]
    half = width // 2
    acc[...] = tn(left_ref[...], dpre_ref[...])
    mine = pl.multiple_of(section * half, half)
    theirs = pl.multiple_of(half - section * half, half)
    for side in range(2):
        o_keep[side] = acc[pl.ds(mine, half), pl.ds(side * width, width)].astype(BF16)
        o_give[side] = acc[pl.ds(theirs, half), pl.ds(side * width, width)].astype(BF16)


def back_kernel(
    cfg,
    sec_ref,
    buckets,
    item_len,
    prev_ref,
    dpre_ref,
    next_ref,
    other_ref,
    dsent_ref,
    conv_w,
    steps,
    vec_ref,
    after_ref,
    o_keep,
    o_give,
    o_rows,
    d_step,
):
    tile, slots, subs, tiles, micro = cfg
    t = pl.program_id(0)
    section = sec_ref[0]
    width = dsent_ref.shape[1]
    half = width // 2
    count = tiles // subs

    @pl.when(t == 0)
    def _():
        d_step[...] = jnp.zeros_like(d_step)

    before = jnp.where(t == 0, other_ref[EDGE:, :], prev_ref[...])
    after = jnp.where(t == count - 1, other_ref[:EDGE, :], next_ref[...])
    ext = jnp.concatenate([before, dpre_ref[...], after], axis=0)
    spread = tile + 2 * EDGE
    place = rows_iota(spread, 128)
    row = rows_iota(tile, 128)
    ahead, behind, valid, item = [], [], [], []
    for k in range(subs):
        mb, slot, lim, prev_in, next_in = plan(
            section * tiles + t * subs + k, tile, slots, buckets, item_len
        )
        item.append(mb * slots + slot)
        lo = jnp.where(prev_in, 0, EDGE)
        hi = jnp.where(next_in, spread, tile + EDGE)
        here = jnp.where((place >= lo) & (place < hi), 1.0, 0.0)
        part = ext[k * tile : k * tile + spread].astype(F32)
        part = part * jnp.concatenate([here] * (2 * width // 128), axis=1)
        ahead.append(pltpu.roll(part, spread - SHIFT, 0)[EDGE : EDGE + tile].astype(BF16))
        behind.append(pltpu.roll(part, SHIFT, 0)[EDGE : EDGE + tile].astype(BF16))
        valid.append(jnp.where(row < lim, 1.0, 0.0))
    valid = jnp.concatenate([jnp.concatenate(valid, axis=0)] * (width // 128), axis=1)
    d_in = nt(jnp.concatenate(ahead, axis=0), conv_w[:width, :])
    d_in += nt(dpre_ref[...], conv_w[width : 2 * width, :])
    d_in += nt(jnp.concatenate(behind, axis=0), conv_w[2 * width :, :])
    d_mixed = (dsent_ref[...].astype(F32) * ISQ2 + d_in) * valid
    for k in range(subs):
        line = jnp.sum(col_sums(d_mixed[k * tile : (k + 1) * tile]), axis=0, keepdims=True)
        d_step[pl.ds(item[k], 1), :] += line
    low = d_mixed.astype(BF16)
    o_keep[...] = jnp.where(section == 0, low[:, :half], low[:, half:])
    o_give[...] = jnp.where(section == 0, low[:, half:], low[:, :half])

    @pl.when(t == count - 1)
    def _():
        items = micro * slots
        group = d_step.shape[0]
        lane = lax.broadcasted_iota(jnp.int32, (1, width), 1)
        index = jnp.zeros((1, width), jnp.int32)
        for i in range(items):
            index = jnp.where(lane == i, steps[i // slots, i % slots], index)
        index = jnp.where(section == 0, index, 0)
        d_step[items : items + 1, :] = (index >> 5).astype(F32)
        d_step[items + 1 : items + 2, :] = (index & 31).astype(F32)
        o_rows[:group, :] = d_step[...].astype(BF16)
        o_rows[group:, :] = vec_ref[...].astype(BF16)


SMALL = pl.CostEstimate(flops=1024, bytes_accessed=1024, transcendentals=0)
LARGE = pl.CostEstimate(flops=1 << 36, bytes_accessed=1024, transcendentals=0)
ANYWHERE = pl.BlockSpec(memory_space=pl.ANY)
PARAMS = pltpu.CompilerParams(vmem_limit_bytes=VMEM)


IN_VMEM = pl.BlockSpec(memory_space=pltpu.VMEM)
IN_SMEM = pl.BlockSpec(memory_space=pltpu.SMEM)
IN_HBM = pl.BlockSpec(memory_space=pltpu.HBM)


def struct(rows, width, dtype=BF16):
    return jax.ShapeDtypeStruct((rows, width), dtype)


def total(a, b):
    return (a.astype(F32) + b.astype(F32)).astype(BF16)


def at_bit(bit, rows):
    return pl.ds(pl.multiple_of(bit * rows, 16), rows)


def split_body(bit, held, got, keep, give):
    rows = keep.shape[0]
    keep[...] = total(held[at_bit(bit, rows), :], got[at_bit(bit, rows), :])
    give[...] = total(held[at_bit(1 - bit, rows), :], got[at_bit(1 - bit, rows), :])


def add_body(bit, held, got, out):
    out[...] = total(held[...], got[...])


def merge_body(bit, cur, got, out):
    rows = cur.shape[0]
    out[at_bit(bit, rows), :] = cur[...]
    out[at_bit(1 - bit, rows), :] = got[...]


def gather_body(bit, cur, got, out):
    rows = cur.shape[0] - EDGE
    out[at_bit(bit, rows), :] = cur[:rows, :]
    out[at_bit(1 - bit, rows), :] = got[:rows, :]
    out[2 * rows :, :] = total(cur[rows:, :], got[rows:, :])


def pair_kernel(bodies, outs, *refs):
    n = len(bodies)
    bits, arrays, results = refs[:n], refs[n : 3 * n], refs[3 * n + 1 :]
    for i, body in enumerate(bodies):
        count = outs[i]
        body(bits[i][0], arrays[2 * i], arrays[2 * i + 1], *results[:count])
        results = results[count:]


def pair_call(works, after, cost):
    outs = [len(w[4]) for w in works]
    shapes = [x for w in works for x in w[4]]
    return pl.pallas_call(
        functools.partial(pair_kernel, [w[0] for w in works], outs),
        in_specs=[IN_SMEM] * len(works) + [IN_VMEM] * (2 * len(works)) + [ANYWHERE],
        out_specs=[IN_VMEM] * len(shapes),
        out_shape=shapes,
        compiler_params=pltpu.CompilerParams(vmem_limit_bytes=24 * 1024 * 1024),
        cost_estimate=cost,
        name=works[0][0].__name__,
    )(*[w[1] for w in works], *[x for w in works for x in w[2:4]], after)


def first_kernel(bit_ref, held, got, after_ref, keep, give, mark, same, bufs, sems):
    mark[...] = jnp.zeros_like(mark)
    rows = keep.shape[0]
    bit = bit_ref[0]
    copies = []
    for i, half in enumerate((1 - bit, bit)):
        for j, array in enumerate((held, got)):
            copies.append(
                pltpu.make_async_copy(
                    array.at[at_bit(half, rows), :], bufs.at[2 * i + j], sems.at[2 * i + j]
                )
            )
    for copy in copies:
        copy.start()
    for i, out in enumerate((give, keep)):
        copies[2 * i].wait()
        copies[2 * i + 1].wait()
        out[...] = total(bufs[2 * i], bufs[2 * i + 1])


def split_first(held, got, bit, after, cost):
    rows, width = held.shape[0] // 2, held.shape[1]
    return pl.pallas_call(
        first_kernel,
        in_specs=[IN_SMEM, ANYWHERE, ANYWHERE, ANYWHERE],
        out_specs=[IN_VMEM] * 3 + [ANYWHERE],
        out_shape=[struct(rows, width)] * 2 + [struct(8, 128, F32), struct(2 * rows, width)],
        input_output_aliases={1: 3},
        scratch_shapes=[pltpu.VMEM((4, rows, width), BF16), pltpu.SemaphoreType.DMA((4,))],
        compiler_params=pltpu.CompilerParams(vmem_limit_bytes=24 * 1024 * 1024),
        cost_estimate=cost,
        name="split_first",
    )(bit, held, got, after)[:3]


def then_kernel(x_ref, after_ref, out_ref):
    out_ref[...] = x_ref[...]


def then(x, after):
    return pl.pallas_call(
        then_kernel,
        in_specs=[IN_VMEM, ANYWHERE],
        out_specs=IN_VMEM,
        out_shape=jax.ShapeDtypeStruct(x.shape, x.dtype),
        compiler_params=pltpu.CompilerParams(vmem_limit_bytes=16 * 1024 * 1024),
        cost_estimate=SMALL,
        name="then",
    )(x, after)


def join_kernel(count, sec_ref, *refs):
    section = sec_ref[0]
    arrays, outs = refs[: 2 * count], refs[2 * count + 1 : 3 * count + 1]
    mark, sems = refs[-2:]
    mark[...] = jnp.zeros_like(mark)
    copies = []
    for i in range(count):
        rows = arrays[2 * i].shape[0]
        for j, place in enumerate((section, 1 - section)):
            copies.append(
                pltpu.make_async_copy(
                    arrays[2 * i + j], outs[i].at[at_bit(place, rows), :], sems.at[2 * i + j]
                )
            )
    for copy in copies:
        copy.start()
    for copy in copies:
        copy.wait()


def join(sec, after, *pairs):
    rows, width = pairs[0][0].shape
    count = len(pairs)
    return pl.pallas_call(
        functools.partial(join_kernel, count),
        in_specs=[IN_SMEM] + [IN_VMEM] * (2 * count) + [ANYWHERE],
        out_specs=[IN_HBM] * count + [IN_VMEM],
        out_shape=[struct(2 * rows, width)] * count + [struct(8, 128, F32)],
        scratch_shapes=[pltpu.SemaphoreType.DMA((2 * count,))],
        compiler_params=pltpu.CompilerParams(vmem_limit_bytes=16 * 1024 * 1024),
        cost_estimate=SMALL,
        name="join",
    )(sec, *[x for pair in pairs for x in pair], after)


def swap(x):
    return lax.ppermute(x, "section", [(0, 1), (1, 0)])


class Sum:
    def __init__(self, orders):
        self.chips = lax.axis_size("dp")
        self.section = lax.axis_index("section")
        self.chip = lax.axis_index("dp")
        self.orders = orders
        self.levels = len(orders[0])

    def bit_of(self, step, section):
        where = jnp.where(section == 0, self.orders[0][step], self.orders[1][step])
        return ((self.chip >> where) & 1).astype(jnp.int32)

    def bit(self, step):
        return self.bit_of(step, self.section).reshape(1)

    def send(self, x, step):
        chips = self.chips
        route = [
            (s * chips + d, s * chips + (d ^ (1 << self.orders[s][step])))
            for s in range(2)
            for d in range(chips)
        ]
        return lax.ppermute(x, ("section", "dp"), route)

    def runs(self):
        mine, theirs = self.section, 1 - self.section
        own, other = self.bit_of(0, mine), self.bit_of(0, theirs)
        return jnp.stack(
            [2 * mine + own, 2 * mine + 1 - own, 2 * theirs + other, 2 * theirs + 1 - other]
        ).astype(jnp.int32)


class Batch:
    def __init__(self, sums, keep, give):
        self.sums = sums
        self.held = keep
        self.got = swap(give)
        self.step = 0

    def turn(self, after, more=(), cost=LARGE):
        sums, last = self.sums, self.sums.levels - 1
        at = self.step
        self.step += 1
        rows, width = self.held.shape
        if at == 0:
            self.held, give, mark = split_first(self.held, self.got, sums.bit(0), after, cost)
            self.got = sums.send(give, 0)
            return (mark,)
        elif at < last:
            work = (split_body, sums.bit(at), self.held, self.got, [struct(rows // 2, width)] * 2)
            self.held, give, *rest = pair_call([work, *more], after, cost)
            self.got = sums.send(give, at)
        elif at <= last + 1:
            work = (add_body, sums.bit(0), self.held, self.got, [struct(rows, width)])
            self.held, *rest = pair_call([work, *more], after, cost)
            self.got = sums.send(self.held, at if at == last else last - 1)
        else:
            back = 2 * last + 1 - at
            work = (merge_body, sums.bit(back), self.held, self.got, [struct(2 * rows, width)])
            self.held, *rest = pair_call([work, *more], after, cost)
            self.got = sums.send(self.held, back - 1)
        return (self.held, *rest)

    @property
    def turns(self):
        return 2 * self.sums.levels - 1

    def early(self, shapes, spots, after, outs=()):
        return place(self.sums.runs(), (0, 2), (self.held, swap(self.held)), shapes, spots, after, outs)

    def arrive(self, after):
        self.got = then(self.got, after)
        self.last = swap(self.got)
        return self.got

    def late(self, shapes, spots, after, outs):
        return place(self.sums.runs(), (1, 3), (self.got, self.last), shapes, spots, after, outs)


def place_kernel(which, spots, count, runs, p0, p1, after_ref, *refs):
    outs, (mark, buf, sems) = refs[-3 - count : -3], refs[-3:]
    mark[...] = jnp.zeros_like(mark)
    rows = buf.shape[1]
    per_run = p0.shape[0] // rows
    for wait in (False, True):
        for run in range(4):
            mine, theirs = runs[which[0]] == run, runs[which[1]] == run
            base = run * per_run

            @pl.when(mine | theirs)
            def _(run=run, mine=mine):
                slot = jnp.where(mine, 0, 1)
                for w in range(run * per_run, (run + 1) * per_run):
                    spot = spots[w]
                    if spot is None:
                        continue
                    j = w - base
                    k, row, col = spot
                    copy = pltpu.make_async_copy(
                        buf.at[slot * per_run + j],
                        outs[k].at[pl.ds(row, rows), pl.ds(col, buf.shape[2])],
                        sems.at[slot * per_run + j],
                    )
                    if wait:
                        copy.wait()
                    else:
                        part = slice(j * rows, (j + 1) * rows)
                        value = jnp.where(mine, p0[part, :], p1[part, :])
                        buf[slot * per_run + j] = value.astype(F32)
                        copy.start()


def spots_of(targets, width):
    quarter = width // 4
    spots = []
    for section in range(2):
        for k, row, col in targets:
            for u in range(2):
                spots.append((k, row + (2 * section + u) * quarter, col))
    return spots


def place(runs, which, pieces, shapes, spots, after, outs=()):
    length, width = pieces[0].shape
    quarter = width // 4
    per_run = length // quarter
    half = len(spots) // 2
    full = [None] * (4 * per_run)
    full[:half] = spots[:half]
    full[2 * per_run : 2 * per_run + half] = spots[half:]
    return pl.pallas_call(
        functools.partial(place_kernel, which, full, len(shapes)),
        in_specs=[IN_SMEM] + [IN_VMEM] * 2 + [ANYWHERE] + [IN_HBM] * len(outs),
        out_specs=[IN_HBM] * len(shapes) + [IN_VMEM],
        out_shape=list(shapes) + [struct(8, 128, F32)],
        input_output_aliases={4 + k: k for k in range(len(outs))},
        scratch_shapes=[
            pltpu.VMEM((2 * per_run, quarter, width), F32),
            pltpu.SemaphoreType.DMA((2 * per_run,)),
        ],
        compiler_params=pltpu.CompilerParams(vmem_limit_bytes=24 * 1024 * 1024),
        cost_estimate=SMALL,
        name="place",
    )(runs, *pieces, after, *outs)


def step_kernel(items, group, rows_ref, after_ref, out_ref, o_low, o_res, o_out, o_levels, mark):
    mark[...] = jnp.zeros_like(mark)
    width = rows_ref.shape[1]
    half = width // 2
    rows = rows_ref[: rows_ref.shape[0] - EDGE, :].astype(F32).reshape(-1, group, width)
    lanes = (rows.shape[0], group, 128)
    index = 32.0 * rows[:, items : items + 1, :128] + rows[:, items + 1 : items + 2, :128]
    diagonal = lax.broadcasted_iota(jnp.int32, lanes, 1) == lax.broadcasted_iota(
        jnp.int32, lanes, 2
    )
    index = jnp.sum(jnp.where(diagonal, index, 0.0), axis=2, keepdims=True)
    index = index.reshape(-1, 1)
    lane = lax.broadcasted_iota(jnp.int32, (index.shape[0], half), 1).astype(F32)
    angle = index * jnp.exp(lane * F32(-math.log(10000.0) / half))
    emb = jnp.concatenate([jnp.sin(angle), jnp.cos(angle)], axis=1)
    used = lax.broadcasted_iota(jnp.int32, rows.shape, 1) < items
    sums = jnp.where(used, rows, 0.0).reshape(-1, width)
    out_ref[...] = tn(emb.astype(BF16), sums.astype(BF16))
    vec = rows_ref[rows_ref.shape[0] - EDGE :, :].astype(F32)
    for i, out in enumerate((o_low, o_res, o_out)):
        out[:, :width] = vec[2 * i : 2 * i + 1, :]
        out[:, width:] = vec[2 * i + 1 : 2 * i + 2, :]
    digit = lax.broadcasted_iota(jnp.int32, (1, width), 1)
    weight = jnp.where(digit < 8, 1 << (3 * jnp.minimum(digit, 8)), 0).astype(F32)
    frames = jnp.sum(vec[9:10, :] * weight, axis=1, keepdims=True) * width
    sizes = jnp.sum(vec[6:9, :], axis=1, keepdims=True)
    o_levels[...] = jnp.broadcast_to(jnp.sqrt(sizes / frames), o_levels.shape)


def padded(x, rows):
    return x if x.shape[0] == rows else jnp.pad(x, ((0, rows - x.shape[0]), (0, 0)))


def on_device(
    input_rows,
    conditioning,
    prompt,
    buckets,
    item_len,
    step_index,
    output_gradient,
    grad_skip,
    step_w,
    conv_w,
    cond_w,
    conv_b,
    res_w,
    res_b,
    query_w,
    key_w,
    value_w,
    out_w,
    out_b,
):
    section = lax.axis_index("section")
    sec = section.astype(jnp.int32).reshape(1)
    total, width = input_rows.shape
    micro, slots = item_len.shape
    nq = prompt.shape[2]
    frames = total // micro
    tile = frames // slots
    own = total // 2
    tiles = own // tile
    subs = 2
    size = subs * tile
    grid = tiles // subs
    mb_own = -(-own // frames)
    items = mb_own * slots
    half = width // 2
    taps = conv_w.shape[0]
    per = size // EDGE
    last = total // EDGE - 1
    wide = 2 * width
    conv_flat = conv_w.reshape(taps * width, wide)
    flat_prompt = prompt.reshape(-1, width)

    def whole(x):
        n = x.ndim
        return pl.BlockSpec(x.shape, lambda t, *_: (0,) * n, pipeline_mode=pl.Buffered(1))

    smem = pl.BlockSpec(memory_space=pltpu.SMEM)

    def chip_tile(cols):
        return pl.BlockSpec((size, cols), lambda t, s, *_: (s[0] * grid + t, 0))

    def own_tile(cols):
        return pl.BlockSpec((size, cols), lambda t, *_: (t, 0))

    def const(shape):
        return pl.BlockSpec(shape, lambda t, *_: (0,) * len(shape))

    prev_chip = pl.BlockSpec(
        (EDGE, width), lambda t, s, *_: (jnp.maximum((s[0] * grid + t) * per - 1, 0), 0)
    )
    next_chip = pl.BlockSpec(
        (EDGE, width), lambda t, s, *_: (jnp.minimum((s[0] * grid + t + 1) * per, last), 0)
    )
    vectors = [x.reshape(1, -1) for x in (conv_b, res_b, out_b)]
    weights = [
        step_w,
        conv_flat,
        cond_w,
        vectors[0],
        res_w,
        vectors[1],
        query_w,
        key_w,
        value_w,
        out_w,
        vectors[2],
    ]

    def shape(*dims, dtype=BF16):
        return jax.ShapeDtypeStruct(dims, dtype)

    def blocks_of(n):
        return const((n, half, width)), shape(n, half, width)

    film_spec, film_shape = blocks_of(4)
    side_spec, side_shape = blocks_of(5)
    (
        stack,
        d_pre,
        edge,
        d_sent,
        block_keep,
        block_give,
        skip_keep,
        skip_give,
        keep_a,
        give_a,
        keep_c,
        give_c,
        vec,
    ) = pl.pallas_call(
        functools.partial(forward_kernel, (tile, slots, nq, subs, tiles, mb_own, micro)),
        grid_spec=pltpu.PrefetchScalarGridSpec(
            num_scalar_prefetch=1,
            grid=(grid,),
            in_specs=[smem, smem, smem, prev_chip, chip_tile(width), next_chip]
            + [chip_tile(width)] * 3
            + [whole(flat_prompt)]
            + [whole(w) for w in weights],
            out_specs=[own_tile(taps * width), own_tile(wide), const((2 * EDGE, wide))]
            + [own_tile(width)]
            + [own_tile(half)] * 4
            + [film_spec, film_spec, side_spec, side_spec, const((16, width))],
            scratch_shapes=[
                pltpu.VMEM((items, width), F32),
                pltpu.VMEM((items * nq, width), BF16),
                pltpu.VMEM((items * nq, width), BF16),
                pltpu.VMEM((items * nq, width), F32),
                pltpu.VMEM((items * nq, width), F32),
                pltpu.VMEM((width, wide), F32),
                pltpu.VMEM((width, width), F32),
                pltpu.VMEM((3, 8, wide), F32),
                pltpu.VMEM((3, 8, width), F32),
                pltpu.SMEM((1,), jnp.int32),
                pltpu.VMEM((wide, width), BF16),
                pltpu.VMEM((width, width), BF16),
                pltpu.VMEM((wide, width), BF16),
                pltpu.VMEM((width, wide), F32),
                pltpu.VMEM((width, wide), F32),
                pltpu.VMEM((HEADS * nq, width), BF16),
            ],
        ),
        out_shape=[
            shape(own, taps * width),
            shape(own, wide),
            shape(2 * EDGE, wide),
            shape(own, width),
            shape(own, half),
            shape(own, half),
            shape(own, half),
            shape(own, half),
            film_shape,
            film_shape,
            side_shape,
            side_shape,
            shape(16, width, dtype=F32),
        ],
        compiler_params=pltpu.CompilerParams(vmem_limit_bytes=VMEM),
        cost_estimate=LARGE,
        name="forward",
    )(
        sec,
        buckets,
        item_len,
        step_index,
        input_rows,
        input_rows,
        input_rows,
        conditioning,
        output_gradient,
        grad_skip,
        flat_prompt,
        *weights,
    )

    bits = list(range(lax.axis_size("dp").bit_length() - 1))
    other = [bits[1], bits[0]] + bits[2:]
    if len(other) > 3:
        other[-2], other[-1] = other[-1], other[-2]
    sums = Sum((bits, other))
    far_first = Sum((bits[2:] + bits[:2], bits[:1:-1] + bits[1::-1]))
    unit = 16 * lax.axis_size("dp") // 2

    def batch(keep, give, sums):
        rows = keep.shape[0] * half
        rows = -(-rows // unit) * unit
        return Batch(
            sums, padded(keep.reshape(-1, width), rows), padded(give.reshape(-1, width), rows)
        )

    batch_a, batch_c = batch(keep_a, give_a, far_first), batch(keep_c, give_c, sums)
    block_got, skip_got, other_edge = swap(block_give), swap(skip_give), swap(edge)
    spec = pl.BlockSpec((2, half, width), lambda i, *_: (i, 0, 0))
    keep_b, give_b, after = pl.pallas_call(
        weight_kernel,
        grid_spec=pltpu.PrefetchScalarGridSpec(
            num_scalar_prefetch=1,
            grid=(taps,),
            in_specs=[pl.BlockSpec((own, width), lambda i, *_: (0, i)), whole(d_pre)],
            out_specs=[spec, spec, const((8, 128))],
            scratch_shapes=[pltpu.VMEM((width, wide), F32)],
        ),
        out_shape=[shape(2 * taps, half, width)] * 2 + [shape(8, 128, dtype=F32)],
        compiler_params=pltpu.CompilerParams(vmem_limit_bytes=KB_VMEM),
        cost_estimate=LARGE,
        name="weights",
    )(sec, stack, d_pre)
    batch_b = batch(keep_b, give_b, sums)
    (after,) = batch_a.turn(after)
    (after,) = batch_c.turn(after)

    group = -(-(micro * slots + 2) // 16) * 16
    rows_last = own // EDGE - 1
    in_keep, in_give, rows_now = pl.pallas_call(
        functools.partial(back_kernel, (tile, slots, subs, tiles, micro)),
        grid_spec=pltpu.PrefetchScalarGridSpec(
            num_scalar_prefetch=1,
            grid=(grid,),
            in_specs=[
                smem,
                smem,
                pl.BlockSpec((EDGE, wide), lambda t, *_: (jnp.maximum(t * per - 1, 0), 0)),
                own_tile(wide),
                pl.BlockSpec(
                    (EDGE, wide), lambda t, *_: (jnp.minimum((t + 1) * per, rows_last), 0)
                ),
                whole(other_edge),
                own_tile(width),
                whole(conv_flat),
                smem,
                whole(vec),
                ANYWHERE,
            ],
            out_specs=[own_tile(half), own_tile(half), const((group + EDGE, width))],
            scratch_shapes=[pltpu.VMEM((group, width), F32)],
        ),
        out_shape=[shape(own, half), shape(own, half), shape(group + EDGE, width)],
        compiler_params=pltpu.CompilerParams(vmem_limit_bytes=KC_VMEM),
        cost_estimate=LARGE,
        name="back",
    )(
        sec,
        buckets,
        item_len,
        d_pre,
        d_pre,
        d_pre,
        other_edge,
        d_sent,
        conv_flat,
        step_index,
        vec,
        after,
    )
    in_got = swap(in_give)

    (after,) = batch_b.turn(rows_now)
    rows_got, rows_bit, gathered = swap(rows_now), sec, 0
    batches = {"a": batch_a, "b": batch_b, "c": batch_c}
    order = "J" + "acb" * 3 + "K" + "acb" * (batch_a.turns - 4)
    for name in order:
        if name == "J":
            block_out, skip_out, after = join(
                sec, after, (block_keep, block_got), (skip_keep, skip_got)
            )
            continue
        if name == "K":
            in_grad, after = join(sec, after, (in_keep, in_got))
            continue
        turner = batches[name]
        if name == "b" and gathered <= sums.levels:
            n = rows_now.shape[0]
            work = (add_body, rows_bit, rows_now, rows_got, [struct(n, width)])
            if gathered:
                work = (gather_body, rows_bit, rows_now, rows_got, [struct(2 * n - EDGE, width)])
            after, rows_now = turner.turn(after, [work])
            if gathered < sums.levels:
                at = sums.levels - 1 - gathered
                route = [(d, d ^ (1 << at)) for d in range(sums.chips)]
                rows_got = lax.ppermute(rows_now, "dp", route)
                rows_bit = ((sums.chip >> at) & 1).astype(jnp.int32).reshape(1)
            gathered += 1
        else:
            (after,) = turner.turn(after)

    line = struct(1, wide, F32)
    g_step, g_convb, g_resb, g_outb, levels, mark = pl.pallas_call(
        functools.partial(step_kernel, micro * slots, group),
        in_specs=[IN_VMEM, ANYWHERE],
        out_specs=[IN_VMEM] * 6,
        out_shape=[struct(width, width, F32), line, line, line]
        + [struct(3, 128, F32), struct(8, 128, F32)],
        compiler_params=pltpu.CompilerParams(vmem_limit_bytes=24 * 1024 * 1024),
        cost_estimate=LARGE,
        name="step_grad",
    )(rows_now, after)

    def pairs(k, count, base=0):
        return [(k, base + i * width, col) for i in range(count) for col in (0, width)]

    square, tall = struct(width, width, F32), struct(width, wide, F32)
    shapes_a = [tall, square, square, square]
    spots_a = spots_of([(k, 0, 0) for k in (1, 2, 3)] + [(0, 0, width)], width)
    shapes_b, spots_b = [struct(taps * width, wide, F32)], spots_of(pairs(0, taps), width)
    shapes_c = [tall, tall, tall]
    spots_c = spots_of(pairs(1, 1) + pairs(2, 1) + [(0, 0, 0)], width)
    g_res, *outs_a, mark = batch_a.early(shapes_a, spots_a, mark)
    g_res, *outs_c, mark = batch_c.early(shapes_c, spots_c, mark, [g_res])
    *outs_b, mark = batch_b.early(shapes_b, spots_b, mark)
    mark = batch_c.arrive(mark)
    mark = batch_a.arrive(mark)
    g_res, *outs_c, mark = batch_c.late(shapes_c, spots_c, mark, [g_res, *outs_c])
    g_res, *outs_a, mark = batch_a.late(shapes_a, spots_a, mark, [g_res, *outs_a])
    mark = batch_b.arrive(mark)
    *outs_b, mark = batch_b.late(shapes_b, spots_b, mark, outs_b)
    g_query, g_key, g_value = outs_a
    g_conv = outs_b[0].reshape(conv_w.shape)
    g_out, g_cond = outs_c
    g_convb, g_resb, g_outb = (x.reshape(wide) for x in (g_convb, g_resb, g_outb))
    levels = levels[:, 0]
    return (
        block_out,
        skip_out,
        in_grad,
        g_step,
        g_conv,
        g_cond,
        g_convb,
        g_res,
        g_resb,
        g_query,
        g_key,
        g_value,
        g_out,
        g_outb,
        levels,
    )


def solution(mesh):
    rows = P("dp", None)
    split = P("dp", "section")
    return jax.shard_map(
        on_device,
        mesh=mesh,
        in_specs=(rows, rows, P("dp", None, None, None), P("dp"), rows, rows, rows, rows)
        + (P(),) * 11,
        out_specs=(split,) * 3 + (P(),) * 12,
        check_vma=False,
    )
```
